32 devices in a mesh: lev: 4 (over x, core), lat: 8 (over z, y).
Axes of the slice: x: 2, y: 2, z: 4, core: 2. Of those that a mesh axis runs over, the one named last changes fastest.
Arguments:
- fields: bfloat16 [48, 8, 72, 384], P('lat', 'lev'), may hold values from -6 to 6
- group_index: int32 [4], replicated, may hold values from 0 to 3
- window_types: int32 [8], replicated, may hold values from 0 to 7, each once
- window_masks: int32 [4, 2, 144], replicated, may hold values from 0 to 3, as said below
- first_gain: float32 [4, 384], replicated, may hold values from 0.1 to 1.9
- first_offset: float32 [4, 384], replicated, may hold values from -4 to 4
- input_weight: bfloat16 [4, 384, 1152], replicated, may hold values from -0.3125 to 0.3125
- input_bias: float32 [4, 768], replicated, may hold values from -4 to 4
- output_weight: bfloat16 [4, 384, 384], replicated, may hold values from -0.875 to 0.875
- output_bias: float32 [4, 384], replicated, may hold values from -4 to 4
- second_gain: float32 [4, 384], replicated, may hold values from 0.1 to 1.9
- second_offset: float32 [4, 384], replicated, may hold values from -4 to 4
- expand_weight: bfloat16 [4, 384, 1536], replicated, may hold values from -0.3125 to 0.3125
- expand_bias: float32 [4, 1536], replicated, may hold values from -6 to 6
- reduce_weight: bfloat16 [4, 1536, 384], replicated, may hold values from -0.21875 to 0.21875
- reduce_bias: float32 [4, 384], replicated, may hold values from -4 to 4
- position_bias: bfloat16 [4, 8, 12, 3312], replicated, may hold values from -6 to 6
- cotangent: bfloat16 [48, 8, 72, 384], P('lat', 'lev'), may hold values from -6 to 6
Outputs:
- output: bfloat16 [48, 8, 72, 384], P('lat', 'lev')
- input_grad: bfloat16 [48, 8, 72, 384], P('lat', 'lev')
- first_gain_grad: float32 [4, 384], replicated
- first_offset_grad: float32 [4, 384], replicated
- input_weight_grad: float32 [4, 384, 1152], replicated
- input_bias_grad: float32 [4, 768], replicated
- output_weight_grad: float32 [4, 384, 384], replicated
- output_bias_grad: float32 [4, 384], replicated
- second_gain_grad: float32 [4, 384], replicated
- second_offset_grad: float32 [4, 384], replicated
- expand_weight_grad: float32 [4, 384, 1536], replicated
- expand_bias_grad: float32 [4, 1536], replicated
- reduce_weight_grad: float32 [4, 1536, 384], replicated
- reduce_bias_grad: float32 [4, 384], replicated
- position_bias_grad: float32 [4, 8, 12, 3312], replicated
The draws below stay inside these ranges and needn't reach their ends.
Inputs may be any that keep to these rules, and one draw needn't show every extreme that they name: `window_types`: entry a * 2 + b is the bias type of shifted window row b of level window a; each type once. `window_masks`: a label for each token of each shifted window; a token attends only to tokens of its label; in the windows of the last level window and of the last latitude window the tokens rolled in from the far edge carry labels of their own.
All inputs are finite; a program needn't handle non-finite values.
Results may differ from the reference program's by a relative error of at most 0.011.
Values may be sent and summed in bfloat16 or wider, within the bound.
No kernel may reach another device: no remote copies, remote signals or barrier semaphores. Data moves between devices by JAX's collectives and lax.ppermute only.
A program may use at most 256 MiB of HBM per device.

```python
import jax
import jax.numpy as jnp
from jax import lax

C = 384
HEADS = 12
MLP = 1536
WZ = 2
WH = 6
WW = 12
G = 4
WROWS = 2
W = 72
HD = 32
Z = 8
H = 12
SAMPLES = 4
LATROWS = 48
TYPES = 8
POS = 3312


def draw_window_masks(key, part):
    key = jax.random.fold_in(key, 7)
    switches = jax.random.randint(key, (Z // WZ, WROWS, 2), 0, 2)
    level_edge = (jnp.arange(Z // WZ) == Z // WZ - 1).astype(jnp.int32)
    row_edge = (jnp.arange(WROWS) == WROWS - 1).astype(jnp.int32)
    level_bit = jnp.maximum(switches[:, :, 0], level_edge[:, None])
    row_bit = jnp.maximum(switches[:, :, 1], row_edge[None, :])
    position = jnp.arange(WZ * WH * WW)
    upper_level = (position // (WH * WW) >= WZ // 2).astype(jnp.int32)
    upper_row = (position // WW % WH >= WH // 2).astype(jnp.int32)
    return (level_bit[:, :, None] * upper_level[None, None, :] + 2 * row_bit[:, :, None] * upper_row[None, None, :]).astype(jnp.int32)


def place_ends(array, own_key, smallest, top_value):
    longest = array.shape.index(max(array.shape))
    spots = []
    for shift in (0, 1):
        where = [jax.random.randint(jax.random.fold_in(own_key, axis), (), 0, length) for axis, length in enumerate(array.shape)]
        where[longest] = (where[longest] + shift) % array.shape[longest]
        spots.append(tuple(where))
    return array.at[spots[0]].set(smallest).at[spots[1]].set(top_value)


def steps_of(own_key, dims, pieces, least, top_value):
    def one(dim, parts):
        heights = jax.random.uniform(jax.random.fold_in(jax.random.fold_in(own_key, 6), dim), (parts,), jnp.float32, least / len(pieces), top_value / len(pieces))
        return jnp.repeat(jnp.exp(heights), dims[dim] // parts).reshape((-1,) + (1,) * (len(dims) - dim - 1))

    factor_of = one(*pieces[0])
    for cut in pieces[1:]:
        factor_of = factor_of * one(*cut)
    return factor_of


def noise(own_key, shape, deviation, bound, pieces=(), kind=jnp.bfloat16):
    drawn = deviation * jax.random.normal(own_key, shape, jnp.float32)
    if pieces:
        drawn = drawn * steps_of(own_key, shape, pieces, -0.22, 0.18)
    return jnp.clip(drawn, -bound, bound).astype(kind)


def setup_inputs(seed: int = 0) -> dict:
    splits = jax.random.split(jax.random.key(seed), 19)
    fields = noise(splits[0], (LATROWS, Z, W, C), 1.0, 6.0, ((0, 8), (1, 4)))
    group_index = place_ends(jax.random.randint(splits[1], (SAMPLES,), 0, G), jax.random.fold_in(splits[1], 1), 0, G - 1).astype(jnp.int32)
    window_types = jax.random.permutation(splits[2], TYPES).astype(jnp.int32)
    window_masks = draw_window_masks(jax.random.fold_in(splits[18], 71), 0)
    first_gain = jnp.clip(1.0 + 0.18 * jax.random.normal(splits[4], (G, C), jnp.float32), 0.1, 1.9)
    first_offset = noise(splits[5], (G, C), 0.3, 4.0, (), jnp.float32)
    input_weight = noise(splits[6], (G, C, 3 * C), C ** -0.5, 0.3125)
    input_bias = noise(splits[7], (G, 2 * C), 0.3, 4.0, (), jnp.float32)
    output_weight = noise(splits[8], (G, C, C), (C // 8) ** -0.5, 0.875)
    output_bias = noise(splits[9], (G, C), 0.3, 4.0, (), jnp.float32)
    second_gain = jnp.clip(1.0 + 0.18 * jax.random.normal(splits[10], (G, C), jnp.float32), 0.1, 1.9)
    second_offset = noise(splits[11], (G, C), 0.3, 4.0, (), jnp.float32)
    expand_weight = noise(splits[12], (G, C, MLP), C ** -0.5, 0.3125)
    expand_bias = noise(splits[13], (G, MLP), 0.5, 6.0, (), jnp.float32)
    reduce_weight = noise(splits[14], (G, MLP, C), (MLP // 2) ** -0.5, 0.21875)
    reduce_bias = noise(splits[15], (G, C), 0.3, 4.0, (), jnp.float32)
    position_bias = noise(splits[16], (G, TYPES, HEADS, POS), 1.0, 6.0)
    cotangent = noise(splits[17], (LATROWS, Z, W, C), 1.0, 6.0, ((0, 8), (1, 4)))
    return {"fields": fields, "group_index": group_index, "window_types": window_types, "window_masks": window_masks, "first_gain": first_gain, "first_offset": first_offset, "input_weight": input_weight, "input_bias": input_bias, "output_weight": output_weight, "output_bias": output_bias, "second_gain": second_gain, "second_offset": second_offset, "expand_weight": expand_weight, "expand_bias": expand_bias, "reduce_weight": reduce_weight, "reduce_bias": reduce_bias, "position_bias": position_bias, "cotangent": cotangent}


@jax.custom_vjp
def low(v):
    return lax.optimization_barrier(v.astype(jnp.bfloat16)).astype(jnp.float32)

@jax.custom_vjp
def low_back(v):
    return v

def low_keep(v):
    return (low(v), None)

def low_pass(kept, grad):
    return (grad,)

def back_keep(v):
    return (v, None)

def back_low(kept, grad):
    return (low(grad),)
low.defvjp(low_keep, low_pass)
low_back.defvjp(back_keep, back_low)
precise = lax.Precision.HIGHEST
masked_value = -1e+30

def layer_norm(values, factor, offset):
    centre = values - lax.optimization_barrier(jnp.mean(values, axis=-1, keepdims=True))
    spread = lax.optimization_barrier(jnp.mean(centre * centre, axis=-1, keepdims=True))
    return centre * lax.rsqrt(spread + 1e-05) * factor + offset

def relative_index():
    position = jnp.arange(WZ * WH * WW, dtype=jnp.int32)
    level_pos = position // (WH * WW)
    row_pos = position // WW % WH
    col_pos = position % WW
    level_part = level_pos[:, None] * WZ + level_pos[None, :]
    row_part = row_pos[:, None] * WH + row_pos[None, :]
    col_part = col_pos[:, None] - col_pos[None, :] + WW - 1
    return ((level_part * WH * WH + row_part) * (2 * WW - 1) + col_part).astype(jnp.int32)

def block_forward(sample_field, params, group_id, window_kind, labels, relative):
    first_gain, first_offset, input_weight, input_bias, output_weight, output_bias, second_gain, second_offset, expand_weight, expand_bias, reduce_weight, reduce_bias, position_bias = params
    shifted = jnp.roll(sample_field, (-(WH // 2), -(WZ // 2), -(WW // 2)), axis=(0, 1, 2))
    shifted = low_back(shifted)
    normed = low(layer_norm(shifted, first_gain[group_id], first_offset[group_id]))
    windows = normed.reshape(WROWS, WH, Z // WZ, WZ, W // WW, WW, C)
    windows = windows.transpose(2, 0, 4, 3, 1, 5, 6).reshape(Z // WZ, WROWS, W // WW, WZ * WH * WW, C)
    bias_row = input_bias[group_id]
    bias_full = jnp.concatenate([bias_row[:C], jnp.zeros((C,), jnp.float32), bias_row[C:]])
    triple = jnp.einsum('abntc,cf->abntf', windows, input_weight[group_id], precision=precise) + bias_full
    triple = low_back(low(triple))
    split_shape = triple.shape[:4] + (HEADS, HD)
    queries = triple[..., :C].reshape(split_shape)
    keyvecs = triple[..., C:2 * C].reshape(split_shape)
    valvecs = triple[..., 2 * C:].reshape(split_shape)
    scores = jnp.einsum('abnihd,abnjhd->abnhij', queries, keyvecs, precision=precise) * HD ** (-0.5)
    table = position_bias[group_id][window_kind]
    gathered = jnp.take(table, relative, axis=-1)
    same_label = labels[:, :, :, None] == labels[:, :, None, :]
    scores = jnp.where(same_label[:, :, None, None], scores + gathered[:, :, None], masked_value)
    scores = low_back(scores)
    row_peak = lax.optimization_barrier(jnp.max(scores, axis=-1, keepdims=True))
    exponent = jnp.exp(scores - row_peak)
    probabilities = exponent / lax.optimization_barrier(jnp.sum(exponent, axis=-1, keepdims=True))
    attended = jnp.einsum('abnhij,abnjhd->abnihd', low(probabilities), valvecs, precision=precise)
    attended = low_back(low(attended.reshape(triple.shape[:4] + (C,))))
    mixed = jnp.einsum('abntc,cf->abntf', attended, output_weight[group_id], precision=precise) + output_bias[group_id]
    mixed = low_back(low(mixed))
    mixed = mixed.reshape(Z // WZ, WROWS, W // WW, WZ, WH, WW, C).transpose(1, 4, 0, 3, 2, 5, 6).reshape(H, Z, W, C)
    mixed = jnp.roll(mixed, (WH // 2, WZ // 2, WW // 2), axis=(0, 1, 2))
    hidden = sample_field + mixed
    normed_second = low(layer_norm(hidden, second_gain[group_id], second_offset[group_id]))
    expanded = jnp.einsum('hzwc,cm->hzwm', normed_second, expand_weight[group_id], precision=precise) + expand_bias[group_id]
    expanded = low_back(expanded)
    active = low(jax.nn.gelu(expanded, approximate=False))
    reduced = jnp.einsum('hzwm,mc->hzwc', active, reduce_weight[group_id], precision=precise) + reduce_bias[group_id]
    return hidden + reduced

def reference(fields, group_index, window_types, window_masks, first_gain, first_offset, input_weight, input_bias, output_weight, output_bias, second_gain, second_offset, expand_weight, expand_bias, reduce_weight, reduce_bias, position_bias, cotangent):
    relative = relative_index()
    params = tuple((tensor.astype(jnp.float32) for tensor in (first_gain, first_offset, input_weight, input_bias, output_weight, output_bias, second_gain, second_offset, expand_weight, expand_bias, reduce_weight, reduce_bias, position_bias)))
    samples = fields.astype(jnp.float32).reshape(SAMPLES, H, Z, W, C)
    cot_samples = cotangent.astype(jnp.float32).reshape(SAMPLES, H, Z, W, C)
    window_kind = window_types.reshape(Z // WZ, WROWS)

    def per_sample(totals, inputs):
        sample_field, sample_cot, group_id = inputs

        def forward(field_in, params_in):
            return block_forward(field_in, params_in, group_id, window_kind, window_masks, relative)
        result, pullback = jax.vjp(forward, sample_field, params)
        field_grad, param_grads = pullback(sample_cot)
        totals = jax.tree.map(jnp.add, totals, param_grads)
        return (totals, (result.astype(jnp.bfloat16), field_grad.astype(jnp.bfloat16)))
    initial = tuple((jnp.zeros_like(tensor) for tensor in params))
    totals, (results, field_grads) = lax.scan(per_sample, initial, (samples, cot_samples, group_index))
    output = results.reshape(LATROWS, Z, W, C)
    input_grad = field_grads.reshape(LATROWS, Z, W, C)
    return (output, input_grad, totals[0], totals[1], totals[2], totals[3], totals[4], totals[5], totals[6], totals[7], totals[8], totals[9], totals[10], totals[11], totals[12])
```

```python
import functools

import jax
import jax.numpy as jnp
import numpy as np
from jax import lax
from jax.experimental import pallas as pl
from jax.experimental.pallas import tpu as pltpu
from jax.sharding import PartitionSpec as P

WZ = 2
WH = 6
WW = 12
WROWS = 2
TOKENS = WZ * WH * WW
GROUP = 4
PADDED = 640
SPAN = 2 * WW - 1
MASKED = -1e30
BF = jnp.bfloat16
F32 = jnp.float32


def dot(a, b):
    return lax.dot_general(a, b, (((1,), (0,)), ((), ())), preferred_element_type=F32)


def dot_nt(a, b):
    return lax.dot_general(a, b, (((1,), (1,)), ((), ())), preferred_element_type=F32)


def dot_tn(a, b):
    return lax.dot_general(a, b, (((0,), (0,)), ((), ())), preferred_element_type=F32)


def one_hot(index, size):
    return (np.asarray(index)[:, None] == np.arange(size)[None, :]).astype(np.float32)


def window_order(columns):
    windows = columns // WW
    n, z, h, w = np.meshgrid(
        np.arange(windows), np.arange(WZ), np.arange(WH), np.arange(WW), indexing="ij"
    )
    half_row = WH // 2
    quadrant = (h // half_row) * WZ + z
    row = (h % half_row) * columns + (n * WW + w + WW // 2) % columns
    full = one_hot((quadrant * half_row * columns + row).reshape(-1), 4 * half_row * columns)
    return full.reshape(full.shape[0], 4, half_row * columns).transpose(1, 0, 2)


def column_maps():
    cells = WZ * WH
    out = np.zeros((WW, cells, SPAN, cells, WW), np.float32)
    for wj in range(WW):
        for wi in range(WW):
            for c in range(cells):
                out[wj, c, wi - wj + WW - 1, c, wi] = 1.0
    return out.reshape(WW, cells * SPAN, cells * WW)


def token_rows():
    j = np.arange(TOKENS)
    return one_hot((j % WW) * 16 + j // WW, WW * 16)


def head_places():
    return np.stack([one_hot(h * TOKENS + np.arange(TOKENS), PADDED) for h in range(GROUP)])


def fold_map():
    return sum(head_places())


def bias_kernel(table_ref, cols_ref, rows_ref, places_ref, own_ref, other_ref, out_ref, held):
    heads = held.shape[0]
    for wj in range(WW):
        part = dot(table_ref[...], cols_ref[wj]).astype(BF)
        for h in range(heads):
            held[h, 16 * wj : 16 * wj + 16, :] = part[16 * h : 16 * h + 16]
    same = own_ref[...] == other_ref[...]
    for g in range(heads // GROUP):
        total = jnp.zeros((TOKENS, PADDED), F32)
        for h in range(GROUP):
            ordered = dot(rows_ref[...], held[g * GROUP + h]).astype(BF)
            total = total + dot(ordered, places_ref[h])
        out_ref[g] = jnp.where(same, total, MASKED)


def fold_kernel(sums_ref, cols_ref, rows_ref, places_ref, out_ref, held):
    groups = sums_ref.shape[0]
    for g in range(groups):
        value = sums_ref[g]
        high = value.astype(BF)
        low = (value - high.astype(F32)).astype(BF)
        for part_index, part in enumerate((high, low)):
            for h in range(GROUP):
                block = dot_nt(part, places_ref[h]).astype(BF)
                ordered = dot_tn(rows_ref[...], block).astype(BF)
                spot = (g * GROUP + h) * 16
                for wj in range(WW):
                    held[part_index, wj, spot : spot + 16, :] = ordered[16 * wj : 16 * wj + 16]
    total = jnp.zeros(out_ref.shape, F32)
    for wj in range(WW):
        for part_index in range(2):
            total = total + dot_nt(held[part_index, wj], cols_ref[wj])
    out_ref[...] = total


def norm_parts(values):
    centre = values - jnp.mean(values, axis=-1, keepdims=True)
    spread = jnp.mean(centre * centre, axis=-1, keepdims=True)
    root = lax.rsqrt(spread + 1e-05)
    return centre * root, root


def norm_back(grad, gain, xhat, root):
    u = grad * gain
    return (
        u - jnp.mean(u, axis=-1, keepdims=True) - xhat * jnp.mean(u * xhat, axis=-1, keepdims=True)
    ) * root


def stacked_heads(block, head_size):
    lane = lax.broadcasted_iota(jnp.int32, block.shape, 1) // head_size
    zero = jnp.zeros_like(block)
    pieces = [jnp.where(lane == h, block, zero) for h in range(GROUP)]
    pieces.append(jnp.zeros((PADDED - GROUP * block.shape[0], block.shape[1]), block.dtype))
    return jnp.concatenate(pieces, axis=0)


def own_lanes(full, head_size):
    row = lax.broadcasted_iota(jnp.int32, full.shape, 0) // head_size
    lane = lax.broadcasted_iota(jnp.int32, full.shape, 1)
    start = row * TOKENS
    return jnp.where((lane >= start) & (lane < start + TOKENS), full, 0.0)


def softmax_t(keys, queries, bias, scale):
    scores = dot_nt(keys, queries) * scale + bias
    exponent = jnp.exp(scores - jnp.max(scores, axis=0, keepdims=True))
    return exponent / jnp.sum(exponent, axis=0, keepdims=True)


def scatter_rows(keep_out, send_out, me, block, value):
    value = value.astype(BF)
    size = value.shape[0] // 8
    for q in range(8):
        rel = q ^ me
        piece = value[q * size : (q + 1) * size]

        @pl.when(rel < 4)
        def _(piece=piece, rel=rel):
            keep_out[rel, block * size : (block + 1) * size] = piece

        @pl.when(rel >= 4)
        def _(piece=piece, rel=rel):
            send_out[rel - 4, block * size : (block + 1) * size] = piece


def scatter_small(keep_out, send_out, me, small):
    start = keep_out.shape[1] - 16
    for q in range(8):
        rel = q ^ me
        row = jnp.broadcast_to(small[q : q + 1, :], (16, small.shape[1])).astype(BF)

        @pl.when(rel < 4)
        def _(row=row, rel=rel):
            keep_out[rel, start : start + 16] = row

        @pl.when(rel >= 4)
        def _(row=row, rel=rel):
            send_out[rel - 4, start : start + 16] = row


def param_row(ref, group):
    return ref[pl.ds(group, 1), :]


def forward_kernel(
    meta, f0, f1, f2, f3, c0, c1, c2, c3, to_win, to_rows, bias_ref, fold_ref,
    g1_ref, o1_ref, win_ref, bin_ref, wout_ref, bout_ref, g2_ref, o2_ref,
    wup_ref, bup_ref, wdn_ref, bdn_ref,
    y0, y1, y2, y3, xw_out, triple_out, att_out, gh_out, keep_out, send_out,
    n2_s, cot_s, acc_s, back_s, small_out,
):
    gid = meta[0]
    me = meta[1]
    channels = xw_out.shape[1]
    tokens = xw_out.shape[0]
    head_size = channels // (GROUP * bias_ref.shape[0])
    scale = head_size**-0.5
    lanes = GROUP * head_size

    def gathered(refs):
        total = dot(to_win[0], refs[0][...])
        for k in range(1, 4):
            total = total + dot(to_win[k], refs[k][...])
        return total

    x = gathered((f0, f1, f2, f3))
    xw_out[...] = x.astype(BF)
    cot_s[...] = gathered((c0, c1, c2, c3)).astype(BF)
    xhat, _ = norm_parts(x)
    normed = (xhat * param_row(g1_ref, gid) + param_row(o1_ref, gid)).astype(BF)
    bias_row = param_row(bin_ref, gid)
    for part in range(3):
        value = dot(normed, win_ref[:, part * channels : (part + 1) * channels])
        if part == 0:
            value = value + bias_row[:, :channels]
        if part == 2:
            value = value + bias_row[:, channels:]
        triple_out[:, part * channels : (part + 1) * channels] = value.astype(BF)

    def window(n, carry):
        rows = pl.ds(pl.multiple_of(n * TOKENS, 16), TOKENS)
        for g in range(channels // lanes):
            lo = g * lanes
            queries = stacked_heads(triple_out[rows, lo : lo + lanes], head_size)
            keys = triple_out[rows, channels + lo : channels + lo + lanes]
            values = triple_out[rows, 2 * channels + lo : 2 * channels + lo + lanes]
            probs = softmax_t(keys, queries, bias_ref[g], scale).astype(BF)
            full = own_lanes(dot_tn(values, probs), head_size).astype(BF)
            att_out[rows, lo : lo + lanes] = dot_nt(fold_ref[...], full).astype(BF)
        return carry

    lax.fori_loop(0, tokens // TOKENS, window, 0)

    mixed = (dot(att_out[...], wout_ref[...]) + param_row(bout_ref, gid)).astype(BF)
    hidden = xw_out[...].astype(F32) + mixed.astype(F32)
    xhat2, root2 = norm_parts(hidden)
    gain2 = param_row(g2_ref, gid)
    n2_s[...] = (xhat2 * gain2 + param_row(o2_ref, gid)).astype(BF)
    acc_s[...] = hidden + param_row(bdn_ref, gid)
    back_s[...] = jnp.zeros_like(back_s)
    step = channels

    def put(block, value):
        scatter_rows(keep_out, send_out, me, block, value)

    bup = param_row(bup_ref, gid)
    for k in range(wup_ref.shape[1] // step):
        cols = slice(k * step, (k + 1) * step)
        up = wup_ref[:, cols]
        down = wdn_ref[cols, :]
        expanded = dot(n2_s[...], up) + bup[:, cols]
        cdf = 0.5 * (1.0 + lax.erf(expanded * (0.5**0.5)))
        active = (expanded * cdf).astype(BF)
        slope = cdf + expanded * (jnp.exp(-0.5 * expanded * expanded) * 0.3989422804014327)
        grad_expanded = (dot_nt(cot_s[...], down) * slope).astype(BF)
        acc_s[...] += dot(active, down)
        back_s[...] += dot_nt(grad_expanded, up)
        put(k, dot_tn(n2_s[...], grad_expanded))
        put(4 + k, dot_tn(active, cot_s[...]))
        small_out[k : k + 1, :] = jnp.sum(grad_expanded.astype(F32), axis=0, keepdims=True)

    out = acc_s[...].astype(BF)
    for k, ref in enumerate((y0, y1, y2, y3)):
        ref[...] = dot(to_rows[k], out).astype(BF)
    cot = cot_s[...].astype(F32)
    grad = back_s[...]
    small_out[4:5, :] = jnp.sum(cot, axis=0, keepdims=True)
    small_out[5:6, :] = jnp.sum(grad * xhat2, axis=0, keepdims=True)
    small_out[6:7, :] = jnp.sum(grad, axis=0, keepdims=True)
    small_out[7:8, :] = jnp.zeros((1, channels), F32)
    scatter_small(keep_out, send_out, me, small_out[...])
    gh_out[...] = cot + norm_back(grad, gain2, xhat2, root2)


def backward_kernel(
    meta, xw_ref, triple_ref, att_ref, gh_ref, to_rows, bias_ref, fold_ref,
    g1_ref, o1_ref, win_ref, wout_ref,
    d0, d1, d2, d3, keep_out, send_out, sums_out,
    ga_s, gt_s, small_out,
):
    gid = meta[0]
    me = meta[1]
    channels = xw_ref.shape[1]
    tokens = xw_ref.shape[0]
    head_size = channels // (GROUP * bias_ref.shape[0])
    scale = head_size**-0.5
    lanes = GROUP * head_size

    def put(block, value):
        scatter_rows(keep_out, send_out, me, block, value)

    grad_mixed = gh_ref[...].astype(BF)
    put(3, dot_tn(att_ref[...], grad_mixed))
    small_out[0:1, :] = jnp.sum(grad_mixed.astype(F32), axis=0, keepdims=True)
    ga_s[...] = dot_nt(grad_mixed, wout_ref[...]).astype(BF)
    sums_out[...] = jnp.zeros_like(sums_out)

    def window(n, carry):
        rows = pl.ds(pl.multiple_of(n * TOKENS, 16), TOKENS)
        for g in range(channels // lanes):
            lo = g * lanes
            queries = stacked_heads(triple_ref[rows, lo : lo + lanes], head_size)
            keys = triple_ref[rows, channels + lo : channels + lo + lanes]
            values = triple_ref[rows, 2 * channels + lo : 2 * channels + lo + lanes]
            probs = softmax_t(keys, queries, bias_ref[g], scale)
            grad_att = stacked_heads(ga_s[rows, lo : lo + lanes], head_size)
            grad_probs = dot_nt(values, grad_att)
            row_dot = jnp.sum(probs * grad_probs, axis=0, keepdims=True)
            grad_scores = (probs * (grad_probs - row_dot)).astype(BF)
            sums_out[g] += grad_scores.astype(F32)
            full = own_lanes(dot_tn(keys, grad_scores) * scale, head_size).astype(BF)
            gt_s[rows, lo : lo + lanes] = dot_nt(fold_ref[...], full).astype(BF)
            gt_s[rows, channels + lo : channels + lo + lanes] = (
                dot(grad_scores, queries) * scale
            ).astype(BF)
            gt_s[rows, 2 * channels + lo : 2 * channels + lo + lanes] = dot(
                probs.astype(BF), grad_att
            ).astype(BF)
        return carry

    lax.fori_loop(0, tokens // TOKENS, window, 0)

    xhat, root = norm_parts(xw_ref[...].astype(F32))
    gain = param_row(g1_ref, gid)
    normed = (xhat * gain + param_row(o1_ref, gid)).astype(BF)
    grad = jnp.zeros((tokens, channels), F32)
    for part in range(3):
        cols = slice(part * channels, (part + 1) * channels)
        piece = gt_s[:, cols]
        put(part, dot_tn(normed, piece))
        grad = grad + dot_nt(piece, win_ref[:, cols])
        if part != 1:
            row = 1 + part // 2
            small_out[row : row + 1, :] = jnp.sum(piece.astype(F32), axis=0, keepdims=True)
    small_out[3:4, :] = jnp.sum(grad * xhat, axis=0, keepdims=True)
    small_out[4:5, :] = jnp.sum(grad, axis=0, keepdims=True)
    small_out[5:8, :] = jnp.zeros((3, channels), F32)
    scatter_small(keep_out, send_out, me, small_out[...])
    shifted = norm_back(grad, gain, xhat, root).astype(BF)
    result = (gh_ref[...] + shifted.astype(F32)).astype(BF)
    for k, ref in enumerate((d0, d1, d2, d3)):
        ref[...] = dot(to_rows[k], result).astype(BF)


def spread_groups(coef, pieces, write):
    count = len(pieces)
    values = [piece.astype(F32) for piece in pieces]
    for g in range(4):
        total = values[0] * coef[g * count]
        for k in range(1, count):
            total = total + values[k] * coef[g * count + k]
        write(g, total)


def finish_kernel(wide, tall, small_slots, meta, coef, *refs):
    halves, outs = refs[:16], refs[16:]
    rel = pl.program_id(0)
    q = rel ^ meta[1]
    size = outs[0].shape[1]
    count = halves[0].shape[0]
    channels = halves[0].shape[2]

    for r in range(8):

        @pl.when(rel == r)
        def _(first=halves[r], second=halves[8 + r]):
            def source(block):
                split = first.shape[1] // size
                ref, at = (first, block) if block < split else (second, block - split)
                return [ref[k, at * size : (at + 1) * size, :] for k in range(count)]

            for block in range(wide):

                def write(g, value, block=block):
                    outs[0][g, :, block * channels : (block + 1) * channels] = value

                spread_groups(coef, source(block), write)
            for block in range(tall):

                def write(g, value, block=block):
                    outs[1][g, block, 0] = value

                spread_groups(coef, source(wide + block), write)
            start = second.shape[1] - 16
            rows = [second[k, start : start + 16, :] for k in range(count)]
            for slot, (out, column) in enumerate(small_slots):

                @pl.when(q == slot)
                def _(out=out, column=column):
                    def write(g, value):
                        outs[2 + out][g : g + 1, column : column + channels] = value[0:1]

                    spread_groups(coef, rows, write)


def finish_positions_kernel(meta, coef, *refs):
    stacks, out = refs[:-1], refs[-1]
    count = len(stacks) // 2
    rel = pl.program_id(0)
    for r in range(8):

        @pl.when(rel == r)
        def _(r=r):
            pieces = [stacks[(r // 4) * count + k][r % 4] for k in range(count)]

            def write(g, value):
                out[g, 0] = value

            spread_groups(coef, pieces, write)


def whole(array_or_shape):
    shape = getattr(array_or_shape, "shape", array_or_shape)
    return pl.BlockSpec(shape, lambda i, *_: (0,) * len(shape))


def stack_member(array):
    return pl.BlockSpec((None,) + array.shape[1:], lambda i, m, *_: (m[0],) + (0,) * (array.ndim - 1))


def call(kernel, scalars, inputs, in_specs, out_shapes, out_specs, scratch, grid=(1,), flops=0, moved=0):
    return pl.pallas_call(
        kernel,
        grid_spec=pltpu.PrefetchScalarGridSpec(
            num_scalar_prefetch=len(scalars),
            grid=grid,
            in_specs=in_specs,
            out_specs=out_specs,
            scratch_shapes=scratch,
        ),
        out_shape=out_shapes,
        compiler_params=pltpu.CompilerParams(vmem_limit_bytes=60 * 1024 * 1024),
        cost_estimate=pl.CostEstimate(flops=flops, bytes_accessed=moved, transcendentals=0),
    )(*scalars, *inputs)


def xor_pairs(axis, distance):
    return [(i, i ^ distance) for i in range(lax.axis_size(axis))]


def swap(value, axis, distance):
    return lax.ppermute(value, axis, xor_pairs(axis, distance))


def swap_both(value, lev_distance, lat_distance):
    lev, lat = lax.axis_size("lev"), lax.axis_size("lat")
    pairs = [
        (a * lat + b, (a ^ lev_distance) * lat + (b ^ lat_distance))
        for a in range(lev)
        for b in range(lat)
    ]
    return lax.ppermute(value, ("lev", "lat"), pairs)


def lev_step(value, step, cross):
    lev, lat = lax.axis_size("lev"), lax.axis_size("lat")
    pairs = [
        (a * lat + b, (a + step) % lev * lat + (b ^ cross)) for a in range(lev) for b in range(lat)
    ]
    return lax.ppermute(value, ("lev", "lat"), pairs)


def quadrants(block):
    half = WH // 2
    rows = half * block.shape[2]

    def flat(part):
        return part.reshape(rows, block.shape[3])

    return [
        flat(block[half:, 1]),
        lev_step(flat(block[half:, 0]), -1, 0),
        swap(flat(block[:half, 1]), "lat", 1),
        lev_step(flat(block[:half, 0]), -1, 1),
    ]


def from_quadrants(parts, shape):
    half = WH // 2
    own, lev, lat, both = parts
    lev = lev_step(lev, 1, 0)
    lat = swap(lat, "lat", 1)
    both = lev_step(both, 1, 1)
    own, lev, lat, both = (p.reshape((half,) + shape[2:]) for p in (own, lev, lat, both))
    return jnp.concatenate(
        [jnp.stack([both, lat], axis=1), jnp.stack([lev, own], axis=1)], axis=0
    )


def reduce_plane(keep, send):
    total = (keep.astype(F32) + swap(send, "lev", 1).astype(F32)).astype(BF)
    arrived = [
        swap(total[1], "lat", 1),
        swap(total[2], "lev", 2),
        swap_both(total[3], 2, 1),
    ]
    result = total[0].astype(F32)
    for part in arrived:
        result = result + part.astype(F32)
    return result.astype(BF)


def across_samples(share, hot):
    lat = lax.axis_size("lat")
    samples = lat // WROWS
    if samples <= hot.shape[0]:
        entries = [share]
        for k in range(1, samples):
            pairs = [(i, (i + WROWS * k) % lat) for i in range(lat)]
            entries.append(lax.ppermute(share, "lat", pairs))
        return entries
    groups = [[s * WROWS + b for s in range(samples)] for b in range(WROWS)]
    weight = hot.reshape((-1,) + (1,) * share.ndim)
    total = lax.psum(weight * share.astype(F32)[None], "lat", axis_index_groups=groups)
    total = total.astype(BF)
    return [total[k] for k in range(total.shape[0])]


def across_plane(first, second):
    first_x = swap(first, "lev", 2)
    second_y = swap(second, "lat", 1)
    first_y = swap(first, "lat", 1)
    second_x = swap(second, "lev", 2)
    first_xy = swap(first_x, "lat", 1)
    second_xy = swap(second_y, "lev", 2)
    firsts = [first, first_y, first_x, first_xy]
    seconds = [second, second_y, second_x, second_xy]
    firsts += [swap(v, "lev", 1) for v in firsts]
    seconds += [swap(v, "lev", 1) for v in seconds]
    return firsts + seconds


def finish(pieces, wide, tall, small_slots, small_widths, meta, coef):
    count, _, channels = pieces[0].shape
    size = channels // 8
    out_shapes = [
        jax.ShapeDtypeStruct((4, channels, wide * channels), F32),
        jax.ShapeDtypeStruct((4, tall, 8, size, channels), F32),
    ] + [jax.ShapeDtypeStruct((4, width), F32) for width in small_widths]
    out_specs = [
        pl.BlockSpec((4, size, wide * channels), lambda r, m, c: (0, r ^ m[1], 0)),
        pl.BlockSpec((4, tall, 1, size, channels), lambda r, m, c: (0, 0, r ^ m[1], 0, 0)),
    ] + [whole((4, width)) for width in small_widths]
    outs = call(
        functools.partial(finish_kernel, wide, tall, small_slots),
        [meta, coef],
        pieces,
        [whole(p) for p in pieces],
        out_shapes,
        out_specs,
        [],
        grid=(8,),
        flops=10**7,
        moved=25 * 10**6,
    )
    return [outs[0], outs[1].reshape(4, tall * channels, channels)] + list(outs[2:])


def body(
    fields,
    group_index,
    window_types,
    window_masks,
    first_gain,
    first_offset,
    input_weight,
    input_bias,
    output_weight,
    output_bias,
    second_gain,
    second_offset,
    expand_weight,
    expand_bias,
    reduce_weight,
    reduce_bias,
    position_bias,
    cotangent,
):
    columns = fields.shape[2]
    channels = fields.shape[3]
    heads = position_bias.shape[2]
    sets = position_bias.shape[0]
    groups = heads // GROUP
    cells = WZ * WH
    tokens = columns * cells
    rows = tokens // 4
    lat_index = lax.axis_index("lat")
    lev_index = lax.axis_index("lev")
    samples = lax.axis_size("lat") // WROWS
    sample_index = lat_index // WROWS
    half = lat_index % WROWS
    kind_index = lev_index * WROWS + half
    group_id = group_index[sample_index]
    kind_id = window_types[kind_index]
    me = (lev_index % 2) * 4 + (lev_index // 2) * 2 + half
    meta = jnp.stack([group_id, me]).astype(jnp.int32)
    hot = (jnp.arange(sets) == group_id).astype(F32)
    if samples <= sets:
        order = (sample_index - jnp.arange(samples)) % samples
        coef = (group_index[order][None, :] == jnp.arange(sets)[:, None]).astype(F32).reshape(-1)
    else:
        coef = jnp.eye(sets, dtype=F32).reshape(-1)

    maps = window_order(columns)
    to_win = jnp.asarray(maps, BF)
    to_rows = jnp.asarray(maps.transpose(0, 2, 1), BF)
    cols_map = jnp.asarray(column_maps(), BF)
    rows_map = jnp.asarray(token_rows(), BF)
    places = jnp.asarray(head_places(), BF)
    fold = jnp.asarray(fold_map(), BF)

    field_parts = quadrants(fields)
    cot_parts = quadrants(cotangent)

    labels = window_masks[lev_index, half]
    other = jnp.pad(jnp.tile(labels, GROUP), (0, PADDED - GROUP * TOKENS))[None, :]
    table = position_bias[group_id, kind_id].reshape(heads, WZ, WZ, WH, WH, SPAN)
    table = table.transpose(0, 2, 4, 1, 3, 5).reshape(heads, cells, cells * SPAN)
    table = jnp.pad(table, ((0, 0), (0, 16 - cells), (0, 0))).reshape(heads * 16, cells * SPAN)
    inputs = [table, cols_map, rows_map, places, labels[:, None], other]
    bias_map = call(
        bias_kernel,
        [],
        inputs,
        [whole(v) for v in inputs],
        jax.ShapeDtypeStruct((groups, TOKENS, PADDED), F32),
        whole((groups, TOKENS, PADDED)),
        [pltpu.VMEM((heads, 16 * WW, TOKENS), BF)],
        flops=10**9,
        moved=4 * 10**6,
    )

    hidden_units = expand_weight.shape[2]
    assert hidden_units == 4 * channels
    up_rows = 8 * (channels // 8) + 16
    low_rows = 4 * (channels // 8) + 16
    inputs = (
        field_parts
        + cot_parts
        + [to_win, to_rows, bias_map, fold, first_gain, first_offset, input_weight, input_bias]
        + [output_weight, output_bias, second_gain, second_offset, expand_weight, expand_bias]
        + [reduce_weight, reduce_bias]
    )
    stacked = {id(v) for v in (input_weight, output_weight, expand_weight, reduce_weight)}
    specs = [stack_member(v) if id(v) in stacked else whole(v) for v in inputs]
    quadrant = jax.ShapeDtypeStruct((rows, channels), BF)
    shapes = [quadrant] * 4 + [
        jax.ShapeDtypeStruct((tokens, channels), BF),
        jax.ShapeDtypeStruct((tokens, 3 * channels), BF),
        jax.ShapeDtypeStruct((tokens, channels), BF),
        jax.ShapeDtypeStruct((tokens, channels), F32),
        jax.ShapeDtypeStruct((4, up_rows, channels), BF),
        jax.ShapeDtypeStruct((4, up_rows, channels), BF),
    ]
    y0, y1, y2, y3, xw, triple, att, grad_hidden, keep, send = call(
        forward_kernel,
        [meta],
        inputs,
        specs,
        shapes,
        [whole(v) for v in shapes],
        [
            pltpu.VMEM((tokens, channels), BF),
            pltpu.VMEM((tokens, channels), BF),
            pltpu.VMEM((tokens, channels), F32),
            pltpu.VMEM((tokens, channels), F32),
            pltpu.VMEM((8, channels), F32),
        ],
        flops=10**10,
        moved=3 * 10**7,
    )

    inputs = [xw, triple, att, grad_hidden, to_rows, bias_map, fold, first_gain, first_offset]
    inputs += [input_weight, output_weight]
    specs = [stack_member(v) if id(v) in stacked else whole(v) for v in inputs]
    shapes = [quadrant] * 4 + [
        jax.ShapeDtypeStruct((4, low_rows, channels), BF),
        jax.ShapeDtypeStruct((4, low_rows, channels), BF),
        jax.ShapeDtypeStruct((groups, TOKENS, PADDED), F32),
    ]
    d0, d1, d2, d3, low_keep, low_send, score_sums = call(
        backward_kernel,
        [meta],
        inputs,
        specs,
        shapes,
        [whole(v) for v in shapes],
        [
            pltpu.VMEM((tokens, channels), BF),
            pltpu.VMEM((tokens, 3 * channels), BF),
            pltpu.VMEM((8, channels), F32),
        ],
        flops=10**10,
        moved=3 * 10**7,
    )

    inputs = [score_sums, cols_map, rows_map, places]
    table_grad = call(
        fold_kernel,
        [],
        inputs,
        [whole(v) for v in inputs],
        jax.ShapeDtypeStruct((heads * 16, cells * SPAN), F32),
        whole((heads * 16, cells * SPAN)),
        [pltpu.VMEM((2, WW, heads * 16, TOKENS), BF)],
        flops=10**9,
        moved=4 * 10**6,
    )
    table_grad = table_grad.astype(BF).reshape(heads, 16, cells * SPAN)[:, :cells]
    table_grad = table_grad.reshape(heads, WZ, WH, WZ, WH, SPAN).transpose(0, 3, 1, 4, 2, 5)
    table_grad = table_grad.reshape(heads, -1)

    share = reduce_plane(keep, send)
    stack = jnp.stack(across_samples(share, hot))
    split = 4 * (channels // 8)
    up_pieces = across_plane(stack[:, :split], stack[:, split:])
    up_grad, down_grad, bup_grad, bdn_grad, g2_grad, o2_grad = finish(
        up_pieces,
        4,
        4,
        [(0, k * channels) for k in range(4)] + [(1, 0), (2, 0), (3, 0)],
        [4 * channels, channels, channels, channels],
        meta,
        coef,
    )

    share = reduce_plane(low_keep, low_send)
    stack = jnp.stack(across_samples(share, hot))
    split = 2 * (channels // 8)
    low_pieces = across_plane(stack[:, :split], stack[:, split:])
    in_grad, out_grad, bout_grad, bin_grad, g1_grad, o1_grad = finish(
        low_pieces,
        3,
        1,
        [(0, 0), (1, 0), (1, channels), (2, 0), (3, 0)],
        [channels, 2 * channels, channels, channels],
        meta,
        coef,
    )

    along_x = swap(table_grad, "lev", 2)
    along_y = swap(table_grad, "lat", 1)
    along_xy = swap(along_x, "lat", 1)
    plane = jnp.stack([table_grad, along_y, along_x, along_xy])
    entries = across_samples(plane, hot)
    entries = entries + [swap(v, "lev", 1) for v in entries]
    device = jnp.arange(8) ^ me
    kinds = window_types[(device // 2 % 2) * 4 + (device // 4) * 2 + device % 2]
    shape = position_bias.shape
    position_grad = call(
        finish_positions_kernel,
        [kinds, coef],
        entries,
        [whole(v) for v in entries],
        jax.ShapeDtypeStruct(shape, F32),
        pl.BlockSpec((sets, 1) + shape[2:], lambda r, t, c: (0, t[r], 0, 0)),
        [],
        grid=(8,),
        flops=10**7,
        moved=8 * 10**6,
    )

    output = from_quadrants((y0, y1, y2, y3), fields.shape)
    input_grad = from_quadrants((d0, d1, d2, d3), fields.shape)
    return (
        output,
        input_grad,
        g1_grad,
        o1_grad,
        in_grad,
        bin_grad,
        out_grad,
        bout_grad,
        g2_grad,
        o2_grad,
        up_grad,
        bup_grad,
        down_grad,
        bdn_grad,
        position_grad,
    )


def solution(mesh):
    slab = P("lat", "lev", None, None)
    return jax.shard_map(
        body,
        mesh=mesh,
        in_specs=(slab,) + (P(),) * 16 + (slab,),
        out_specs=(slab, slab) + (P(),) * 13,
        check_vma=False,
    )
```

```python
import functools

import jax
import jax.numpy as jnp
import numpy as np
from jax import lax
from jax.experimental import pallas as pl
from jax.experimental.pallas import tpu as pltpu
from jax.sharding import PartitionSpec as P

WZ = 2
WH = 6
WW = 12
WROWS = 2
TOKENS = WZ * WH * WW
GROUP = 4
PADDED = 640
SPAN = 2 * WW - 1
MASKED = -1e30
LOG2E = 1.4426950408889634
BF = jnp.bfloat16
F32 = jnp.float32


def dot(a, b):
    return lax.dot_general(a, b, (((1,), (0,)), ((), ())), preferred_element_type=F32)


def dot_nt(a, b):
    return lax.dot_general(a, b, (((1,), (1,)), ((), ())), preferred_element_type=F32)


def dot_tn(a, b):
    return lax.dot_general(a, b, (((0,), (0,)), ((), ())), preferred_element_type=F32)


def one_hot(index, size):
    return (np.asarray(index)[:, None] == np.arange(size)[None, :]).astype(np.float32)


def window_order(columns):
    windows = columns // WW
    n, h, w = np.meshgrid(np.arange(windows), np.arange(WH), np.arange(WW), indexing="ij")
    source = h * columns + (n * WW + w + WW // 2) % columns
    return one_hot(source.reshape(-1), WH * columns)


def column_maps():
    cells = WZ * WH
    out = np.zeros((WW, cells, SPAN, cells, WW), np.float32)
    for wj in range(WW):
        for wi in range(WW):
            for c in range(cells):
                out[wj, c, wi - wj + WW - 1, c, wi] = 1.0
    return out.reshape(WW, cells * SPAN, cells * WW)


def token_rows():
    j = np.arange(TOKENS)
    return one_hot((j % WW) * 16 + j // WW, WW * 16)


def head_places():
    return np.stack([one_hot(h * TOKENS + np.arange(TOKENS), PADDED) for h in range(GROUP)])


def fold_map():
    return sum(head_places())


def head_lanes(lanes):
    return np.repeat(np.eye(GROUP, dtype=np.float32), lanes // GROUP, axis=1)


def select_kernel(group_index, window_types, tables_ref, out_ref):
    heads, kinds, positions = tables_ref.shape
    place = lax.axis_index("lev") * WROWS + lax.axis_index("lat") % WROWS
    kind = window_types[place]
    shape = (heads, heads * kinds)
    row = lax.broadcasted_iota(jnp.int32, shape, 0)
    col = lax.broadcasted_iota(jnp.int32, shape, 1)
    pick = jnp.where(col == row * kinds + kind, 1.0, 0.0).astype(BF)
    tables = tables_ref[...].astype(F32).reshape(heads * kinds, positions).astype(BF)
    out_ref[...] = dot(pick, tables).astype(BF)


def bias_kernel(masks_ref, table_ref, cols_ref, rows_ref, places_ref, fold_ref, out_ref, held):
    heads = held.shape[0]
    for wj in range(WW):
        part = dot(table_ref[...], cols_ref[wj]).astype(BF)
        for h in range(heads):
            held[h, 16 * wj : 16 * wj + 16, :] = part[16 * h : 16 * h + 16]
    half = lax.axis_index("lat") % WROWS
    labels = masks_ref[lax.axis_index("lev"), pl.ds(half, 1), :].astype(F32)
    top = lax.broadcasted_iota(jnp.int32, (8, TOKENS), 0) == 0
    labels = jnp.where(top, jnp.broadcast_to(labels, (8, TOKENS)), 0.0)
    across = dot(jnp.ones((TOKENS, 8), BF), dot(labels.astype(BF), fold_ref[...]).astype(BF))
    down = dot_tn(labels.astype(BF), jnp.ones((8, PADDED), BF))
    same = jnp.abs(across - down) < 0.5
    for g in range(heads // GROUP):
        total = dot(held[g * GROUP], places_ref[0])
        for h in range(1, GROUP):
            total = total + dot(held[g * GROUP + h], places_ref[h])
        out_ref[g] = jnp.where(same, dot(rows_ref[...], total.astype(BF)), MASKED) * LOG2E


def fold_kernel(sums_ref, cols_ref, rows_ref, places_ref, out_ref, held):
    groups = sums_ref.shape[0]
    for g in range(groups):
        value = sums_ref[g]
        high = value.astype(BF)
        low = (value - high.astype(F32)).astype(BF)
        for index, part in enumerate((high, low)):
            ordered = dot(rows_ref[...], part).astype(BF)
            for h in range(GROUP):
                block = dot_nt(ordered, places_ref[h]).astype(BF)
                spot = (g * GROUP + h) * 16
                for wj in range(WW):
                    held[index, wj, spot : spot + 16, :] = block[16 * wj : 16 * wj + 16]
    total = jnp.zeros(out_ref.shape, F32)
    for wj in range(WW):
        for index in range(2):
            total = total + dot_nt(held[index, wj], cols_ref[wj])
    out_ref[...] = total.astype(BF)


def norm_parts(values):
    centre = values - jnp.mean(values, axis=-1, keepdims=True)
    spread = jnp.mean(centre * centre, axis=-1, keepdims=True)
    root = lax.rsqrt(spread + 1e-05)
    return centre * root, root


def norm_back(grad, gain, xhat, root):
    u = grad * gain
    return (
        u - jnp.mean(u, axis=-1, keepdims=True) - xhat * jnp.mean(u * xhat, axis=-1, keepdims=True)
    ) * root


def stacked_heads(block, lanes_ref):
    pieces = [block * lanes_ref[h : h + 1, :] for h in range(GROUP)]
    pieces.append(jnp.zeros((PADDED - GROUP * block.shape[0], block.shape[1]), block.dtype))
    return jnp.concatenate(pieces, axis=0)


def own_head(full):
    size = full.shape[0] // GROUP
    return jnp.concatenate(
        [
            full[h * size : (h + 1) * size, h * TOKENS : (h + 1) * TOKENS]
            for h in range(GROUP)
        ],
        axis=0,
    )


def softmax_t(keys, queries, bias, scale):
    scores = dot_nt(keys, queries) * (scale * LOG2E) + bias
    exponent = jnp.exp2(scores - jnp.max(scores, axis=0, keepdims=True))
    return exponent * (1.0 / jnp.sum(exponent, axis=0, keepdims=True))


def to_windows(level_map, levels):
    half = WH * WW
    parts = [dot(level_map, level) for level in levels]
    pieces = []
    for n in range(parts[0].shape[0] // half):
        for part in parts:
            pieces.append(part[n * half : (n + 1) * half])
    return jnp.concatenate(pieces, axis=0)


def to_levels(level_map, value):
    half = WH * WW
    count = value.shape[0] // (2 * half)
    quadrants = [None] * 4
    for z in range(WZ):
        level = [value[(2 * n + z) * half : (2 * n + z + 1) * half] for n in range(count)]
        level = dot(level_map, jnp.concatenate(level, axis=0).astype(BF))
        rows = level.shape[0] // 2
        for side in range(2):
            quadrants[side * WZ + z] = level[side * rows : (side + 1) * rows].astype(BF)
    return quadrants


def place_slot(keep_out, send_out, rel, rows, value):
    @pl.when(rel < 4)
    def _():
        keep_out[rel, rows] = value

    if isinstance(send_out, (list, tuple)):
        for k, out in enumerate(send_out):

            @pl.when(rel == 4 + k)
            def _(out=out):
                out[0, rows] = value

    else:

        @pl.when(rel >= 4)
        def _():
            send_out[rel - 4, rows] = value


def scatter_rows(keep_out, send_out, me, block, value):
    value = value.astype(BF)
    size = value.shape[0] // 8
    for q in range(8):
        rows = slice(block * size, (block + 1) * size)
        place_slot(keep_out, send_out, q ^ me, rows, value[q * size : (q + 1) * size])


def scatter_small(keep_out, send_out, me, small):
    start = keep_out.shape[1] - 16
    for q in range(8):
        row = jnp.broadcast_to(small[q : q + 1, :], (16, small.shape[1])).astype(BF)
        place_slot(keep_out, send_out, q ^ me, slice(start, start + 16), row)


def my_set(group_index):
    return group_index[lax.axis_index("lat") // WROWS]


def my_slot():
    lev = lax.axis_index("lev")
    return (lev % 2) * 4 + (lev // 2) * 2 + lax.axis_index("lat") % WROWS


def entry_sets(group_index, count, sets):
    samples = lax.axis_size("lat") // WROWS
    if samples > sets:
        return list(range(sets)), [True] * sets
    owners = [group_index[k] for k in range(count)]
    first = []
    for k in range(count):
        fresh = jnp.bool_(True)
        for j in range(k):
            fresh = fresh & (owners[j] != owners[k])
        first.append(fresh)
    return owners, first


def param_row(ref, group):
    return ref[pl.ds(group, 1), :]


def forward_kernel(
    group_index, f0, f1, f2, f3, to_win, to_rows, bias_ref, lanes_ref,
    g1_ref, o1_ref, win_ref, bin_ref, wout_ref, bout_ref, g2_ref, o2_ref,
    wup_ref, bup_ref, wdn_ref, bdn_ref,
    y0, y1, y2, y3, xw_out, triple_out, att_out, gh_out, keep_out, send_out,
    n2_s, n2t_s, cot_s, acc_s, back_s, small_out,
):
    gid = my_set(group_index)
    me = my_slot()
    tokens, channels = xw_out.shape
    lanes = lanes_ref.shape[1]
    scale = (lanes // GROUP) ** -0.5

    def gathered(which):
        levels = [
            jnp.concatenate([low[which].astype(F32), high[which].astype(F32)], axis=0).astype(BF)
            for low, high in ((f0, f2), (f1, f3))
        ]
        return to_windows(to_win[...], levels)

    x = gathered(0)
    xw_out[...] = x.astype(BF)
    cot_s[...] = gathered(1).astype(BF)
    xhat, _ = norm_parts(x)
    normed = (xhat * param_row(g1_ref, gid) + param_row(o1_ref, gid)).astype(BF)
    bias_row = param_row(bin_ref, gid)
    bias_row = jnp.concatenate(
        [bias_row[:, :channels], jnp.zeros((1, channels), F32), bias_row[:, channels:]], axis=1
    )
    triple_out[...] = (dot(normed, win_ref[...]) + bias_row).astype(BF)

    def window(n, carry):
        rows = pl.ds(pl.multiple_of(n * TOKENS, 16), TOKENS)
        for g in range(channels // lanes):
            lo = g * lanes
            queries = stacked_heads(triple_out[rows, lo : lo + lanes], lanes_ref)
            keys = triple_out[rows, channels + lo : channels + lo + lanes]
            values = triple_out[rows, 2 * channels + lo : 2 * channels + lo + lanes]
            probs = softmax_t(keys, queries, bias_ref[g], scale).astype(BF)
            full = dot_tn(values, probs)
            att_out[rows, lo : lo + lanes] = own_head(full).T.astype(BF)
        return carry

    lax.fori_loop(0, tokens // TOKENS, window, 0, unroll=2)

    mixed = (dot(att_out[...], wout_ref[...]) + param_row(bout_ref, gid)).astype(BF)
    hidden = xw_out[...].astype(F32) + mixed.astype(F32)
    xhat2, root2 = norm_parts(hidden)
    gain2 = param_row(g2_ref, gid)
    n2 = (xhat2 * gain2 + param_row(o2_ref, gid)).astype(BF)
    n2_s[...] = n2
    n2t_s[...] = n2.T
    acc_s[...] = hidden + param_row(bdn_ref, gid)
    per = 2
    step = per * channels

    def put(block, value):
        scatter_rows(keep_out, send_out, me, block, value)

    bup = param_row(bup_ref, gid)
    for k in range(wup_ref.shape[1] // step):
        cols = slice(k * step, (k + 1) * step)
        up = wup_ref[:, cols]
        down = wdn_ref[cols, :]
        expanded = dot(n2_s[...], up) + bup[:, cols]
        cdf = 0.5 * (1.0 + lax.erf(expanded * (0.5**0.5)))
        active = (expanded * cdf).astype(BF)
        slope = cdf + expanded * (jnp.exp(-0.5 * expanded * expanded) * 0.3989422804014327)
        grad_expanded = (dot_nt(cot_s[...], down) * slope).astype(BF)
        acc_s[...] += dot(active, down)
        back = dot_nt(grad_expanded, up)
        back_s[...] = back if k == 0 else back_s[...] + back
        grad_up = dot(n2t_s[...], grad_expanded)
        grad_down = dot_tn(active, cot_s[...])
        sums = jnp.sum(grad_expanded.astype(F32), axis=0, keepdims=True)
        for j in range(per):
            part = slice(j * channels, (j + 1) * channels)
            put(per * k + j, grad_up[:, part])
            put(4 + per * k + j, grad_down[part])
            small_out[per * k + j : per * k + j + 1, :] = sums[:, part]

    for ref, value in zip((y0, y1, y2, y3), to_levels(to_rows[...], acc_s[...])):
        ref[...] = value
    cot = cot_s[...].astype(F32)
    grad = back_s[...]
    small_out[4:5, :] = jnp.sum(cot, axis=0, keepdims=True)
    small_out[5:6, :] = jnp.sum(grad * xhat2, axis=0, keepdims=True)
    small_out[6:7, :] = jnp.sum(grad, axis=0, keepdims=True)
    small_out[7:8, :] = jnp.zeros((1, channels), F32)
    scatter_small(keep_out, send_out, me, small_out[...])
    gh_out[...] = cot + norm_back(grad, gain2, xhat2, root2)


def scores_back_kernel(
    group_index, triple_ref, gh_ref, bias_ref, lanes_ref, wout_ref,
    gt_out, sums_out, ga_s,
):
    channels = gh_ref.shape[1]
    tokens = gh_ref.shape[0]
    lanes = lanes_ref.shape[1]
    scale = (lanes // GROUP) ** -0.5
    ga_s[...] = dot_nt(gh_ref[...].astype(BF), wout_ref[...]).astype(BF)
    sums_out[...] = jnp.zeros_like(sums_out)

    def window(n, carry):
        rows = pl.ds(pl.multiple_of(n * TOKENS, 16), TOKENS)
        for g in range(channels // lanes):
            lo = g * lanes
            queries = stacked_heads(triple_ref[rows, lo : lo + lanes], lanes_ref)
            keys = triple_ref[rows, channels + lo : channels + lo + lanes]
            values = triple_ref[rows, 2 * channels + lo : 2 * channels + lo + lanes]
            probs = softmax_t(keys, queries, bias_ref[g], scale)
            grad_att = stacked_heads(ga_s[rows, lo : lo + lanes], lanes_ref)
            grad_probs = dot_nt(values, grad_att)
            row_dot = jnp.sum(probs * grad_probs, axis=0, keepdims=True)
            grad_scores = (probs * (grad_probs - row_dot)).astype(BF)
            sums_out[g] += grad_scores.astype(F32)
            full = dot_tn(keys, grad_scores)
            gt_out[rows, lo : lo + lanes] = (own_head(full) * scale).T.astype(BF)
            gt_out[rows, channels + lo : channels + lo + lanes] = (
                dot(grad_scores, queries) * scale
            ).astype(BF)
            gt_out[rows, 2 * channels + lo : 2 * channels + lo + lanes] = dot(
                probs.astype(BF), grad_att
            ).astype(BF)
        return carry

    lax.fori_loop(0, tokens // TOKENS, window, 0, unroll=2)


def input_back_kernel(
    group_index, xw_ref, att_ref, gh_ref, gt_ref, to_rows, g1_ref, o1_ref, win_ref,
    d0, d1, d2, d3, low_out, small_out,
):
    gid = my_set(group_index)
    channels = xw_ref.shape[1]
    grad_mixed = gh_ref[...].astype(BF)
    low_out[3] = dot_tn(att_ref[...], grad_mixed).astype(BF)
    small_out[0:1, :] = jnp.sum(grad_mixed.astype(F32), axis=0, keepdims=True)
    xhat, root = norm_parts(xw_ref[...].astype(F32))
    gain = param_row(g1_ref, gid)
    normed = (xhat * gain + param_row(o1_ref, gid)).astype(BF)
    grad_in = dot(normed.T, gt_ref[...])
    grad = dot_nt(gt_ref[...], win_ref[...])
    for part in range(3):
        cols = slice(part * channels, (part + 1) * channels)
        low_out[part] = grad_in[:, cols].astype(BF)
        if part != 1:
            row = 1 + part // 2
            piece = gt_ref[:, cols].astype(F32)
            small_out[row : row + 1, :] = jnp.sum(piece, axis=0, keepdims=True)
    small_out[3:4, :] = jnp.sum(grad * xhat, axis=0, keepdims=True)
    small_out[4:5, :] = jnp.sum(grad, axis=0, keepdims=True)
    small_out[5:8, :] = jnp.zeros((3, channels), F32)
    shifted = norm_back(grad, gain, xhat, root).astype(BF)
    parts = to_levels(to_rows[...], gh_ref[...] + shifted.astype(F32))
    for part, ref in zip(parts, (d0, d1, d2, d3)):
        ref[...] = part


def assemble_kernel(y0, d0, lev_ref, lat_ref, both_ref, y_out, d_out):
    half, columns = WH // 2, y_out.shape[2]
    for k, (own, out) in enumerate(((y0[...], y_out), (d0[...], d_out))):
        for source, row, level in (
            (own, half, 1), (lev_ref[k], half, 0), (lat_ref[k], 0, 1), (both_ref[k], 0, 0)
        ):
            source = source.astype(F32)
            for h in range(half):
                out[row + h, level] = source[h * columns : (h + 1) * columns].astype(BF)


def spread_kernel(low_ref, small_ref, *refs):
    me = my_slot()
    pairs = (len(refs) - 4) // 3
    keep_out, send_out = refs[2 * pairs + 1], refs[2 * pairs + 2]
    for block in range(low_ref.shape[0]):
        scatter_rows(keep_out, send_out, me, block, low_ref[block])
    scatter_small(keep_out, send_out, me, small_ref[...])
    for k in range(pairs):
        refs[2 * pairs + 3 + k][0] = refs[k][...]
        refs[2 * pairs + 3 + k][1] = refs[pairs + k][...]
    refs[-1][...] = refs[2 * pairs][...]


def spread_kernel(low_ref, small_ref, *refs):
    me = my_slot()
    pairs = (len(refs) - 5) // 3
    keep_out, send_outs = refs[2 * pairs], refs[2 * pairs + 1 : 2 * pairs + 5]
    for block in range(low_ref.shape[0]):
        scatter_rows(keep_out, send_outs, me, block, low_ref[block])
    scatter_small(keep_out, send_outs, me, small_ref[...])
    for k in range(pairs):
        refs[2 * pairs + 5 + k][0] = refs[k][...]
        refs[2 * pairs + 5 + k][1] = refs[pairs + k][...]


def first_sum_kernel(keep_ref, *refs):
    arrived, outs = refs[:-4], refs[-4:]
    for k in range(4):
        part = arrived[0][k] if len(arrived) == 1 else arrived[k][0]
        outs[k][...] = (keep_ref[k].astype(F32) + part.astype(F32)).astype(BF)


def second_sum_kernel(own_ref, y_ref, x_ref, xy_ref, *refs):
    tables, outs = refs[:-2], refs[-2:]
    channels = own_ref.shape[1]
    total = own_ref[...].astype(F32) + y_ref[...].astype(F32)
    total = (total + x_ref[...].astype(F32) + xy_ref[...].astype(F32)).astype(BF)
    split = outs[0].shape[1]
    for k in range(outs[0].shape[0]):
        outs[0][k] = total[:split]
        outs[1][k, : total.shape[0] - split] = total[split:]
        for table in tables:
            for band in range(table.shape[1] // channels):
                at = total.shape[0] - split + 16 * band
                outs[1][k, at : at + 16] = table[:, band * channels : (band + 1) * channels]


def sum_kernel(*refs):
    total = refs[0][...].astype(F32)
    for ref in refs[1:-1]:
        total = total + ref[...].astype(F32)
    refs[-1][...] = total.astype(BF)


def stack_kernel(split, group_index, *refs):
    entries, outs = refs[:-2], refs[-2:]
    count = len(entries)
    mine = lax.axis_index("lat") // WROWS
    samples = lax.axis_size("lat") // WROWS
    for k in range(count):
        slot = (mine + samples - k) % samples if samples == count else k
        outs[0][slot] = entries[k][:split]
        outs[1][slot] = entries[k][split:]


def double_kernel(count, *refs):
    outs = refs[2 * count :]
    at = 0
    for k in range(count):
        rows = refs[2 * k].shape[1]
        for j in range(2):
            value = refs[2 * k + j][...]
            outs[k][j] = value
            if len(outs) > count:
                outs[count][j, :, at : at + rows] = value
        at += rows


def finish_kernel(layout, slots, small, start_at, before, group_index, *refs):
    count_parts = len(layout)
    arrays = len(set(place[0] for places in slots for place in places))
    sources = [
        [refs[number].at[at, :, cut[0] : cut[1]] for number, at, cut in places] for places in slots
    ]
    steps = len(slots[0])
    outs = refs[arrays + before : -count_parts - 1]
    buffers = refs[-count_parts - 1 : -1]
    semaphores = refs[-1]
    rel = pl.program_id(0)
    sets = outs[0].shape[0]
    size, channels = buffers[0].shape[3] // 8, buffers[0].shape[3]
    count = buffers[0].shape[1]
    owners, first = entry_sets(group_index, count, sets)

    def copy(p, r, slot):
        return pltpu.make_async_copy(sources[p][r], buffers[p].at[slot], semaphores.at[p, slot])

    @pl.when(rel == 0)
    def _():
        for r in range(steps):
            for p in range(count_parts):
                copy(p, r, r).start()

    slot = rel
    for p in range(count_parts):
        copy(p, 0, slot).wait()

    def spread(read, write):
        for k in range(count):

            @pl.when(first[k])
            def _(k=k):
                write(owners[k], False, read(k))

            @pl.when(jnp.logical_not(first[k]))
            def _(k=k):
                write(owners[k], True, read(k))

        if not isinstance(owners[0], int):
            for g in range(sets):
                there = owners[0] == g
                for owner in owners[1:]:
                    there = there | (owner == g)

                @pl.when(jnp.logical_not(there))
                def _(g=g):
                    write(g, False, [jnp.zeros_like(value) for value in read(0)])

    places = []
    wide_at, tall_at = 0, 0
    for p, (wide, tall) in enumerate(layout):
        for block in range(wide + tall):
            rows = slice(block * size, (block + 1) * size)
            if block < wide:
                cols = slice(wide_at * channels, (wide_at + 1) * channels)
                wide_at += 1
                places.append((p, rows, lambda g, cols=cols: (outs[0], (g, slice(None), cols))))
            else:
                at = tall_at
                tall_at += 1
                target = outs[1] if wide_at else outs[0]
                places.append((p, rows, lambda g, at=at, target=target: (target, (g, at, 0))))

    def read(k):
        return [buffers[p][slot, k, rows, :].astype(F32) for p, rows, _ in places]

    def write(g, add, values):
        for (_, _, where), value in zip(places, values):
            ref, index = where(g)
            ref[index] = ref[index] + value if add else value

    spread(read, write)
    q = (rel + start_at) ^ my_slot()
    start = buffers[-1].shape[2] - 16
    for number, (out, column) in enumerate(small):

        @pl.when(q == number)
        def _(out=out, column=column):
            cols = slice(column, column + channels)

            def read(k):
                return [buffers[-1][slot, k, start : start + 16, :].astype(F32)[0:1]]

            def write(g, add, values):
                index = (pl.ds(g, 1), cols)
                outs[out][index] = outs[out][index] + values[0] if add else values[0]

            spread(read, write)


def finish_positions_kernel(places, small, group_index, window_types, *refs):
    arrays = 1 + max(place[0] for place in places)
    pieces = [refs[number].at[at] for number, at, _ in places]
    outs, held, rows = refs[arrays:-2], refs[-2], refs[-1]
    out = outs[0]
    count, _, channels = pieces[0].shape
    sets, (heads, _, positions) = outs[1].shape[0], out.shape[1:]
    step = pl.program_id(0)
    owners, first = entry_sets(group_index, count, sets)
    me = my_slot()

    @pl.when(step == 0)
    def _():
        for k in range(count):
            for r in range(8):
                at = (k * 8 + r) * 16
                for band in range(held.shape[1] // channels):
                    held[at : at + 16, band * channels : (band + 1) * channels] = pieces[r][
                        k, 16 * band + 16 : 16 * band + 32
                    ]
                rows[r, k : k + 1, :] = pieces[r][k, 0:16].astype(F32)[0:1]
        for ref in outs[1:]:
            ref[...] = jnp.zeros_like(ref)
        for q, (number, column) in enumerate(small):
            values = rows[q ^ me]
            for k in range(count):
                index = (pl.ds(owners[k], 1), slice(column, column + channels))
                outs[number][index] = outs[number][index] + values[k : k + 1]

    shape = (heads * 8, count * 128)
    row = lax.broadcasted_iota(jnp.int32, shape, 0)
    col = lax.broadcasted_iota(jnp.int32, shape, 1)
    kind_of = jnp.zeros(shape, jnp.int32)
    for r in range(8):
        q = r ^ me
        kind = window_types[(q // 2 % 2) * 4 + (q // 4) * 2 + q % 2]
        kind_of = jnp.where(col // 16 % 8 == r, kind, kind_of)
    set_of = jnp.zeros(shape, jnp.int32)
    for k in range(count):
        set_of = jnp.where(col // 128 == k, owners[k], set_of)
    hit = (row // 8 == col % 16) & (row % 8 == kind_of) & (set_of == step)
    value = dot(jnp.where(hit, 1.0, 0.0).astype(BF), held[...])
    out[0] = value[:, :positions].reshape(out.shape[1:])


def whole(array_or_shape):
    shape = getattr(array_or_shape, "shape", array_or_shape)
    return pl.BlockSpec(shape, lambda i, *_: (0,) * len(shape))


def own_member(array):
    def index(i, group_index, *_):
        return (my_set(group_index),) + (0,) * (array.ndim - 1)

    return pl.BlockSpec((None,) + array.shape[1:], index)


def call(
    kernel, scalars, inputs, out_shapes, *, in_specs=None, out_specs=None, scratch=(), grid=(1,),
    after=(), cost=1.0, aliases=None,
):
    in_specs = [whole(v) for v in inputs] if in_specs is None else in_specs
    out_specs = jax.tree.map(whole, out_shapes) if out_specs is None else out_specs
    count = len(scalars) + len(inputs)
    body = kernel
    if after:

        def body(*refs):
            kernel(*refs[:count], *refs[count + len(after) :])

    after = list(after)

    return pl.pallas_call(
        body,
        grid_spec=pltpu.PrefetchScalarGridSpec(
            num_scalar_prefetch=len(scalars),
            grid=grid,
            in_specs=list(in_specs) + [pl.BlockSpec(memory_space=pl.ANY)] * len(after),
            out_specs=out_specs,
            scratch_shapes=list(scratch),
        ),
        out_shape=out_shapes,
        input_output_aliases=aliases or {},
        compiler_params=pltpu.CompilerParams(vmem_limit_bytes=60 * 1024 * 1024),
        cost_estimate=pl.CostEstimate(
            flops=int(cost * 1.1e9), bytes_accessed=10**3, transcendentals=0
        ),
    )(*scalars, *inputs, *after)


def like(shape, kind=BF):
    return jax.ShapeDtypeStruct(tuple(shape), kind)


def swap(value, axis, distance):
    pairs = [(i, i ^ distance) for i in range(lax.axis_size(axis))]
    return lax.ppermute(value, axis, pairs)


def move_both(value, step, cross):
    lev, lat = lax.axis_size("lev"), lax.axis_size("lat")
    pairs = [
        (a * lat + b, step(a, lev) * lat + (b ^ cross)) for a in range(lev) for b in range(lat)
    ]
    return lax.ppermute(value, ("lev", "lat"), pairs)


def below(a, size):
    return (a - 1) % size


def above(a, size):
    return (a + 1) % size


def over_x(a, size):
    return a ^ 2


def quadrants(*blocks):
    half = WH // 2
    rows = half * blocks[0].shape[2]

    def flat(part):
        return jnp.stack([part(block).reshape(rows, block.shape[3]) for block in blocks])

    return [
        flat(lambda block: block[half:, 1]),
        move_both(flat(lambda block: block[half:, 0]), below, 0),
        swap(flat(lambda block: block[:half, 1]), "lat", 1),
        move_both(flat(lambda block: block[:half, 0]), below, 1),
    ]


def reduce_cores(keep, sends, after=()):
    arrived = [swap(send, "lev", 1) for send in sends]
    shape = like(keep.shape[1:])
    return call(first_sum_kernel, [], [keep] + arrived, [shape] * 4, after=after, cost=0.1)


def move_chips(parts):
    own, along_y, along_x, along_both = parts
    return [own, swap(along_y, "lat", 1), swap(along_x, "lev", 2), move_both(along_both, over_x, 1)]


def reduce_chips(parts, split, tables=(), sets=4, after=()):
    rows, channels = parts[0].shape
    samples = lax.axis_size("lat") // WROWS
    copies = samples if samples <= sets else 1
    below = rows - split + sum(16 * (table.shape[1] // channels) for table in tables)
    shapes = [like((copies, split, channels)), like((copies, below, channels))]
    return call(second_sum_kernel, [], parts + list(tables), shapes, after=after, cost=0.1)


def across_samples(copies, group_index, sets):
    samples = lax.axis_size("lat") // WROWS
    groups = [[s * WROWS + b for s in range(samples)] for b in range(WROWS)]
    if samples <= sets:
        return lax.all_to_all(copies, "lat", 0, 0, axis_index_groups=groups)
    hot = (jnp.arange(sets) == group_index[lax.axis_index("lat") // WROWS]).astype(F32)
    total = lax.psum(hot[:, None, None] * copies.astype(F32), "lat", axis_index_groups=groups)
    return total.astype(BF)


def round_samples(share, group_index, sets):
    lat = lax.axis_size("lat")
    samples = lat // WROWS
    if samples > sets:
        total = across_samples(share[None], group_index, sets)
        return [total[k] for k in range(sets)]
    entries = [share]
    for k in range(1, samples):
        pairs = [(i, (i + WROWS * k) % lat) for i in range(lat)]
        entries.append(lax.ppermute(share, "lat", pairs))
    return entries


def doubled(pairs, merged=False, after=()):
    inputs = [value for pair in pairs for value in pair]
    shapes = [like((2,) + pair[0].shape) for pair in pairs]
    if merged:
        count, _, channels = pairs[0][0].shape
        rows = sum(pair[0].shape[1] for pair in pairs)
        shapes.append(like((2, count, rows, channels)))
    kernel = functools.partial(double_kernel, len(pairs))
    return call(kernel, [], inputs, shapes, after=after, cost=0.1)


def by_slot(value, moved, other, other_rows, x_first):
    moved_other = swap(moved, "lev", 1)
    rows = (0, value.shape[2])
    places = []
    for near, cut, far in ((value, rows, moved), (other, other_rows, moved_other)):
        if x_first:
            places += [(near, 0, cut), (far, 0, rows), (near, 1, cut), (far, 1, rows)]
        else:
            places += [(near, 0, cut), (near, 1, cut), (far, 0, rows), (far, 1, rows)]
    return places


def numbered(parts):
    arrays, slots = [], []
    for part in parts:
        places = []
        for array, at, cut in part:
            found = [n for n, known in enumerate(arrays) if known is array]
            if not found:
                arrays.append(array)
            places.append((found[0] if found else len(arrays) - 1, at, cut))
        slots.append(places)
    return arrays, slots


def finish(parts, layout, shapes, small, group_index, cost, start_at=0, into=(), after=()):
    sets, (count, _, channels) = shapes[0][0], parts[0][0][0].shape[1:]
    size = channels // 8
    specs = []
    for shape in shapes:
        if len(shape) == 5:
            block = (sets, shape[1], 1, size, channels)
            specs.append(pl.BlockSpec(block, lambda r, g: (0, 0, (r + start_at) ^ my_slot(), 0, 0)))
        elif len(shape) == 3:
            block = (sets, size, shape[2])
            specs.append(pl.BlockSpec(block, lambda r, g: (0, (r + start_at) ^ my_slot(), 0)))
        else:
            specs.append(whole(shape))
    inputs, slots = numbered(parts)
    scratch = [
        pltpu.VMEM((len(part), count, part[0][2][1] - part[0][2][0], channels), BF)
        for part in parts
    ]
    outs = call(
        functools.partial(finish_kernel, layout, slots, small, start_at, len(into)),
        [group_index],
        inputs + list(into),
        [like(shape, F32) for shape in shapes],
        in_specs=[pl.BlockSpec(memory_space=pl.ANY)] * (len(inputs) + len(into)),
        out_specs=specs,
        scratch=scratch + [pltpu.SemaphoreType.DMA((len(parts), len(slots[0])))],
        grid=(len(slots[0]),),
        after=after,
        cost=cost,
        aliases={1 + len(inputs) + k: k for k in range(len(into))},
    )
    return list(outs)


def body(
    fields,
    group_index,
    window_types,
    window_masks,
    first_gain,
    first_offset,
    input_weight,
    input_bias,
    output_weight,
    output_bias,
    second_gain,
    second_offset,
    expand_weight,
    expand_bias,
    reduce_weight,
    reduce_bias,
    position_bias,
    cotangent,
):
    columns = fields.shape[2]
    channels = fields.shape[3]
    sets, kinds, heads, positions = position_bias.shape
    groups = heads // GROUP
    cells = WZ * WH
    tokens = columns * cells
    rows = tokens // 4
    share = channels // 8
    lanes = channels // groups
    to_win = jnp.asarray(window_order(columns), BF)
    to_rows = jnp.asarray(window_order(columns).T, BF)
    own_lanes = jnp.asarray(head_lanes(lanes), BF)
    cols_map = jnp.asarray(column_maps(), BF)
    rows_map = jnp.asarray(token_rows(), BF)
    rows_back = jnp.asarray(token_rows().T, BF)
    places = jnp.asarray(head_places(), BF)
    fold = jnp.asarray(fold_map(), BF)

    arrived = quadrants(fields, cotangent)

    by_head = position_bias.transpose(0, 2, 1, 3)
    table = call(
        select_kernel,
        [group_index, window_types],
        [by_head],
        like((heads, positions)),
        in_specs=[own_member(by_head)],
        cost=1.0,
    )
    table = table.reshape(heads, WZ, WZ, WH, WH, SPAN).transpose(0, 2, 4, 1, 3, 5)
    table = table.reshape(heads, cells, cells * SPAN)
    table = jnp.pad(table, ((0, 0), (0, 16 - cells), (0, 0))).reshape(heads * 16, cells * SPAN)
    bias_map = call(
        bias_kernel,
        [],
        [window_masks, table, cols_map, rows_map, places, fold],
        like((groups, TOKENS, PADDED), F32),
        scratch=[pltpu.VMEM((heads, 16 * WW, TOKENS), BF)],
        cost=5.0,
    )

    hidden_units = expand_weight.shape[2]
    assert hidden_units == 4 * channels
    up_rows = 8 * share + 16
    low_rows = 4 * share + 16
    inputs = (
        arrived
        + [to_win, to_rows, bias_map, own_lanes, first_gain, first_offset]
        + [input_weight, input_bias, output_weight, output_bias, second_gain, second_offset]
        + [expand_weight, expand_bias, reduce_weight, reduce_bias]
    )
    weights = {id(v) for v in (input_weight, output_weight, expand_weight, reduce_weight)}
    quadrant = like((rows, channels))
    y0, y1, y2, y3, xw, triple, att, grad_hidden, keep, send = call(
        forward_kernel,
        [group_index],
        inputs,
        [quadrant] * 4
        + [
            like((tokens, channels)),
            like((tokens, 3 * channels)),
            like((tokens, channels)),
            like((tokens, channels), F32),
            like((4, up_rows, channels)),
            like((4, up_rows, channels)),
        ],
        in_specs=[own_member(v) if id(v) in weights else whole(v) for v in inputs],
        scratch=[
            pltpu.VMEM((tokens, channels), BF),
            pltpu.VMEM((channels, tokens), BF),
            pltpu.VMEM((tokens, channels), BF),
            pltpu.VMEM((tokens, channels), F32),
            pltpu.VMEM((tokens, channels), F32),
            pltpu.VMEM((8, channels), F32),
        ],
        cost=33.0,
    )

    up_parts = reduce_cores(keep, [send])
    inputs = [triple, grad_hidden, bias_map, own_lanes, output_weight]
    grad_triple, score_sums = call(
        scores_back_kernel,
        [group_index],
        inputs,
        [like((tokens, 3 * channels)), like((groups, TOKENS, PADDED), F32)],
        in_specs=[own_member(v) if id(v) in weights else whole(v) for v in inputs],
        scratch=[pltpu.VMEM((tokens, channels), BF)],
        after=[up_parts[3]],
        cost=20.0,
    )
    up_share = call(
        sum_kernel,
        [],
        move_chips(up_parts),
        like(up_parts[0].shape),
        after=[grad_triple],
        cost=0.1,
    )

    up_entries = round_samples(up_share, group_index, sets)
    inputs = [xw, att, grad_hidden, grad_triple, to_rows, first_gain, first_offset, input_weight]
    d0, d1, d2, d3, low_grads, low_small = call(
        input_back_kernel,
        [group_index],
        inputs,
        [quadrant] * 4 + [like((4, channels, channels)), like((8, channels), F32)],
        in_specs=[own_member(v) if id(v) in weights else whole(v) for v in inputs],
        after=[up_share],
        cost=8.0,
    )
    low_keep, *rest = call(
        spread_kernel,
        [],
        [low_grads, low_small, y1, y2, y3, d1, d2, d3],
        [like((4, low_rows, channels))]
        + [like((1, low_rows, channels))] * 4
        + [like((2, rows, channels))] * 3,
        cost=0.1,
    )
    low_send, (s1, s2, s3) = rest[:4], rest[4:]
    count = len(up_entries)
    up_stack, down_stack = call(
        functools.partial(stack_kernel, 4 * share),
        [group_index],
        up_entries,
        [like((count, 4 * share, channels)), like((count, up_rows - 4 * share, channels))],
        after=[low_keep],
        cost=0.1,
    )
    low_parts = reduce_cores(low_keep, low_send, after=[up_stack])

    up_x = swap(up_stack, "lev", 2)
    down_y = swap(down_stack, "lat", 1)
    low_sums = move_chips(low_parts)
    table_grad = call(
        fold_kernel,
        [],
        [score_sums, cols_map, rows_back, places],
        like((heads * 16, cells * SPAN)),
        scratch=[pltpu.VMEM((2, WW, heads * 16, TOKENS), BF)],
        after=[up_stack],
        cost=7.0,
    )
    table_grad = table_grad.reshape(heads, 16, cells * SPAN)[:, :cells]
    table_grad = table_grad.reshape(heads, WZ, WH, WZ, WH, SPAN).transpose(0, 3, 1, 4, 2, 5)
    wide = -(-positions // channels) * channels
    table_grad = jnp.pad(
        table_grad.reshape(heads, positions), ((0, 16 - heads), (0, wide - positions))
    )
    low_copies, table_copies = reduce_chips(
        low_sums, 4 * share, [table_grad], sets=sets, after=[up_x, down_y]
    )
    up_pair, down_pair, both_pair = doubled(
        [(up_stack, up_x), (down_stack, down_y)], True, after=[low_copies]
    )
    both_other = swap(both_pair, "lev", 1)

    up_moved = swap(up_pair, "lat", 1)
    down_moved = swap(down_pair, "lev", 2)
    low_stack = across_samples(low_copies, group_index, sets)
    table_stack = across_samples(table_copies, group_index, sets)
    up_pieces = by_slot(up_pair, up_moved, both_other, (0, 4 * share), True)
    down_pieces = by_slot(down_pair, down_moved, both_other, (4 * share, up_rows), False)

    low_x = swap(low_stack, "lev", 2)
    table_y = swap(table_stack, "lat", 1)
    low_pair, table_pair = doubled([(low_stack, low_x), (table_stack, table_y)])
    low_moved = swap(low_pair, "lat", 1)
    table_moved = swap(table_pair, "lev", 2)
    low_pieces = by_slot(low_pair, low_moved, swap(low_pair, "lev", 1), (0, low_pair.shape[2]), True)
    table_pieces = by_slot(
        table_pair, table_moved, swap(table_pair, "lev", 1), (0, table_pair.shape[2]), False
    )

    up_grad, down_grad, bup_grad, bdn_grad, g2_grad, o2_grad = finish(
        [up_pieces, down_pieces],
        [(4, 0), (0, 4)],
        [(sets, channels, hidden_units), (sets, 4, 8, share, channels), (sets, hidden_units)]
        + [(sets, channels)] * 3,
        [(2, k * channels) for k in range(4)] + [(3, 0), (4, 0), (5, 0)],
        group_index,
        13.0,
    )
    shapes = [(sets, channels, 3 * channels), (sets, 1, 8, share, channels)]
    near = finish(
        [low_pieces[:4]], [(3, 1)], shapes, [], group_index, 14.0, after=[up_grad]
    )
    in_grad, out_grad = finish(
        [low_pieces[4:]], [(3, 1)], shapes, [], group_index, 3.0, start_at=4, into=near
    )
    widths = (channels, 2 * channels, channels, channels)
    arrays, (slots,) = numbered([table_pieces])
    position_grad, bout_grad, bin_grad, g1_grad, o1_grad = call(
        functools.partial(
            finish_positions_kernel, slots, [(1, 0), (2, 0), (2, channels), (3, 0), (4, 0)]
        ),
        [group_index, window_types],
        arrays,
        [like((sets, heads, kinds, positions), F32)] + [like((sets, w), F32) for w in widths],
        out_specs=[pl.BlockSpec((1, heads, kinds, positions), lambda g, *_: (g, 0, 0, 0))]
        + [whole((sets, w)) for w in widths],
        scratch=[
            pltpu.VMEM((table_pieces[0][0].shape[1] * 128, wide), BF),
            pltpu.VMEM((8, 8, channels), F32),
        ],
        grid=(sets,),
        after=[in_grad],
        cost=5.0,
    )

    back = [move_both(s1, above, 0), swap(s2, "lat", 1), move_both(s3, above, 1)]
    output, input_grad = call(
        assemble_kernel,
        [],
        [y0, d0] + back,
        [like(fields.shape)] * 2,
        after=[position_grad],
        cost=1.0,
    )
    out_grad = out_grad.reshape(sets, -1, channels)
    down_grad = down_grad.reshape(sets, -1, channels)
    position_grad = position_grad.transpose(0, 2, 1, 3)
    return (
        output,
        input_grad,
        g1_grad,
        o1_grad,
        in_grad,
        bin_grad,
        out_grad,
        bout_grad,
        g2_grad,
        o2_grad,
        up_grad,
        bup_grad,
        down_grad,
        bdn_grad,
        position_grad,
    )


def solution(mesh):
    slab = P("lat", "lev", None, None)
    return jax.shard_map(
        body,
        mesh=mesh,
        in_specs=(slab,) + (P(),) * 16 + (slab,),
        out_specs=(slab, slab) + (P(),) * 13,
        check_vma=False,
    )
```

```python
import functools

import jax
import jax.numpy as jnp
import numpy as np
from jax import lax
from jax.experimental import pallas as pl
from jax.experimental.pallas import tpu as pltpu
from jax.sharding import PartitionSpec as P

WZ = 2
WH = 6
WW = 12
WROWS = 2
TOKENS = WZ * WH * WW
GROUP = 4
PADDED = 640
SPAN = 2 * WW - 1
MASKED = -1e30
LOG2E = 1.4426950408889634
BF = jnp.bfloat16
F32 = jnp.float32


def dot(a, b):
    return lax.dot_general(a, b, (((1,), (0,)), ((), ())), preferred_element_type=F32)


def dot_nt(a, b):
    return lax.dot_general(a, b, (((1,), (1,)), ((), ())), preferred_element_type=F32)


def dot_tn(a, b):
    return lax.dot_general(a, b, (((0,), (0,)), ((), ())), preferred_element_type=F32)


def one_hot(index, size):
    return (np.asarray(index)[:, None] == np.arange(size)[None, :]).astype(np.float32)


def window_order(columns):
    windows = columns // WW
    n, h, w = np.meshgrid(np.arange(windows), np.arange(WH), np.arange(WW), indexing="ij")
    source = h * columns + (n * WW + w + WW // 2) % columns
    return one_hot(source.reshape(-1), WH * columns)


def column_maps():
    cells = WZ * WH
    out = np.zeros((WW, cells, SPAN, cells, WW), np.float32)
    for wj in range(WW):
        for wi in range(WW):
            for c in range(cells):
                out[wj, c, wi - wj + WW - 1, c, wi] = 1.0
    return out.reshape(WW, cells * SPAN, cells * WW)


def token_rows():
    j = np.arange(TOKENS)
    return one_hot((j % WW) * 16 + j // WW, WW * 16)


def head_places():
    return np.stack([one_hot(h * TOKENS + np.arange(TOKENS), PADDED) for h in range(GROUP)])


def fold_map():
    return sum(head_places())


def head_lanes(lanes):
    return np.repeat(np.eye(GROUP, dtype=np.float32), lanes // GROUP, axis=1)


def select_kernel(group_index, window_types, tables_ref, out_ref):
    heads, kinds, positions = tables_ref.shape
    place = lax.axis_index("lev") * WROWS + lax.axis_index("lat") % WROWS
    kind = window_types[place]
    shape = (heads, heads * kinds)
    row = lax.broadcasted_iota(jnp.int32, shape, 0)
    col = lax.broadcasted_iota(jnp.int32, shape, 1)
    pick = jnp.where(col == row * kinds + kind, 1.0, 0.0).astype(BF)
    tables = tables_ref[...].astype(F32).reshape(heads * kinds, positions).astype(BF)
    out_ref[...] = dot(pick, tables).astype(BF)


def bias_kernel(masks_ref, table_ref, cols_ref, rows_ref, places_ref, fold_ref, out_ref, held):
    heads = held.shape[0]
    for wj in range(WW):
        part = dot(table_ref[...], cols_ref[wj]).astype(BF)
        for h in range(heads):
            held[h, 16 * wj : 16 * wj + 16, :] = part[16 * h : 16 * h + 16]
    half = lax.axis_index("lat") % WROWS
    labels = masks_ref[lax.axis_index("lev"), pl.ds(half, 1), :].astype(F32)
    top = lax.broadcasted_iota(jnp.int32, (8, TOKENS), 0) == 0
    labels = jnp.where(top, jnp.broadcast_to(labels, (8, TOKENS)), 0.0)
    across = dot(jnp.ones((TOKENS, 8), BF), dot(labels.astype(BF), fold_ref[...]).astype(BF))
    down = dot_tn(labels.astype(BF), jnp.ones((8, PADDED), BF))
    same = jnp.abs(across - down) < 0.5
    for g in range(heads // GROUP):
        total = dot(held[g * GROUP], places_ref[0])
        for h in range(1, GROUP):
            total = total + dot(held[g * GROUP + h], places_ref[h])
        out_ref[g] = jnp.where(same, dot(rows_ref[...], total.astype(BF)), MASKED) * LOG2E


def fold_kernel(sums_ref, cols_ref, rows_ref, places_ref, out_ref, held):
    groups = sums_ref.shape[0]
    for g in range(groups):
        value = sums_ref[g]
        high = value.astype(BF)
        low = (value - high.astype(F32)).astype(BF)
        for index, part in enumerate((high, low)):
            ordered = dot(rows_ref[...], part).astype(BF)
            for h in range(GROUP):
                block = dot_nt(ordered, places_ref[h]).astype(BF)
                spot = (g * GROUP + h) * 16
                for wj in range(WW):
                    held[index, wj, spot : spot + 16, :] = block[16 * wj : 16 * wj + 16]
    total = jnp.zeros(out_ref.shape, F32)
    for wj in range(WW):
        for index in range(2):
            total = total + dot_nt(held[index, wj], cols_ref[wj])
    out_ref[...] = total.astype(BF)


def norm_parts(values):
    centre = values - jnp.mean(values, axis=-1, keepdims=True)
    spread = jnp.mean(centre * centre, axis=-1, keepdims=True)
    root = lax.rsqrt(spread + 1e-05)
    return centre * root, root


def norm_back(grad, gain, xhat, root):
    u = grad * gain
    return (
        u - jnp.mean(u, axis=-1, keepdims=True) - xhat * jnp.mean(u * xhat, axis=-1, keepdims=True)
    ) * root


def stacked_heads(block, lanes_ref):
    pieces = [block * lanes_ref[h : h + 1, :] for h in range(GROUP)]
    pieces.append(jnp.zeros((PADDED - GROUP * block.shape[0], block.shape[1]), block.dtype))
    return jnp.concatenate(pieces, axis=0)


def own_head(full):
    size = full.shape[0] // GROUP
    return jnp.concatenate(
        [
            full[h * size : (h + 1) * size, h * TOKENS : (h + 1) * TOKENS]
            for h in range(GROUP)
        ],
        axis=0,
    )


def softmax_t(keys, queries, bias, scale):
    scores = dot_nt(keys, queries) * (scale * LOG2E) + bias
    exponent = jnp.exp2(scores - jnp.max(scores, axis=0, keepdims=True))
    return exponent * (1.0 / jnp.sum(exponent, axis=0, keepdims=True))


def to_windows(level_map, levels):
    half = WH * WW
    parts = [dot(level_map, level) for level in levels]
    pieces = []
    for n in range(parts[0].shape[0] // half):
        for part in parts:
            pieces.append(part[n * half : (n + 1) * half])
    return jnp.concatenate(pieces, axis=0)


def to_levels(level_map, value):
    half = WH * WW
    count = value.shape[0] // (2 * half)
    quadrants = [None] * 4
    for z in range(WZ):
        level = [value[(2 * n + z) * half : (2 * n + z + 1) * half] for n in range(count)]
        level = dot(level_map, jnp.concatenate(level, axis=0).astype(BF))
        rows = level.shape[0] // 2
        for side in range(2):
            quadrants[side * WZ + z] = level[side * rows : (side + 1) * rows].astype(BF)
    return quadrants


def my_place():
    return (lax.axis_index("lev") // 2) * 2 + lax.axis_index("lat") % WROWS


def my_core():
    return lax.axis_index("lev") % 2


def place_slot(keep_out, send_outs, owner, rel, start, value):
    @pl.when(my_core() == owner)
    def _():
        keep_out[rel, start : start + value.shape[0]] = value

    @pl.when(my_core() != owner)
    def _():
        at = start
        for out in send_outs:
            if 0 <= at < out.shape[1]:
                out[rel, at : at + value.shape[0]] = value
            at -= out.shape[1]


def scatter_rows(keep_out, send_outs, owner, block, value):
    value = value.astype(BF)
    size = value.shape[0] // 4
    for q in range(4):
        piece = value[q * size : (q + 1) * size]
        place_slot(keep_out, send_outs, owner, q ^ my_place(), block * size, piece)


def scatter_small(keep_out, send_outs, small):
    start = keep_out.shape[1] - 16
    for n in range(8):
        row = jnp.broadcast_to(small[n : n + 1, :], (16, small.shape[1])).astype(BF)
        place_slot(keep_out, send_outs, n // 4, (n % 4) ^ my_place(), start, row)


def my_set(group_index):
    return group_index[lax.axis_index("lat") // WROWS]


def entry_sets(group_index, count, sets):
    samples = lax.axis_size("lat") // WROWS
    if samples > sets:
        return list(range(sets)), [True] * sets
    owners = [group_index[k] for k in range(count)]
    first = []
    for k in range(count):
        fresh = jnp.bool_(True)
        for j in range(k):
            fresh = fresh & (owners[j] != owners[k])
        first.append(fresh)
    return owners, first


def param_row(ref, group):
    return ref[pl.ds(group, 1), :]


def forward_kernel(
    group_index, f0, f1, f2, f3, to_win, to_rows, bias_ref, lanes_ref,
    g1_ref, o1_ref, win_ref, bin_ref, wout_ref, bout_ref, g2_ref, o2_ref,
    wups_ref, bup_ref, wdns_ref, bdn_ref,
    y0, y1, y2, y3, xw_any, triple_any, att_any, gh_out, keep_out, send_out,
    n2_s, n2t_s, cot_s, acc_s, back_s, small_out,
    wup_ref, wdn_ref, xw_out, triple_out, att_out, semaphores,
):
    gid = my_set(group_index)
    tokens, channels = xw_out.shape
    weights = [
        pltpu.make_async_copy(source.at[gid], target, semaphores.at[k])
        for k, (source, target) in enumerate(((wups_ref, wup_ref), (wdns_ref, wdn_ref)))
    ]
    for copy in weights:
        copy.start()
    results = [
        pltpu.make_async_copy(source, target, semaphores.at[2 + k])
        for k, (source, target) in enumerate(
            ((xw_out, xw_any), (triple_out, triple_any), (att_out, att_any))
        )
    ]
    lanes = lanes_ref.shape[1]
    scale = (lanes // GROUP) ** -0.5

    def gathered(which):
        levels = [
            jnp.concatenate([low[which].astype(F32), high[which].astype(F32)], axis=0).astype(BF)
            for low, high in ((f0, f2), (f1, f3))
        ]
        return to_windows(to_win[...], levels)

    x = gathered(0)
    xw_out[...] = x.astype(BF)
    cot_s[...] = gathered(1).astype(BF)
    xhat, _ = norm_parts(x)
    normed = (xhat * param_row(g1_ref, gid) + param_row(o1_ref, gid)).astype(BF)
    bias_row = param_row(bin_ref, gid)
    bias_row = jnp.concatenate(
        [bias_row[:, :channels], jnp.zeros((1, channels), F32), bias_row[:, channels:]], axis=1
    )
    triple_out[...] = (dot(normed, win_ref[...]) + bias_row).astype(BF)
    results[0].start()
    results[1].start()

    def window(n, carry):
        rows = pl.ds(pl.multiple_of(n * TOKENS, 16), TOKENS)
        for g in range(channels // lanes):
            lo = g * lanes
            queries = stacked_heads(triple_out[rows, lo : lo + lanes], lanes_ref)
            keys = triple_out[rows, channels + lo : channels + lo + lanes]
            values = triple_out[rows, 2 * channels + lo : 2 * channels + lo + lanes]
            probs = softmax_t(keys, queries, bias_ref[g], scale).astype(BF)
            full = dot_tn(values, probs)
            att_out[rows, lo : lo + lanes] = own_head(full).T.astype(BF)
        return carry

    lax.fori_loop(0, tokens // TOKENS, window, 0, unroll=2)

    results[2].start()
    mixed = (dot(att_out[...], wout_ref[...]) + param_row(bout_ref, gid)).astype(BF)
    hidden = xw_out[...].astype(F32) + mixed.astype(F32)
    xhat2, root2 = norm_parts(hidden)
    gain2 = param_row(g2_ref, gid)
    n2 = (xhat2 * gain2 + param_row(o2_ref, gid)).astype(BF)
    n2_s[...] = n2
    n2t_s[...] = n2.T
    acc_s[...] = hidden + param_row(bdn_ref, gid)
    per = 4
    step = per * channels

    bup = param_row(bup_ref, gid)
    for copy in weights:
        copy.wait()
    for k in range(wup_ref.shape[1] // step):
        cols = slice(k * step, (k + 1) * step)
        up = wup_ref[:, cols]
        down = wdn_ref[cols, :]
        expanded = dot(n2_s[...], up) + bup[:, cols]
        cdf = 0.5 * (1.0 + lax.erf(expanded * (0.5**0.5)))
        active = (expanded * cdf).astype(BF)
        slope = cdf + expanded * (jnp.exp(-0.5 * expanded * expanded) * 0.3989422804014327)
        grad_expanded = (dot_nt(cot_s[...], down) * slope).astype(BF)
        acc_s[...] += dot(active, down)
        back = dot_nt(grad_expanded, up)
        back_s[...] = back if k == 0 else back_s[...] + back
        grad_up = dot(n2t_s[...], grad_expanded)
        grad_down = dot_tn(active, cot_s[...])
        sums = jnp.sum(grad_expanded.astype(F32), axis=0, keepdims=True)
        for j in range(per):
            part = slice(j * channels, (j + 1) * channels)
            scatter_rows(keep_out, [send_out], 0, per * k + j, grad_up[:, part])
            scatter_rows(keep_out, [send_out], 1, per * k + j, grad_down[part])
            small_out[per * k + j : per * k + j + 1, :] = sums[:, part]

    for ref, value in zip((y0, y1, y2, y3), to_levels(to_rows[...], acc_s[...])):
        ref[...] = value
    cot = cot_s[...].astype(F32)
    grad = back_s[...]
    small_out[4:5, :] = jnp.sum(cot, axis=0, keepdims=True)
    small_out[5:6, :] = jnp.sum(grad * xhat2, axis=0, keepdims=True)
    small_out[6:7, :] = jnp.sum(grad, axis=0, keepdims=True)
    small_out[7:8, :] = jnp.zeros((1, channels), F32)
    scatter_small(keep_out, [send_out], small_out[...])
    gh_out[...] = cot + norm_back(grad, gain2, xhat2, root2)
    for copy in results:
        copy.wait()


def scores_back_kernel(
    group_index, triple_ref, gh_ref, bias_ref, lanes_ref, wout_ref,
    gt_out, sums_out, ga_s,
):
    channels = gh_ref.shape[1]
    tokens = gh_ref.shape[0]
    lanes = lanes_ref.shape[1]
    scale = (lanes // GROUP) ** -0.5
    ga_s[...] = dot_nt(gh_ref[...].astype(BF), wout_ref[...]).astype(BF)
    sums_out[...] = jnp.zeros_like(sums_out)

    def window(n, carry):
        rows = pl.ds(pl.multiple_of(n * TOKENS, 16), TOKENS)
        for g in range(channels // lanes):
            lo = g * lanes
            queries = stacked_heads(triple_ref[rows, lo : lo + lanes], lanes_ref)
            keys = triple_ref[rows, channels + lo : channels + lo + lanes]
            values = triple_ref[rows, 2 * channels + lo : 2 * channels + lo + lanes]
            probs = softmax_t(keys, queries, bias_ref[g], scale)
            grad_att = stacked_heads(ga_s[rows, lo : lo + lanes], lanes_ref)
            grad_probs = dot_nt(values, grad_att)
            row_dot = jnp.sum(probs * grad_probs, axis=0, keepdims=True)
            grad_scores = (probs * (grad_probs - row_dot)).astype(BF)
            sums_out[g] += grad_scores.astype(F32)
            full = dot_tn(keys, grad_scores)
            gt_out[rows, lo : lo + lanes] = (own_head(full) * scale).T.astype(BF)
            gt_out[rows, channels + lo : channels + lo + lanes] = (
                dot(grad_scores, queries) * scale
            ).astype(BF)
            gt_out[rows, 2 * channels + lo : 2 * channels + lo + lanes] = dot(
                probs.astype(BF), grad_att
            ).astype(BF)
        return carry

    lax.fori_loop(0, tokens // TOKENS, window, 0, unroll=2)


def input_back_kernel(
    group_index, xw_ref, att_ref, gh_ref, gt_ref, to_rows, g1_ref, o1_ref, win_ref,
    d0, d1, d2, d3, low_out, band_out, small_out,
):
    gid = my_set(group_index)
    channels = xw_ref.shape[1]
    grad_mixed = gh_ref[...].astype(BF)
    low_out[3] = dot_tn(att_ref[...], grad_mixed).astype(BF)
    small_out[0:1, :] = jnp.sum(grad_mixed.astype(F32), axis=0, keepdims=True)
    xhat, root = norm_parts(xw_ref[...].astype(F32))
    gain = param_row(g1_ref, gid)
    normed = (xhat * gain + param_row(o1_ref, gid)).astype(BF)
    grad_in = dot(normed.T, gt_ref[...])
    grad = dot_nt(gt_ref[...], win_ref[...])
    for part in range(3):
        cols = slice(part * channels, (part + 1) * channels)
        low_out[part] = grad_in[:, cols].astype(BF)
        if part != 1:
            row = 1 + part // 2
            piece = gt_ref[:, cols].astype(F32)
            small_out[row : row + 1, :] = jnp.sum(piece, axis=0, keepdims=True)
    small_out[3:4, :] = jnp.sum(grad * xhat, axis=0, keepdims=True)
    small_out[4:5, :] = jnp.sum(grad, axis=0, keepdims=True)
    small_out[5:16, :] = jnp.zeros((11, channels), F32)
    band_out[...] = small_out[...].astype(BF)
    shifted = norm_back(grad, gain, xhat, root).astype(BF)
    parts = to_levels(to_rows[...], gh_ref[...] + shifted.astype(F32))
    for part, ref in zip(parts, (d0, d1, d2, d3)):
        ref[...] = part


def assemble_kernel(y0, d0, lev_ref, lat_ref, both_ref, y_out, d_out):
    half, columns = WH // 2, y_out.shape[2]
    for k, (own, out) in enumerate(((y0[...], y_out), (d0[...], d_out))):
        for source, row, level in (
            (own, half, 1), (lev_ref[k], half, 0), (lat_ref[k], 0, 1), (both_ref[k], 0, 0)
        ):
            source = source.astype(F32)
            for h in range(half):
                out[row + h, level] = source[h * columns : (h + 1) * columns].astype(BF)


def spread_kernel(low_ref, *refs):
    pairs = (len(refs) - 3) // 3
    keep_out, send_outs = refs[2 * pairs], refs[2 * pairs + 1 : 2 * pairs + 3]
    for block in range(low_ref.shape[0]):
        scatter_rows(keep_out, send_outs, block // 2, block % 2, low_ref[block])
    for k in range(pairs):
        refs[2 * pairs + 3 + k][0] = refs[k][...]
        refs[2 * pairs + 3 + k][1] = refs[pairs + k][...]


def first_sum_kernel(keep_ref, *refs):
    arrived, outs = refs[:-4], refs[-4:]
    at = 0
    for part in arrived:
        rows = slice(at, at + part.shape[1])
        at += part.shape[1]
        for k in range(4):
            total = keep_ref[k, rows].astype(F32) + part[k].astype(F32)
            outs[k][rows] = total.astype(BF)


def second_sum_kernel(own_ref, y_ref, x_ref, xy_ref, *refs):
    tables, out = refs[:-1], refs[-1]
    rows, channels = own_ref.shape
    total = own_ref[...].astype(F32) + y_ref[...].astype(F32)
    out[:rows] = (total + x_ref[...].astype(F32) + xy_ref[...].astype(F32)).astype(BF)
    at = rows
    for table in tables:
        for band in range(table.shape[1] // channels):
            out[at : at + 16] = table[:, band * channels : (band + 1) * channels]
            at += 16


def stack_kernel(group_index, *refs):
    entries, out, held, arrivals, leavings = refs[:-4], refs[-4], refs[-3], refs[-2], refs[-1]
    count = len(entries)
    mine = lax.axis_index("lat") // WROWS
    samples = lax.axis_size("lat") // WROWS
    inward, outward = [], []
    for k in range(count):
        slot = (mine + samples - k) % samples if samples == count else k
        inward.append(pltpu.make_async_copy(entries[k], held.at[k], arrivals.at[k]))
        outward.append(pltpu.make_async_copy(held.at[k], out.at[slot], leavings.at[k]))
    for copy in inward:
        copy.start()
    for k in range(count):
        inward[k].wait()
        outward[k].start()
    for copy in outward:
        copy.wait()


def anchor_kernel(*refs):
    pass


def slot_of(core_type, index):
    return (index % 2) * 2 + index // 2 if core_type == 0 else index


def fetch_pieces(sources, buffer, semaphores):
    def copies(own, other):
        for core_type, arrays in ((0, own), (1, other)):
            for index in range(4):
                slot = slot_of(core_type, index)
                yield pltpu.make_async_copy(
                    arrays[index],
                    buffer.at[core_type, slot],
                    semaphores.at[core_type, slot],
                )

    @pl.when(my_core() == 0)
    def _():
        for copy in copies(sources[:4], sources[4:]):
            copy.start()

    @pl.when(my_core() == 1)
    def _():
        for copy in copies(sources[4:], sources[:4]):
            copy.start()


def wait_piece(sources, buffer, semaphores, core_type, slot):
    pltpu.make_async_copy(
        sources[0], buffer.at[core_type, slot], semaphores.at[core_type, slot]
    ).wait()


def spread_sets(owners, first, sets, read, write):
    for k in range(len(owners)):

        @pl.when(first[k])
        def _(k=k):
            write(owners[k], False, read(k))

        @pl.when(jnp.logical_not(first[k]))
        def _(k=k):
            write(owners[k], True, read(k))

    if not isinstance(owners[0], int):
        for g in range(sets):
            there = owners[0] == g
            for owner in owners[1:]:
                there = there | (owner == g)

            @pl.when(jnp.logical_not(there))
            def _(g=g):
                write(g, False, [jnp.zeros_like(value) for value in read(0)])


def finish_step(layout, small, outs, buffer, rel, owners, first, sets):
    channels = buffer.shape[4]
    size = channels // 4
    places = []
    for core_type, blocks in enumerate(layout):
        for at, place in enumerate(blocks):
            places.append((core_type, slice(at * size, (at + 1) * size), place))

    def read(k):
        return [buffer[t, rel, k, rows, :].astype(F32) for t, rows, _ in places]

    def write(g, add, values):
        for (_, _, place), value in zip(places, values):
            if place[1] is None:
                index = (g, place[2], 0)
            else:
                index = (g, slice(None), slice(place[1] * channels, (place[1] + 1) * channels))
            ref = outs[place[0]]
            ref[index] = ref[index] + value if add else value

    spread_sets(owners, first, sets, read, write)
    start = len(layout[0]) * size
    q = rel ^ my_place()
    for number, place in enumerate(small):
        if place is None:
            continue

        @pl.when(q == number % 4)
        def _(number=number, place=place):
            out, column = place
            cols = slice(column, column + channels)

            def read(k):
                rows = buffer[number // 4, rel, k, start : start + 16, :]
                return [rows.astype(F32)[0:1]]

            def write(g, add, values):
                index = (pl.ds(g, 1), cols)
                outs[out][index] = outs[out][index] + values[0] if add else values[0]

            spread_sets(owners, first, sets, read, write)


def finish_up_kernel(layout, small, group_index, *refs):
    sources, outs, buffer, semaphores = refs[:8], refs[8:-2], refs[-2], refs[-1]
    step = pl.program_id(0)
    sets, count = outs[0].shape[0], buffer.shape[2]
    owners, first = entry_sets(group_index, count, sets)

    @pl.when(step == 0)
    def _():
        fetch_pieces(sources, buffer, semaphores)

    for core_type in range(2):
        wait_piece(sources, buffer, semaphores, core_type, step)
    finish_step(layout, small, outs, buffer, step, owners, first, sets)


def finish_low_kernel(layout, small, group_index, window_types, *refs):
    sources, outs, buffer, semaphores, held = refs[:8], refs[8:-3], refs[-3], refs[-2], refs[-1]
    step = pl.program_id(0)
    sets, count, channels = outs[0].shape[0], buffer.shape[2], buffer.shape[4]
    owners, first = entry_sets(group_index, count, sets)
    out = outs[-1]
    heads, kinds, positions = out.shape[1:]

    @pl.when(step == 0)
    def _():
        fetch_pieces(sources, buffer, semaphores)

    @pl.when(step < 4)
    def _():
        for core_type in range(2):
            wait_piece(sources, buffer, semaphores, core_type, step)
        finish_step(layout, [], outs, buffer, step, owners, first, sets)

    top = 2 * (channels // 4)

    @pl.when(step == 4)
    def _():
        for ref in outs[2:-1]:
            ref[...] = jnp.zeros_like(ref)
        for k in range(count):
            band = jnp.zeros((16, channels), F32)
            for t in range(2):
                for r in range(4):
                    band = band + buffer[t, r, k, top + held.shape[1] // channels * 16 :].astype(F32)
            for n, (number, column) in enumerate(small):
                index = (pl.ds(owners[k], 1), slice(column, column + channels))
                outs[number][index] = outs[number][index] + band[n : n + 1]
            for t in range(2):
                for r in range(4):
                    at = ((k * 2 + t) * 4 + r) * 16
                    for band in range(held.shape[1] // channels):
                        rows = slice(top + 16 * band, top + 16 * band + 16)
                        held[at : at + 16, band * channels : (band + 1) * channels] = buffer[
                            t, r, k, rows
                        ]

    @pl.when(step >= 4)
    def _():
        shape = (heads * kinds, count * 128)
        row = lax.broadcasted_iota(jnp.int32, shape, 0)
        col = lax.broadcasted_iota(jnp.int32, shape, 1)
        kind_of = jnp.zeros(shape, jnp.int32)
        for t in range(2):
            for r in range(4):
                q = r ^ my_place()
                kind = window_types[q // 2 * 4 + t * 2 + q % 2]
                kind_of = jnp.where(col // 16 % 8 == t * 4 + r, kind, kind_of)
        set_of = jnp.zeros(shape, jnp.int32)
        for k in range(count):
            set_of = jnp.where(col // 128 == k, owners[k], set_of)
        hit = (row // kinds == col % 16) & (row % kinds == kind_of) & (set_of == step - 4)
        value = dot(jnp.where(hit, 1.0, 0.0).astype(BF), held[...])
        out[0] = value[:, :positions].reshape(out.shape[1:])


def whole(array_or_shape):
    shape = getattr(array_or_shape, "shape", array_or_shape)
    return pl.BlockSpec(shape, lambda i, *_: (0,) * len(shape))


def own_member(array):
    def index(i, group_index, *_):
        return (my_set(group_index),) + (0,) * (array.ndim - 1)

    return pl.BlockSpec((None,) + array.shape[1:], index)


def call(
    kernel, scalars, inputs, out_shapes, *, in_specs=None, out_specs=None, scratch=(), grid=(1,),
    after=(), cost=1.0, aliases=None,
):
    in_specs = [whole(v) for v in inputs] if in_specs is None else in_specs
    out_specs = jax.tree.map(whole, out_shapes) if out_specs is None else out_specs
    count = len(scalars) + len(inputs)
    body = kernel
    if after:

        def body(*refs):
            kernel(*refs[:count], *refs[count + len(after) :])

    after = list(after)

    return pl.pallas_call(
        body,
        grid_spec=pltpu.PrefetchScalarGridSpec(
            num_scalar_prefetch=len(scalars),
            grid=grid,
            in_specs=list(in_specs) + [pl.BlockSpec(memory_space=pl.ANY)] * len(after),
            out_specs=out_specs,
            scratch_shapes=list(scratch),
        ),
        out_shape=out_shapes,
        input_output_aliases=aliases or {},
        compiler_params=pltpu.CompilerParams(vmem_limit_bytes=60 * 1024 * 1024),
        cost_estimate=pl.CostEstimate(
            flops=int(cost * 1.1e9), bytes_accessed=10**3, transcendentals=0
        ),
    )(*scalars, *inputs, *after)


def like(shape, kind=BF):
    return jax.ShapeDtypeStruct(tuple(shape), kind)


def swap(value, axis, distance):
    pairs = [(i, i ^ distance) for i in range(lax.axis_size(axis))]
    return lax.ppermute(value, axis, pairs)


def move_both(value, step, cross):
    lev, lat = lax.axis_size("lev"), lax.axis_size("lat")
    pairs = [
        (a * lat + b, step(a, lev) * lat + (b ^ cross)) for a in range(lev) for b in range(lat)
    ]
    return lax.ppermute(value, ("lev", "lat"), pairs)


def below(a, size):
    return (a - 1) % size


def above(a, size):
    return (a + 1) % size


def over_x(a, size):
    return a ^ 2


def quadrants(*blocks):
    half = WH // 2
    rows = half * blocks[0].shape[2]

    def flat(part):
        return jnp.stack([part(block).reshape(rows, block.shape[3]) for block in blocks])

    return [
        flat(lambda block: block[half:, 1]),
        move_both(flat(lambda block: block[half:, 0]), below, 0),
        swap(flat(lambda block: block[:half, 1]), "lat", 1),
        move_both(flat(lambda block: block[:half, 0]), below, 1),
    ]


def reduce_cores(keep, arrived, after=()):
    shape = like(keep.shape[1:])
    return call(first_sum_kernel, [], [keep] + arrived, [shape] * 4, after=after, cost=0.1)


def move_chips(parts):
    own, along_y, along_x, along_both = parts
    return [own, swap(along_y, "lat", 1), swap(along_x, "lev", 2), move_both(along_both, over_x, 1)]


def reduce_chips(parts, tables=(), after=()):
    rows, channels = parts[0].shape
    rows += sum(16 * (table.shape[1] // channels) for table in tables)
    shape = like((rows, channels))
    return call(second_sum_kernel, [], parts + list(tables), shape, after=after, cost=0.1)


def round_samples(share, group_index, sets, after=(), cost=0.1):
    lat = lax.axis_size("lat")
    samples = lat // WROWS
    if samples > sets:
        groups = [[s * WROWS + b for s in range(samples)] for b in range(WROWS)]
        hot = (jnp.arange(sets) == group_index[lax.axis_index("lat") // WROWS]).astype(F32)
        total = hot[:, None, None] * share.astype(F32)[None]
        total = lax.psum(total, "lat", axis_index_groups=groups).astype(BF)
        entries = [total[k] for k in range(sets)]
    else:
        entries = [share]
        for k in range(1, samples):
            pairs = [(i, (i + WROWS * k) % lat) for i in range(lat)]
            entries.append(lax.ppermute(share, "lat", pairs))
    shape = like((len(entries),) + share.shape)
    anywhere = pl.BlockSpec(memory_space=pl.ANY)
    return call(
        stack_kernel,
        [group_index],
        entries,
        shape,
        in_specs=[anywhere] * len(entries),
        out_specs=anywhere,
        scratch=[pltpu.VMEM(shape.shape, BF)] + [pltpu.SemaphoreType.DMA((len(entries),))] * 2,
        after=after,
        cost=cost,
    )


def hop(value, turn):
    lev, lat = lax.axis_size("lev"), lax.axis_size("lat")
    pairs = [
        (a * lat + b, (a ^ 2) * lat + b if a % 2 == turn else a * lat + (b ^ 1))
        for a in range(lev)
        for b in range(lat)
    ]
    return lax.ppermute(value, ("lev", "lat"), pairs)


def anchored(value, after, cost=0.1):
    anywhere = pl.BlockSpec(memory_space=pl.ANY)
    return call(
        anchor_kernel, [], [value], like(value.shape), in_specs=[anywhere], out_specs=anywhere,
        after=after, aliases={0: 0}, cost=cost,
    )


def body(
    fields,
    group_index,
    window_types,
    window_masks,
    first_gain,
    first_offset,
    input_weight,
    input_bias,
    output_weight,
    output_bias,
    second_gain,
    second_offset,
    expand_weight,
    expand_bias,
    reduce_weight,
    reduce_bias,
    position_bias,
    cotangent,
):
    columns = fields.shape[2]
    channels = fields.shape[3]
    sets, kinds, heads, positions = position_bias.shape
    groups = heads // GROUP
    cells = WZ * WH
    tokens = columns * cells
    rows = tokens // 4
    quarter = channels // 4
    lanes = channels // groups
    to_win = jnp.asarray(window_order(columns), BF)
    to_rows = jnp.asarray(window_order(columns).T, BF)
    own_lanes = jnp.asarray(head_lanes(lanes), BF)
    cols_map = jnp.asarray(column_maps(), BF)
    rows_map = jnp.asarray(token_rows(), BF)
    rows_back = jnp.asarray(token_rows().T, BF)
    places = jnp.asarray(head_places(), BF)
    fold = jnp.asarray(fold_map(), BF)

    arrived = quadrants(fields, cotangent)

    by_head = position_bias.transpose(0, 2, 1, 3)
    table = call(
        select_kernel,
        [group_index, window_types],
        [by_head],
        like((heads, positions)),
        in_specs=[own_member(by_head)],
        cost=1.0,
    )
    table = table.reshape(heads, WZ, WZ, WH, WH, SPAN).transpose(0, 2, 4, 1, 3, 5)
    table = table.reshape(heads, cells, cells * SPAN)
    table = jnp.pad(table, ((0, 0), (0, 16 - cells), (0, 0))).reshape(heads * 16, cells * SPAN)
    bias_map = call(
        bias_kernel,
        [],
        [window_masks, table, cols_map, rows_map, places, fold],
        like((groups, TOKENS, PADDED), F32),
        scratch=[pltpu.VMEM((heads, 16 * WW, TOKENS), BF)],
        cost=5.0,
    )

    hidden_units = expand_weight.shape[2]
    assert hidden_units == 4 * channels
    up_rows = 4 * quarter + 16
    low_rows = 2 * quarter
    inputs = (
        arrived
        + [to_win, to_rows, bias_map, own_lanes, first_gain, first_offset]
        + [input_weight, input_bias, output_weight, output_bias, second_gain, second_offset]
        + [expand_weight, expand_bias, reduce_weight, reduce_bias]
    )
    weights = {id(v) for v in (input_weight, output_weight, expand_weight, reduce_weight)}
    quadrant = like((rows, channels))
    anywhere = pl.BlockSpec(memory_space=pl.ANY)
    y0, y1, y2, y3, xw, triple, att, grad_hidden, keep, send = call(
        forward_kernel,
        [group_index],
        inputs,
        [quadrant] * 4
        + [
            like((tokens, channels)),
            like((tokens, 3 * channels)),
            like((tokens, channels)),
            like((tokens, channels), F32),
            like((4, up_rows, channels)),
            like((4, up_rows, channels)),
        ],
        in_specs=[
            anywhere if v is expand_weight or v is reduce_weight
            else own_member(v) if id(v) in weights
            else whole(v)
            for v in inputs
        ],
        out_specs=[whole(quadrant)] * 4
        + [anywhere] * 3
        + [whole((tokens, channels))]
        + [whole((4, up_rows, channels))] * 2,
        scratch=[
            pltpu.VMEM((tokens, channels), BF),
            pltpu.VMEM((channels, tokens), BF),
            pltpu.VMEM((tokens, channels), BF),
            pltpu.VMEM((tokens, channels), F32),
            pltpu.VMEM((tokens, channels), F32),
            pltpu.VMEM((8, channels), F32),
            pltpu.VMEM((channels, hidden_units), BF),
            pltpu.VMEM((hidden_units, channels), BF),
            pltpu.VMEM((tokens, channels), BF),
            pltpu.VMEM((tokens, 3 * channels), BF),
            pltpu.VMEM((tokens, channels), BF),
            pltpu.SemaphoreType.DMA((5,)),
        ],
        cost=33.0,
    )

    up_parts = reduce_cores(keep, [swap(send, "lev", 1)])
    inputs = [triple, grad_hidden, bias_map, own_lanes, output_weight]
    grad_triple, score_sums = call(
        scores_back_kernel,
        [group_index],
        inputs,
        [like((tokens, 3 * channels)), like((groups, TOKENS, PADDED), F32)],
        in_specs=[own_member(v) if id(v) in weights else whole(v) for v in inputs],
        scratch=[pltpu.VMEM((tokens, channels), BF)],
        after=[up_parts[3]],
        cost=20.0,
    )
    up_share = reduce_chips(move_chips(up_parts), after=[grad_triple])

    inputs = [xw, att, grad_hidden, grad_triple, to_rows, first_gain, first_offset, input_weight]
    d0, d1, d2, d3, low_grads, low_small = call(
        input_back_kernel,
        [group_index],
        inputs,
        [quadrant] * 4 + [like((4, channels, channels)), like((16, channels))],
        in_specs=[own_member(v) if id(v) in weights else whole(v) for v in inputs],
        scratch=[pltpu.VMEM((16, channels), F32)],
        after=[up_share],
        cost=8.0,
    )
    low_keep, *rest = call(
        spread_kernel,
        [],
        [low_grads, y1, y2, y3, d1, d2, d3],
        [like((4, low_rows, channels))]
        + [like((4, quarter, channels))] * 2
        + [like((2, rows, channels))] * 3,
        cost=0.1,
    )
    low_send, (s1, s2, s3) = rest[:2], rest[2:]
    low_arrived = [swap(send, "lev", 1) for send in low_send]
    up_stack = round_samples(up_share, group_index, sets, after=low_arrived)
    low_parts = reduce_cores(low_keep, low_arrived, after=[up_stack])

    up_hop = hop(up_stack, 0)
    low_sums = move_chips(low_parts)
    table_grad = call(
        fold_kernel,
        [],
        [score_sums, cols_map, rows_back, places],
        like((heads * 16, cells * SPAN)),
        scratch=[pltpu.VMEM((2, WW, heads * 16, TOKENS), BF)],
        after=[up_stack],
        cost=7.0,
    )
    table_grad = table_grad.reshape(heads, 16, cells * SPAN)[:, :cells]
    table_grad = table_grad.reshape(heads, WZ, WH, WZ, WH, SPAN).transpose(0, 3, 1, 4, 2, 5)
    wide = -(-positions // channels) * channels
    table_grad = jnp.pad(
        table_grad.reshape(heads, positions), ((0, 16 - heads), (0, wide - positions))
    )
    low_share = reduce_chips(low_sums, [table_grad, low_small], after=[up_hop])

    up_stack = anchored(up_stack, [low_share])
    up_own = [up_stack, up_hop, hop(up_stack, 1), hop(up_hop, 1)]
    low_stack = round_samples(low_share, group_index, sets, after=up_own[2:], cost=10.0)
    up_other = [swap(v, "lev", 1) for v in up_own]
    low_hop = hop(low_stack, 0)
    low_stack = anchored(low_stack, [low_hop], cost=12.0)
    low_own = [low_stack, low_hop, hop(low_stack, 1), hop(low_hop, 1)]

    count = low_stack.shape[0]
    up_shapes = [
        like((sets, channels, hidden_units), F32),
        like((sets, 4, 4, quarter, channels), F32),
        like((sets, hidden_units), F32),
    ] + [like((sets, channels), F32)] * 3
    up_grad, down_grad, bup_grad, bdn_grad, g2_grad, o2_grad = call(
        functools.partial(
            finish_up_kernel,
            [[(0, k) for k in range(4)], [(1, None, k) for k in range(4)]],
            [(2, k * channels) for k in range(4)] + [(3, 0), (4, 0), (5, 0)],
        ),
        [group_index],
        up_own + up_other,
        up_shapes,
        in_specs=[anywhere] * 8,
        out_specs=[
            pl.BlockSpec((sets, quarter, hidden_units), lambda r, g: (0, r ^ my_place(), 0)),
            pl.BlockSpec(
                (sets, 4, 1, quarter, channels), lambda r, g: (0, 0, r ^ my_place(), 0, 0)
            ),
        ]
        + [whole(v) for v in up_shapes[2:]],
        scratch=[
            pltpu.VMEM((2, 4, count, up_rows, channels), BF),
            pltpu.SemaphoreType.DMA((2, 4)),
        ],
        grid=(4,),
        cost=11.0,
    )
    low_own[3] = anchored(low_own[3], [up_grad])
    low_other = [swap(v, "lev", 1) for v in low_own]
    low_shapes = (
        [
            like((sets, channels, 3 * channels), F32),
            like((sets, 1, 4, quarter, channels), F32),
        ]
        + [like((sets, w), F32) for w in (channels, 2 * channels, channels, channels)]
        + [like((sets, heads, kinds, positions), F32)]
    )

    def row_block(i):
        return jnp.minimum(i, 3) ^ my_place()

    in_grad, out_grad, bout_grad, bin_grad, g1_grad, o1_grad, position_grad = call(
        functools.partial(
            finish_low_kernel,
            [[(0, 0), (0, 1)], [(0, 2), (1, None, 0)]],
            [(2, 0), (3, 0), (3, channels), (4, 0), (5, 0)],
        ),
        [group_index, window_types],
        low_own + low_other,
        low_shapes,
        in_specs=[anywhere] * 8,
        out_specs=[
            pl.BlockSpec((sets, quarter, 3 * channels), lambda i, *_: (0, row_block(i), 0)),
            pl.BlockSpec(
                (sets, 1, 1, quarter, channels), lambda i, *_: (0, 0, row_block(i), 0, 0)
            ),
        ]
        + [whole(v) for v in low_shapes[2:-1]]
        + [
            pl.BlockSpec(
                (1, heads, kinds, positions), lambda i, *_: (jnp.maximum(i - 4, 0), 0, 0, 0)
            )
        ],
        scratch=[
            pltpu.VMEM((2, 4, count, low_stack.shape[1], channels), BF),
            pltpu.SemaphoreType.DMA((2, 4)),
            pltpu.VMEM((count * 128, wide), BF),
        ],
        grid=(4 + sets,),
        cost=10.0,
    )

    back = [move_both(s1, above, 0), swap(s2, "lat", 1), move_both(s3, above, 1)]
    output, input_grad = call(
        assemble_kernel,
        [],
        [y0, d0] + back,
        [like(fields.shape)] * 2,
        after=[position_grad],
        cost=1.0,
    )
    out_grad = out_grad.reshape(sets, -1, channels)
    down_grad = down_grad.reshape(sets, -1, channels)
    position_grad = position_grad.transpose(0, 2, 1, 3)
    return (
        output,
        input_grad,
        g1_grad,
        o1_grad,
        in_grad,
        bin_grad,
        out_grad,
        bout_grad,
        g2_grad,
        o2_grad,
        up_grad,
        bup_grad,
        down_grad,
        bdn_grad,
        position_grad,
    )


def solution(mesh):
    slab = P("lat", "lev", None, None)
    return jax.shard_map(
        body,
        mesh=mesh,
        in_specs=(slab,) + (P(),) * 16 + (slab,),
        out_specs=(slab, slab) + (P(),) * 13,
        check_vma=False,
    )
```

```python
import functools

import jax
import jax.numpy as jnp
import numpy as np
from jax import lax
from jax.experimental import pallas as pl
from jax.experimental.pallas import tpu as pltpu
from jax.sharding import PartitionSpec as P

WZ = 2
WH = 6
WW = 12
WROWS = 2
TOKENS = WZ * WH * WW
GROUP = 4
PADDED = 640
SPAN = 2 * WW - 1
MASKED = -1e30
LOG2E = 1.4426950408889634
BF = jnp.bfloat16
F32 = jnp.float32


def dot(a, b):
    return lax.dot_general(a, b, (((1,), (0,)), ((), ())), preferred_element_type=F32)


def dot_nt(a, b):
    return lax.dot_general(a, b, (((1,), (1,)), ((), ())), preferred_element_type=F32)


def dot_tn(a, b):
    return lax.dot_general(a, b, (((0,), (0,)), ((), ())), preferred_element_type=F32)


def one_hot(index, size):
    return (np.asarray(index)[:, None] == np.arange(size)[None, :]).astype(np.float32)


def window_order(columns):
    windows = columns // WW
    n, h, w = np.meshgrid(np.arange(windows), np.arange(WH), np.arange(WW), indexing="ij")
    source = h * columns + (n * WW + w + WW // 2) % columns
    return one_hot(source.reshape(-1), WH * columns)


def column_maps():
    cells = WZ * WH
    out = np.zeros((WW, cells, SPAN, cells, WW), np.float32)
    for wj in range(WW):
        for wi in range(WW):
            for c in range(cells):
                out[wj, c, wi - wj + WW - 1, c, wi] = 1.0
    return out.reshape(WW, cells * SPAN, cells * WW)


def token_rows():
    j = np.arange(TOKENS)
    return one_hot((j % WW) * 16 + j // WW, WW * 16)


def head_places():
    return np.stack([one_hot(h * TOKENS + np.arange(TOKENS), PADDED) for h in range(GROUP)])


def fold_map():
    return sum(head_places())


def head_lanes(lanes):
    return np.repeat(np.eye(GROUP, dtype=np.float32), lanes // GROUP, axis=1)


def select_kernel(group_index, window_types, tables_ref, out_ref):
    heads, kinds, positions = tables_ref.shape
    place = lax.axis_index("lev") * WROWS + lax.axis_index("lat") % WROWS
    kind = window_types[place]
    shape = (heads, heads * kinds)
    row = lax.broadcasted_iota(jnp.int32, shape, 0)
    col = lax.broadcasted_iota(jnp.int32, shape, 1)
    pick = jnp.where(col == row * kinds + kind, 1.0, 0.0).astype(BF)
    tables = tables_ref[...].astype(F32).reshape(heads * kinds, positions).astype(BF)
    out_ref[...] = dot(pick, tables).astype(BF)


def bias_kernel(masks_ref, table_ref, cols_ref, rows_ref, places_ref, fold_ref, out_ref, held):
    heads = held.shape[0]
    for wj in range(WW):
        part = dot(table_ref[...], cols_ref[wj]).astype(BF)
        for h in range(heads):
            held[h, 16 * wj : 16 * wj + 16, :] = part[16 * h : 16 * h + 16]
    half = lax.axis_index("lat") % WROWS
    labels = masks_ref[lax.axis_index("lev"), pl.ds(half, 1), :].astype(F32)
    top = lax.broadcasted_iota(jnp.int32, (8, TOKENS), 0) == 0
    labels = jnp.where(top, jnp.broadcast_to(labels, (8, TOKENS)), 0.0)
    across = dot(jnp.ones((TOKENS, 8), BF), dot(labels.astype(BF), fold_ref[...]).astype(BF))
    down = dot_tn(labels.astype(BF), jnp.ones((8, PADDED), BF))
    same = jnp.abs(across - down) < 0.5
    for g in range(heads // GROUP):
        total = dot(held[g * GROUP], places_ref[0])
        for h in range(1, GROUP):
            total = total + dot(held[g * GROUP + h], places_ref[h])
        out_ref[g] = jnp.where(same, dot(rows_ref[...], total.astype(BF)), MASKED) * LOG2E


def fold_kernel(sums_ref, cols_ref, rows_ref, places_ref, out_ref, held):
    groups = sums_ref.shape[0]
    for g in range(groups):
        value = sums_ref[g]
        high = value.astype(BF)
        low = (value - high.astype(F32)).astype(BF)
        for index, part in enumerate((high, low)):
            ordered = dot(rows_ref[...], part).astype(BF)
            for h in range(GROUP):
                block = dot_nt(ordered, places_ref[h]).astype(BF)
                spot = (g * GROUP + h) * 16
                for wj in range(WW):
                    held[index, wj, spot : spot + 16, :] = block[16 * wj : 16 * wj + 16]
    total = jnp.zeros(out_ref.shape, F32)
    for wj in range(WW):
        for index in range(2):
            total = total + dot_nt(held[index, wj], cols_ref[wj])
    out_ref[...] = total.astype(BF)


def norm_parts(values):
    centre = values - jnp.mean(values, axis=-1, keepdims=True)
    spread = jnp.mean(centre * centre, axis=-1, keepdims=True)
    root = lax.rsqrt(spread + 1e-05)
    return centre * root, root


def norm_back(grad, gain, xhat, root):
    u = grad * gain
    return (
        u - jnp.mean(u, axis=-1, keepdims=True) - xhat * jnp.mean(u * xhat, axis=-1, keepdims=True)
    ) * root


def stacked_heads(block, lanes_ref):
    pieces = [block * lanes_ref[h : h + 1, :] for h in range(GROUP)]
    pieces.append(jnp.zeros((PADDED - GROUP * block.shape[0], block.shape[1]), block.dtype))
    return jnp.concatenate(pieces, axis=0)


def own_head(full):
    size = full.shape[0] // GROUP
    return jnp.concatenate(
        [
            full[h * size : (h + 1) * size, h * TOKENS : (h + 1) * TOKENS]
            for h in range(GROUP)
        ],
        axis=0,
    )


def softmax_t(keys, queries, bias, scale):
    scores = dot_nt(keys, queries) * (scale * LOG2E) + bias
    exponent = jnp.exp2(scores - jnp.max(scores, axis=0, keepdims=True))
    return exponent * (1.0 / jnp.sum(exponent, axis=0, keepdims=True))


def to_windows(level_map, levels):
    half = WH * WW
    parts = [dot(level_map, level) for level in levels]
    pieces = []
    for n in range(parts[0].shape[0] // half):
        for part in parts:
            pieces.append(part[n * half : (n + 1) * half])
    return jnp.concatenate(pieces, axis=0)


def to_levels(level_map, value):
    half = WH * WW
    count = value.shape[0] // (2 * half)
    quadrants = [None] * 4
    for z in range(WZ):
        level = [value[(2 * n + z) * half : (2 * n + z + 1) * half] for n in range(count)]
        level = dot(level_map, jnp.concatenate(level, axis=0).astype(BF))
        rows = level.shape[0] // 2
        for side in range(2):
            quadrants[side * WZ + z] = level[side * rows : (side + 1) * rows].astype(BF)
    return quadrants


def my_place():
    return (lax.axis_index("lev") // 2) * 2 + lax.axis_index("lat") % WROWS


def my_core():
    return lax.axis_index("lev") % 2


def place_slot(keep_out, send_outs, owner, rel, start, value):
    @pl.when(my_core() == owner)
    def _():
        keep_out[rel, start : start + value.shape[0]] = value

    @pl.when(my_core() != owner)
    def _():
        at = start
        for out in send_outs:
            if 0 <= at < out.shape[1]:
                out[rel, at : at + value.shape[0]] = value
            at -= out.shape[1]


def scatter_rows(keep_out, send_outs, owner, block, value):
    value = value.astype(BF)
    size = value.shape[0] // 4
    for q in range(4):
        piece = value[q * size : (q + 1) * size]
        place_slot(keep_out, send_outs, owner, q ^ my_place(), block * size, piece)


def scatter_small(keep_out, send_outs, small):
    start = keep_out.shape[1] - 16
    for n in range(8):
        row = jnp.broadcast_to(small[n : n + 1, :], (16, small.shape[1])).astype(BF)
        place_slot(keep_out, send_outs, n // 4, (n % 4) ^ my_place(), start, row)


def my_set(group_index):
    return group_index[lax.axis_index("lat") // WROWS]


def entry_sets(group_index, count, sets):
    samples = lax.axis_size("lat") // WROWS
    if samples > sets:
        return list(range(sets)), [True] * sets
    owners = [group_index[k] for k in range(count)]
    first = []
    for k in range(count):
        fresh = jnp.bool_(True)
        for j in range(k):
            fresh = fresh & (owners[j] != owners[k])
        first.append(fresh)
    return owners, first


def param_row(ref, group):
    return ref[pl.ds(group, 1), :]


def forward_kernel(
    group_index, f0, f1, f2, f3, to_win, to_rows, bias_ref, lanes_ref,
    g1_ref, o1_ref, win_ref, bin_ref, wout_ref, bout_ref, g2_ref, o2_ref,
    wups_ref, bup_ref, wdns_ref, bdn_ref,
    y0, y1, y2, y3, xw_any, triple_any, att_any, gh_out, keep_out, send_out,
    n2_s, n2t_s, cot_s, acc_s, back_s, small_out,
    wup_ref, wdn_ref, xw_out, triple_out, att_out, semaphores,
):
    gid = my_set(group_index)
    tokens, channels = xw_out.shape
    weights = [
        pltpu.make_async_copy(source.at[gid], target, semaphores.at[k])
        for k, (source, target) in enumerate(((wups_ref, wup_ref), (wdns_ref, wdn_ref)))
    ]
    for copy in weights:
        copy.start()
    results = [
        pltpu.make_async_copy(source, target, semaphores.at[2 + k])
        for k, (source, target) in enumerate(
            ((xw_out, xw_any), (triple_out, triple_any), (att_out, att_any))
        )
    ]
    lanes = lanes_ref.shape[1]
    scale = (lanes // GROUP) ** -0.5

    def gathered(which):
        levels = [
            jnp.concatenate([low[which].astype(F32), high[which].astype(F32)], axis=0).astype(BF)
            for low, high in ((f0, f2), (f1, f3))
        ]
        return to_windows(to_win[...], levels)

    x = gathered(0)
    xw_out[...] = x.astype(BF)
    cot_s[...] = gathered(1).astype(BF)
    xhat, _ = norm_parts(x)
    normed = (xhat * param_row(g1_ref, gid) + param_row(o1_ref, gid)).astype(BF)
    bias_row = param_row(bin_ref, gid)
    bias_row = jnp.concatenate(
        [bias_row[:, :channels], jnp.zeros((1, channels), F32), bias_row[:, channels:]], axis=1
    )
    triple_out[...] = (dot(normed, win_ref[...]) + bias_row).astype(BF)
    results[0].start()
    results[1].start()

    def window(n, carry):
        rows = pl.ds(pl.multiple_of(n * TOKENS, 16), TOKENS)
        for g in range(channels // lanes):
            lo = g * lanes
            queries = stacked_heads(triple_out[rows, lo : lo + lanes], lanes_ref)
            keys = triple_out[rows, channels + lo : channels + lo + lanes]
            values = triple_out[rows, 2 * channels + lo : 2 * channels + lo + lanes]
            probs = softmax_t(keys, queries, bias_ref[g], scale).astype(BF)
            full = dot_tn(values, probs)
            att_out[rows, lo : lo + lanes] = own_head(full).T.astype(BF)
        return carry

    lax.fori_loop(0, tokens // TOKENS, window, 0, unroll=2)

    results[2].start()
    mixed = (dot(att_out[...], wout_ref[...]) + param_row(bout_ref, gid)).astype(BF)
    hidden = xw_out[...].astype(F32) + mixed.astype(F32)
    xhat2, root2 = norm_parts(hidden)
    gain2 = param_row(g2_ref, gid)
    n2 = (xhat2 * gain2 + param_row(o2_ref, gid)).astype(BF)
    n2_s[...] = n2
    n2t_s[...] = n2.T
    acc_s[...] = hidden + param_row(bdn_ref, gid)
    per = 4
    step = per * channels

    bup = param_row(bup_ref, gid)
    for copy in weights:
        copy.wait()
    for k in range(wup_ref.shape[1] // step):
        cols = slice(k * step, (k + 1) * step)
        up = wup_ref[:, cols]
        down = wdn_ref[cols, :]
        expanded = dot(n2_s[...], up) + bup[:, cols]
        cdf = 0.5 * (1.0 + lax.erf(expanded * (0.5**0.5)))
        active = (expanded * cdf).astype(BF)
        slope = cdf + expanded * (jnp.exp(-0.5 * expanded * expanded) * 0.3989422804014327)
        grad_expanded = (dot_nt(cot_s[...], down) * slope).astype(BF)
        acc_s[...] += dot(active, down)
        back = dot_nt(grad_expanded, up)
        back_s[...] = back if k == 0 else back_s[...] + back
        grad_up = dot(n2t_s[...], grad_expanded)
        grad_down = dot_tn(active, cot_s[...])
        sums = jnp.sum(grad_expanded.astype(F32), axis=0, keepdims=True)
        for j in range(per):
            part = slice(j * channels, (j + 1) * channels)
            scatter_rows(keep_out, [send_out], 0, per * k + j, grad_up[:, part])
            scatter_rows(keep_out, [send_out], 1, per * k + j, grad_down[part])
            small_out[per * k + j : per * k + j + 1, :] = sums[:, part]

    for ref, value in zip((y0, y1, y2, y3), to_levels(to_rows[...], acc_s[...])):
        ref[...] = value
    cot = cot_s[...].astype(F32)
    grad = back_s[...]
    small_out[4:5, :] = jnp.sum(cot, axis=0, keepdims=True)
    small_out[5:6, :] = jnp.sum(grad * xhat2, axis=0, keepdims=True)
    small_out[6:7, :] = jnp.sum(grad, axis=0, keepdims=True)
    small_out[7:8, :] = jnp.zeros((1, channels), F32)
    scatter_small(keep_out, [send_out], small_out[...])
    gh_out[...] = cot + norm_back(grad, gain2, xhat2, root2)
    for copy in results:
        copy.wait()


def scores_back_kernel(
    group_index, triple_ref, gh_ref, bias_ref, lanes_ref, wout_ref,
    gt_out, sums_out, ga_s,
):
    channels = gh_ref.shape[1]
    tokens = gh_ref.shape[0]
    lanes = lanes_ref.shape[1]
    scale = (lanes // GROUP) ** -0.5
    ga_s[...] = dot_nt(gh_ref[...].astype(BF), wout_ref[...]).astype(BF)
    sums_out[...] = jnp.zeros_like(sums_out)

    def window(n, carry):
        rows = pl.ds(pl.multiple_of(n * TOKENS, 16), TOKENS)
        for g in range(channels // lanes):
            lo = g * lanes
            queries = stacked_heads(triple_ref[rows, lo : lo + lanes], lanes_ref)
            keys = triple_ref[rows, channels + lo : channels + lo + lanes]
            values = triple_ref[rows, 2 * channels + lo : 2 * channels + lo + lanes]
            probs = softmax_t(keys, queries, bias_ref[g], scale)
            grad_att = stacked_heads(ga_s[rows, lo : lo + lanes], lanes_ref)
            grad_probs = dot_nt(values, grad_att)
            row_dot = jnp.sum(probs * grad_probs, axis=0, keepdims=True)
            grad_scores = (probs * (grad_probs - row_dot)).astype(BF)
            sums_out[g] += grad_scores.astype(F32)
            full = dot_tn(keys, grad_scores)
            gt_out[rows, lo : lo + lanes] = (own_head(full) * scale).T.astype(BF)
            gt_out[rows, channels + lo : channels + lo + lanes] = (
                dot(grad_scores, queries) * scale
            ).astype(BF)
            gt_out[rows, 2 * channels + lo : 2 * channels + lo + lanes] = dot(
                probs.astype(BF), grad_att
            ).astype(BF)
        return carry

    lax.fori_loop(0, tokens // TOKENS, window, 0, unroll=2)


def input_back_kernel(
    group_index, xw_ref, att_ref, gh_ref, gt_ref, to_rows, g1_ref, o1_ref, win_ref,
    d0, d1, d2, d3, low_out, band_out, small_out,
):
    gid = my_set(group_index)
    channels = xw_ref.shape[1]
    grad_mixed = gh_ref[...].astype(BF)
    low_out[3] = dot_tn(att_ref[...], grad_mixed).astype(BF)
    small_out[0:1, :] = jnp.sum(grad_mixed.astype(F32), axis=0, keepdims=True)
    xhat, root = norm_parts(xw_ref[...].astype(F32))
    gain = param_row(g1_ref, gid)
    normed = (xhat * gain + param_row(o1_ref, gid)).astype(BF)
    grad_in = dot(normed.T, gt_ref[...])
    grad = dot_nt(gt_ref[...], win_ref[...])
    for part in range(3):
        cols = slice(part * channels, (part + 1) * channels)
        low_out[part] = grad_in[:, cols].astype(BF)
        if part != 1:
            row = 1 + part // 2
            piece = gt_ref[:, cols].astype(F32)
            small_out[row : row + 1, :] = jnp.sum(piece, axis=0, keepdims=True)
    small_out[3:4, :] = jnp.sum(grad * xhat, axis=0, keepdims=True)
    small_out[4:5, :] = jnp.sum(grad, axis=0, keepdims=True)
    small_out[5:16, :] = jnp.zeros((11, channels), F32)
    band_out[...] = small_out[...].astype(BF)
    shifted = norm_back(grad, gain, xhat, root).astype(BF)
    parts = to_levels(to_rows[...], gh_ref[...] + shifted.astype(F32))
    for part, ref in zip(parts, (d0, d1, d2, d3)):
        ref[...] = part


def split_kernel(fields_ref, cot_ref, *outs):
    half = WH // 2
    for out, (row, level) in zip(outs, ((half, 1), (half, 0), (0, 1), (0, 0))):
        for k, ref in enumerate((fields_ref, cot_ref)):
            parts = [ref[row + h, level].astype(F32) for h in range(half)]
            out[k] = jnp.concatenate(parts, axis=0).astype(BF)


def assemble_kernel(own_ref, lev_ref, lat_ref, both_ref, out):
    half, columns = WH // 2, out.shape[2]
    for ref, row, level in (
        (own_ref, half, 1), (lev_ref, half, 0), (lat_ref, 0, 1), (both_ref, 0, 0)
    ):
        value = ref[...].astype(F32)
        for h in range(half):
            out[row + h, level] = value[h * columns : (h + 1) * columns].astype(BF)


def spread_kernel(low_ref, keep_out, *send_outs):
    for block in range(low_ref.shape[0]):
        scatter_rows(keep_out, send_outs, block // 2, block % 2, low_ref[block])


def first_sum_kernel(keep_ref, *refs):
    arrived, outs = refs[:-4], refs[-4:]
    at = 0
    for part in arrived:
        rows = slice(at, at + part.shape[1])
        at += part.shape[1]
        for k in range(4):
            total = keep_ref[k, rows].astype(F32) + part[k].astype(F32)
            outs[k][rows] = total.astype(BF)


def second_sum_kernel(own_ref, y_ref, x_ref, xy_ref, *refs):
    tables, out = refs[:-1], refs[-1]
    rows, channels = own_ref.shape
    total = own_ref[...].astype(F32) + y_ref[...].astype(F32)
    out[:rows] = (total + x_ref[...].astype(F32) + xy_ref[...].astype(F32)).astype(BF)
    at = rows
    for table in tables:
        for band in range(table.shape[1] // channels):
            out[at : at + 16] = table[:, band * channels : (band + 1) * channels]
            at += 16


def stack_kernel(group_index, *refs):
    entries, out, held, arrivals, leavings = refs[:-4], refs[-4], refs[-3], refs[-2], refs[-1]
    count = len(entries)
    mine = lax.axis_index("lat") // WROWS
    samples = lax.axis_size("lat") // WROWS
    inward, outward = [], []
    for k in range(count):
        slot = (mine + samples - k) % samples if samples == count else k
        inward.append(pltpu.make_async_copy(entries[k], held.at[k], arrivals.at[k]))
        outward.append(pltpu.make_async_copy(held.at[k], out.at[slot], leavings.at[k]))
    for copy in inward:
        copy.start()
    for k in range(count):
        inward[k].wait()
        outward[k].start()
    for copy in outward:
        copy.wait()


def anchor_kernel(*refs):
    pass


def slot_of(core_type, index):
    return (index % 2) * 2 + index // 2 if core_type == 0 else index


def fetch_pieces(sources, buffer, semaphores):
    def copies(own, other):
        for core_type, arrays in ((0, own), (1, other)):
            for index in range(4):
                slot = slot_of(core_type, index)
                yield pltpu.make_async_copy(
                    arrays[index],
                    buffer.at[core_type, slot],
                    semaphores.at[core_type, slot],
                )

    @pl.when(my_core() == 0)
    def _():
        for copy in copies(sources[:4], sources[4:]):
            copy.start()

    @pl.when(my_core() == 1)
    def _():
        for copy in copies(sources[4:], sources[:4]):
            copy.start()


def wait_piece(sources, buffer, semaphores, core_type, slot):
    pltpu.make_async_copy(
        sources[0], buffer.at[core_type, slot], semaphores.at[core_type, slot]
    ).wait()


def spread_sets(owners, first, sets, read, write):
    for k in range(len(owners)):

        @pl.when(first[k])
        def _(k=k):
            write(owners[k], False, read(k))

        @pl.when(jnp.logical_not(first[k]))
        def _(k=k):
            write(owners[k], True, read(k))

    if not isinstance(owners[0], int):
        for g in range(sets):
            there = owners[0] == g
            for owner in owners[1:]:
                there = there | (owner == g)

            @pl.when(jnp.logical_not(there))
            def _(g=g):
                write(g, False, [jnp.zeros_like(value) for value in read(0)])


def finish_step(layout, small, outs, buffer, rel, owners, first, sets):
    channels = buffer.shape[4]
    size = channels // 4
    places = []
    for core_type, blocks in enumerate(layout):
        for at, place in enumerate(blocks):
            places.append((core_type, slice(at * size, (at + 1) * size), place))

    def read(k):
        return [buffer[t, rel, k, rows, :].astype(F32) for t, rows, _ in places]

    def write(g, add, values):
        for (_, _, place), value in zip(places, values):
            if place[1] is None:
                index = (g, place[2], 0)
            else:
                index = (g, slice(None), slice(place[1] * channels, (place[1] + 1) * channels))
            ref = outs[place[0]]
            ref[index] = ref[index] + value if add else value

    spread_sets(owners, first, sets, read, write)
    start = len(layout[0]) * size
    q = rel ^ my_place()
    for number, place in enumerate(small):
        if place is None:
            continue

        @pl.when(q == number % 4)
        def _(number=number, place=place):
            out, column = place
            cols = slice(column, column + channels)

            def read(k):
                rows = buffer[number // 4, rel, k, start : start + 16, :]
                return [rows.astype(F32)[0:1]]

            def write(g, add, values):
                index = (pl.ds(g, 1), cols)
                outs[out][index] = outs[out][index] + values[0] if add else values[0]

            spread_sets(owners, first, sets, read, write)


def finish_up_kernel(layout, small, group_index, *refs):
    sources, outs, buffer, semaphores = refs[:8], refs[8:-2], refs[-2], refs[-1]
    step = pl.program_id(0)
    sets, count = outs[0].shape[0], buffer.shape[2]
    owners, first = entry_sets(group_index, count, sets)

    @pl.when(step == 0)
    def _():
        fetch_pieces(sources, buffer, semaphores)

    for core_type in range(2):
        wait_piece(sources, buffer, semaphores, core_type, step)
    finish_step(layout, small, outs, buffer, step, owners, first, sets)


def by_type(sources, number, act):
    own, other = sources[:number], sources[number : 2 * number]

    @pl.when(my_core() == 0)
    def _():
        act((own, other))

    @pl.when(my_core() == 1)
    def _():
        act((other, own))


def row_copies(core_type, index, stage, in_any, out_any, semaphores):
    channels = out_any.shape[2]
    size = channels // 4
    q = slot_of(core_type, index) ^ my_place()
    rows = pl.ds(pl.multiple_of(q * size, size), size)
    if core_type == 0:
        targets = [in_any.at[:, rows, 0:channels], in_any.at[:, rows, channels : 2 * channels]]
    else:
        targets = [in_any.at[:, rows, 2 * channels :], out_any.at[:, rows, :]]
    return [
        pltpu.make_async_copy(stage.at[k], target, semaphores.at[k])
        for k, target in enumerate(targets)
    ]


def finish_rows(piece, stage, owners, first, sets):
    size = stage.shape[2]

    def read(k):
        return [piece[k, n * size : (n + 1) * size, :].astype(F32) for n in range(2)]

    def write(g, add, values):
        for n, value in enumerate(values):
            stage[n, g] = stage[n, g] + value if add else value

    spread_sets(owners, first, sets, read, write)


def finish_near_kernel(group_index, *refs):
    sources, (in_any, out_any), (buffer, stage, arrivals, leavings) = refs[:4], refs[4:6], refs[6:]
    sets, count = stage.shape[3], buffer.shape[2]
    owners, first = entry_sets(group_index, count, sets)
    rows = buffer.shape[3]
    items = [(t, n) for n in range(2) for t in range(2)]

    def start(lists):
        for t, n in items:
            pltpu.make_async_copy(
                lists[t][n].at[:, :rows], buffer.at[t, n], arrivals.at[t, n]
            ).start()

    by_type(sources, 2, start)
    copies = []
    for t, n in items:
        pltpu.make_async_copy(
            sources[0].at[:, :rows], buffer.at[t, n], arrivals.at[t, n]
        ).wait()
        finish_rows(buffer.at[t, n], stage.at[t, n], owners, first, sets)
        copies += row_copies(t, n, stage.at[t, n], in_any, out_any, leavings.at[t, n])
        for copy in copies[-2:]:
            copy.start()
    for copy in copies:
        copy.wait()


def finish_low_kernel(small, group_index, window_types, *refs):
    sources, outs = refs[:8], refs[10:-7]
    buffer, tables, stage, held, arrivals, table_arrivals, leavings = refs[-7:]
    in_any, out_any, out = outs[0], outs[1], outs[-1]
    step = pl.program_id(0)
    sets, count, channels = stage.shape[3], buffer.shape[2], buffer.shape[4]
    heads, kinds, positions = out.shape[1:]
    owners, first = entry_sets(group_index, count, sets)
    top = buffer.shape[3] - tables.shape[3]
    items = [(t, n) for n in range(2) for t in range(2)]

    @pl.when(step == 0)
    def _():
        def start(lists):
            for t, n in items:
                pltpu.make_async_copy(
                    lists[t][2 + n], buffer.at[t, n], arrivals.at[t, n]
                ).start()
            for t, n in items:
                pltpu.make_async_copy(
                    lists[t][n].at[:, top:], tables.at[t, n], table_arrivals.at[t, n]
                ).start()

        by_type(sources, 4, start)
        for t, n in items:
            pltpu.make_async_copy(sources[0], buffer.at[t, n], arrivals.at[t, n]).wait()
            finish_rows(buffer.at[t, n], stage.at[t, n], owners, first, sets)
            for copy in row_copies(t, 2 + n, stage.at[t, n], in_any, out_any, leavings.at[t, n]):
                copy.start()
        for t, n in items:
            pltpu.make_async_copy(
                sources[0].at[:, top:], tables.at[t, n], table_arrivals.at[t, n]
            ).wait()
        for ref in outs[2:-1]:
            ref[...] = jnp.zeros_like(ref)
        bands = held.shape[1] // channels
        for k in range(count):
            sums = jnp.zeros((16, channels), F32)
            for t in range(2):
                for index in range(4):
                    at = ((k * 2 + t) * 4 + slot_of(t, index)) * 16

                    def rows(band, index=index, t=t, k=k):
                        if index < 2:
                            return tables[t, index, k, 16 * band : 16 * band + 16]
                        return buffer[
                            t, index - 2, k, top + 16 * band : top + 16 * band + 16
                        ]

                    for band in range(bands):
                        held[at : at + 16, band * channels : (band + 1) * channels] = rows(band)
                    sums = sums + rows(bands).astype(F32)
            for n, (number, column) in enumerate(small):
                index = (pl.ds(owners[k], 1), slice(column, column + channels))
                outs[number][index] = outs[number][index] + sums[n : n + 1]

    shape = (heads * kinds, count * 128)
    row = lax.broadcasted_iota(jnp.int32, shape, 0)
    col = lax.broadcasted_iota(jnp.int32, shape, 1)
    kind_of = jnp.zeros(shape, jnp.int32)
    for t in range(2):
        for r in range(4):
            q = r ^ my_place()
            kind = window_types[q // 2 * 4 + t * 2 + q % 2]
            kind_of = jnp.where(col // 16 % 8 == t * 4 + r, kind, kind_of)
    set_of = jnp.zeros(shape, jnp.int32)
    for k in range(count):
        set_of = jnp.where(col // 128 == k, owners[k], set_of)
    hit = (row // kinds == col % 16) & (row % kinds == kind_of) & (set_of == step)
    value = dot(jnp.where(hit, 1.0, 0.0).astype(BF), held[...])
    out[0] = value[:, :positions].reshape(out.shape[1:])

    @pl.when(step == sets - 1)
    def _():
        for t, n in items:
            for copy in row_copies(t, 2 + n, stage.at[t, n], in_any, out_any, leavings.at[t, n]):
                copy.wait()


def whole(array_or_shape):
    shape = getattr(array_or_shape, "shape", array_or_shape)
    return pl.BlockSpec(shape, lambda i, *_: (0,) * len(shape))


def own_member(array):
    def index(i, group_index, *_):
        return (my_set(group_index),) + (0,) * (array.ndim - 1)

    return pl.BlockSpec((None,) + array.shape[1:], index)


def call(
    kernel, scalars, inputs, out_shapes, *, in_specs=None, out_specs=None, scratch=(), grid=(1,),
    after=(), cost=1.0, aliases=None,
):
    in_specs = [whole(v) for v in inputs] if in_specs is None else in_specs
    out_specs = jax.tree.map(whole, out_shapes) if out_specs is None else out_specs
    count = len(scalars) + len(inputs)
    body = kernel
    if after:

        def body(*refs):
            kernel(*refs[:count], *refs[count + len(after) :])

    after = list(after)

    return pl.pallas_call(
        body,
        grid_spec=pltpu.PrefetchScalarGridSpec(
            num_scalar_prefetch=len(scalars),
            grid=grid,
            in_specs=list(in_specs) + [pl.BlockSpec(memory_space=pl.ANY)] * len(after),
            out_specs=out_specs,
            scratch_shapes=list(scratch),
        ),
        out_shape=out_shapes,
        input_output_aliases=aliases or {},
        compiler_params=pltpu.CompilerParams(vmem_limit_bytes=64 * 1024 * 1024),
        cost_estimate=pl.CostEstimate(
            flops=int(cost * 1.1e9), bytes_accessed=10**3, transcendentals=0
        ),
    )(*scalars, *inputs, *after)


def like(shape, kind=BF):
    return jax.ShapeDtypeStruct(tuple(shape), kind)


def swap(value, axis, distance):
    pairs = [(i, i ^ distance) for i in range(lax.axis_size(axis))]
    return lax.ppermute(value, axis, pairs)


def move_both(value, step, cross):
    lev, lat = lax.axis_size("lev"), lax.axis_size("lat")
    pairs = [
        (a * lat + b, step(a, lev) * lat + (b ^ cross)) for a in range(lev) for b in range(lat)
    ]
    return lax.ppermute(value, ("lev", "lat"), pairs)


def below(a, size):
    return (a - 1) % size


def above(a, size):
    return (a + 1) % size


def over_x(a, size):
    return a ^ 2


def quadrants(fields, cotangent):
    rows = WH // 2 * fields.shape[2]
    shape = like((2, rows, fields.shape[3]))
    own, lev, lat, both = call(split_kernel, [], [fields, cotangent], [shape] * 4, cost=1.0)
    return [own, move_both(lev, below, 0), swap(lat, "lat", 1), move_both(both, below, 1)]


def returned(parts):
    own, lev, lat, both = parts
    return [own, move_both(lev, above, 0), swap(lat, "lat", 1), move_both(both, above, 1)]


def reduce_cores(keep, arrived, after=(), cost=0.1):
    shape = like(keep.shape[1:])
    return call(first_sum_kernel, [], [keep] + arrived, [shape] * 4, after=after, cost=cost)


def move_chips(parts):
    own, along_y, along_x, along_both = parts
    return [own, swap(along_y, "lat", 1), swap(along_x, "lev", 2), move_both(along_both, over_x, 1)]


def reduce_chips(parts, tables=(), after=()):
    rows, channels = parts[0].shape
    rows += sum(16 * (table.shape[1] // channels) for table in tables)
    shape = like((rows, channels))
    return call(second_sum_kernel, [], parts + list(tables), shape, after=after, cost=0.1)


def round_samples(share, group_index, sets, after=(), cost=0.1):
    lat = lax.axis_size("lat")
    samples = lat // WROWS
    if samples > sets:
        groups = [[s * WROWS + b for s in range(samples)] for b in range(WROWS)]
        hot = (jnp.arange(sets) == group_index[lax.axis_index("lat") // WROWS]).astype(F32)
        total = hot[:, None, None] * share.astype(F32)[None]
        total = lax.psum(total, "lat", axis_index_groups=groups).astype(BF)
        entries = [total[k] for k in range(sets)]
    else:
        entries = [share]
        for k in range(1, samples):
            pairs = [(i, (i + WROWS * k) % lat) for i in range(lat)]
            entries.append(lax.ppermute(share, "lat", pairs))
    shape = like((len(entries),) + share.shape)
    anywhere = pl.BlockSpec(memory_space=pl.ANY)
    return call(
        stack_kernel,
        [group_index],
        entries,
        shape,
        in_specs=[anywhere] * len(entries),
        out_specs=anywhere,
        scratch=[pltpu.VMEM(shape.shape, BF)] + [pltpu.SemaphoreType.DMA((len(entries),))] * 2,
        after=after,
        cost=cost,
    )


def hop(value, turn):
    lev, lat = lax.axis_size("lev"), lax.axis_size("lat")
    pairs = [
        (a * lat + b, (a ^ 2) * lat + b if a % 2 == turn else a * lat + (b ^ 1))
        for a in range(lev)
        for b in range(lat)
    ]
    return lax.ppermute(value, ("lev", "lat"), pairs)


def anchored(value, after, cost=0.1):
    anywhere = pl.BlockSpec(memory_space=pl.ANY)
    return call(
        anchor_kernel, [], [value], like(value.shape), in_specs=[anywhere], out_specs=anywhere,
        after=after, aliases={0: 0}, cost=cost,
    )


def body(
    fields,
    group_index,
    window_types,
    window_masks,
    first_gain,
    first_offset,
    input_weight,
    input_bias,
    output_weight,
    output_bias,
    second_gain,
    second_offset,
    expand_weight,
    expand_bias,
    reduce_weight,
    reduce_bias,
    position_bias,
    cotangent,
):
    columns = fields.shape[2]
    channels = fields.shape[3]
    sets, kinds, heads, positions = position_bias.shape
    groups = heads // GROUP
    cells = WZ * WH
    tokens = columns * cells
    rows = tokens // 4
    quarter = channels // 4
    lanes = channels // groups
    to_win = jnp.asarray(window_order(columns), BF)
    to_rows = jnp.asarray(window_order(columns).T, BF)
    own_lanes = jnp.asarray(head_lanes(lanes), BF)
    cols_map = jnp.asarray(column_maps(), BF)
    rows_map = jnp.asarray(token_rows(), BF)
    rows_back = jnp.asarray(token_rows().T, BF)
    places = jnp.asarray(head_places(), BF)
    fold = jnp.asarray(fold_map(), BF)

    arrived = quadrants(fields, cotangent)

    by_head = position_bias.transpose(0, 2, 1, 3)
    table = call(
        select_kernel,
        [group_index, window_types],
        [by_head],
        like((heads, positions)),
        in_specs=[own_member(by_head)],
        cost=1.0,
    )
    table = table.reshape(heads, WZ, WZ, WH, WH, SPAN).transpose(0, 2, 4, 1, 3, 5)
    table = table.reshape(heads, cells, cells * SPAN)
    table = jnp.pad(table, ((0, 0), (0, 16 - cells), (0, 0))).reshape(heads * 16, cells * SPAN)
    bias_map = call(
        bias_kernel,
        [],
        [window_masks, table, cols_map, rows_map, places, fold],
        like((groups, TOKENS, PADDED), F32),
        scratch=[pltpu.VMEM((heads, 16 * WW, TOKENS), BF)],
        cost=5.0,
    )

    hidden_units = expand_weight.shape[2]
    assert hidden_units == 4 * channels
    up_rows = 4 * quarter + 16
    low_rows = 2 * quarter
    inputs = (
        arrived
        + [to_win, to_rows, bias_map, own_lanes, first_gain, first_offset]
        + [input_weight, input_bias, output_weight, output_bias, second_gain, second_offset]
        + [expand_weight, expand_bias, reduce_weight, reduce_bias]
    )
    weights = {id(v) for v in (input_weight, output_weight, expand_weight, reduce_weight)}
    quadrant = like((rows, channels))
    anywhere = pl.BlockSpec(memory_space=pl.ANY)
    y0, y1, y2, y3, xw, triple, att, grad_hidden, keep, send = call(
        forward_kernel,
        [group_index],
        inputs,
        [quadrant] * 4
        + [
            like((tokens, channels)),
            like((tokens, 3 * channels)),
            like((tokens, channels)),
            like((tokens, channels), F32),
            like((4, up_rows, channels)),
            like((4, up_rows, channels)),
        ],
        in_specs=[
            anywhere if v is expand_weight or v is reduce_weight
            else own_member(v) if id(v) in weights
            else whole(v)
            for v in inputs
        ],
        out_specs=[whole(quadrant)] * 4
        + [anywhere] * 3
        + [whole((tokens, channels))]
        + [whole((4, up_rows, channels))] * 2,
        scratch=[
            pltpu.VMEM((tokens, channels), BF),
            pltpu.VMEM((channels, tokens), BF),
            pltpu.VMEM((tokens, channels), BF),
            pltpu.VMEM((tokens, channels), F32),
            pltpu.VMEM((tokens, channels), F32),
            pltpu.VMEM((8, channels), F32),
            pltpu.VMEM((channels, hidden_units), BF),
            pltpu.VMEM((hidden_units, channels), BF),
            pltpu.VMEM((tokens, channels), BF),
            pltpu.VMEM((tokens, 3 * channels), BF),
            pltpu.VMEM((tokens, channels), BF),
            pltpu.SemaphoreType.DMA((5,)),
        ],
        cost=33.0,
    )

    up_parts = reduce_cores(keep, [swap(send, "lev", 1)], cost=5.0)
    output_parts = returned([y0, y1, y2, y3])
    inputs = [triple, grad_hidden, bias_map, own_lanes, output_weight]
    grad_triple, score_sums = call(
        scores_back_kernel,
        [group_index],
        inputs,
        [like((tokens, 3 * channels)), like((groups, TOKENS, PADDED), F32)],
        in_specs=[own_member(v) if id(v) in weights else whole(v) for v in inputs],
        scratch=[pltpu.VMEM((tokens, channels), BF)],
        after=[up_parts[3]] + output_parts[1:3],
        cost=20.0,
    )
    up_share = reduce_chips(move_chips(up_parts), after=[grad_triple, output_parts[3]])

    inputs = [xw, att, grad_hidden, grad_triple, to_rows, first_gain, first_offset, input_weight]
    d0, d1, d2, d3, low_grads, low_small = call(
        input_back_kernel,
        [group_index],
        inputs,
        [quadrant] * 4 + [like((4, channels, channels)), like((16, channels))],
        in_specs=[own_member(v) if id(v) in weights else whole(v) for v in inputs],
        scratch=[pltpu.VMEM((16, channels), F32)],
        after=[up_share],
        cost=8.0,
    )
    low_keep, *low_send = call(
        spread_kernel,
        [],
        [low_grads],
        [like((4, low_rows, channels))] + [like((4, quarter, channels))] * 2,
        cost=0.1,
    )
    low_arrived = [swap(send, "lev", 1) for send in low_send]
    up_stack = round_samples(up_share, group_index, sets, after=low_arrived)
    low_parts = reduce_cores(low_keep, low_arrived, after=[up_stack])

    up_hop = hop(up_stack, 0)
    low_sums = move_chips(low_parts)
    output = call(assemble_kernel, [], output_parts, like(fields.shape), cost=1.0)
    table_grad = call(
        fold_kernel,
        [],
        [score_sums, cols_map, rows_back, places],
        like((heads * 16, cells * SPAN)),
        scratch=[pltpu.VMEM((2, WW, heads * 16, TOKENS), BF)],
        after=[up_stack, output],
        cost=7.0,
    )
    table_grad = table_grad.reshape(heads, 16, cells * SPAN)[:, :cells]
    table_grad = table_grad.reshape(heads, WZ, WH, WZ, WH, SPAN).transpose(0, 3, 1, 4, 2, 5)
    wide = -(-positions // channels) * channels
    table_grad = jnp.pad(
        table_grad.reshape(heads, positions), ((0, 16 - heads), (0, wide - positions))
    )
    low_share = reduce_chips(low_sums, [table_grad, low_small], after=[up_hop])

    up_stack = anchored(up_stack, [low_share])
    up_own = [up_stack, up_hop, hop(up_stack, 1), hop(up_hop, 1)]
    low_stack = round_samples(low_share, group_index, sets, after=up_own[2:], cost=10.0)
    up_other = [swap(v, "lev", 1) for v in up_own]
    low_hop = hop(low_stack, 0)
    low_stack = anchored(low_stack, [low_hop], cost=12.0)
    low_own = [low_stack, low_hop, hop(low_stack, 1), hop(low_hop, 1)]

    count = low_stack.shape[0]
    up_shapes = [
        like((sets, channels, hidden_units), F32),
        like((sets, 4, 4, quarter, channels), F32),
        like((sets, hidden_units), F32),
    ] + [like((sets, channels), F32)] * 3
    up_grad, down_grad, bup_grad, bdn_grad, g2_grad, o2_grad = call(
        functools.partial(
            finish_up_kernel,
            [[(0, k) for k in range(4)], [(1, None, k) for k in range(4)]],
            [(2, k * channels) for k in range(4)] + [(3, 0), (4, 0), (5, 0)],
        ),
        [group_index],
        up_own + up_other,
        up_shapes,
        in_specs=[anywhere] * 8,
        out_specs=[
            pl.BlockSpec((sets, quarter, hidden_units), lambda r, g: (0, r ^ my_place(), 0)),
            pl.BlockSpec(
                (sets, 4, 1, quarter, channels), lambda r, g: (0, 0, r ^ my_place(), 0, 0)
            ),
        ]
        + [whole(v) for v in up_shapes[2:]],
        scratch=[
            pltpu.VMEM((2, 4, count, up_rows, channels), BF),
            pltpu.SemaphoreType.DMA((2, 4)),
        ],
        grid=(4,),
        cost=11.0,
    )
    low_other = [swap(v, "lev", 1) for v in low_own[:2]]
    block_shapes = [
        like((sets, channels, 3 * channels), F32),
        like((sets, channels, channels), F32),
    ]
    near = call(
        finish_near_kernel,
        [group_index],
        low_own[:2] + low_other,
        block_shapes,
        in_specs=[anywhere] * 4,
        out_specs=[anywhere] * 2,
        scratch=[
            pltpu.VMEM((2, 2, count, low_rows, channels), BF),
            pltpu.VMEM((2, 2, 2, sets, quarter, channels), F32),
            pltpu.SemaphoreType.DMA((2, 2)),
            pltpu.SemaphoreType.DMA((2, 2, 2)),
        ],
        after=[up_grad],
        cost=5.0,
    )
    low_own[3] = anchored(low_own[3], [near[0]])
    low_other += [swap(v, "lev", 1) for v in low_own[2:]]
    small_shapes = [like((sets, w), F32) for w in (channels, 2 * channels, channels, channels)]
    all_rows = low_stack.shape[1]
    in_grad, out_grad, bout_grad, bin_grad, g1_grad, o1_grad, position_grad = call(
        functools.partial(
            finish_low_kernel, [(2, 0), (3, 0), (3, channels), (4, 0), (5, 0)]
        ),
        [group_index, window_types],
        low_own + low_other + list(near),
        block_shapes + small_shapes + [like((sets, heads, kinds, positions), F32)],
        in_specs=[anywhere] * 10,
        out_specs=[anywhere] * 2
        + [whole(v) for v in small_shapes]
        + [pl.BlockSpec((1, heads, kinds, positions), lambda g, *_: (g, 0, 0, 0))],
        scratch=[
            pltpu.VMEM((2, 2, count, all_rows, channels), BF),
            pltpu.VMEM((2, 2, count, all_rows - low_rows, channels), BF),
            pltpu.VMEM((2, 2, 2, sets, quarter, channels), F32),
            pltpu.VMEM((count * 128, wide), BF),
            pltpu.SemaphoreType.DMA((2, 2)),
            pltpu.SemaphoreType.DMA((2, 2)),
            pltpu.SemaphoreType.DMA((2, 2, 2)),
        ],
        grid=(sets,),
        aliases={10: 0, 11: 1},
        cost=8.0,
    )

    input_grad = call(
        assemble_kernel,
        [],
        returned([d0, d1, d2, d3]),
        like(fields.shape),
        after=[position_grad],
        cost=1.0,
    )
    down_grad = down_grad.reshape(sets, -1, channels)
    position_grad = position_grad.transpose(0, 2, 1, 3)
    return (
        output,
        input_grad,
        g1_grad,
        o1_grad,
        in_grad,
        bin_grad,
        out_grad,
        bout_grad,
        g2_grad,
        o2_grad,
        up_grad,
        bup_grad,
        down_grad,
        bdn_grad,
        position_grad,
    )


def solution(mesh):
    slab = P("lat", "lev", None, None)
    return jax.shard_map(
        body,
        mesh=mesh,
        in_specs=(slab,) + (P(),) * 16 + (slab,),
        out_specs=(slab, slab) + (P(),) * 13,
        check_vma=False,
    )
```

```python
import functools

import jax
import jax.numpy as jnp
import numpy as np
from jax import lax
from jax.experimental import pallas as pl
from jax.experimental.pallas import tpu as pltpu
from jax.sharding import PartitionSpec as P

WZ = 2
WH = 6
WW = 12
WROWS = 2
TOKENS = WZ * WH * WW
GROUP = 4
PADDED = 640
SPAN = 2 * WW - 1
MASKED = -1e30
LOG2E = 1.4426950408889634
BF = jnp.bfloat16
F32 = jnp.float32


def dot(a, b):
    return lax.dot_general(a, b, (((1,), (0,)), ((), ())), preferred_element_type=F32)


def dot_nt(a, b):
    return lax.dot_general(a, b, (((1,), (1,)), ((), ())), preferred_element_type=F32)


def dot_tn(a, b):
    return lax.dot_general(a, b, (((0,), (0,)), ((), ())), preferred_element_type=F32)


def one_hot(index, size):
    return (np.asarray(index)[:, None] == np.arange(size)[None, :]).astype(np.float32)


def window_order(columns):
    windows = columns // WW
    n, h, w = np.meshgrid(np.arange(windows), np.arange(WH), np.arange(WW), indexing="ij")
    source = h * columns + (n * WW + w + WW // 2) % columns
    return one_hot(source.reshape(-1), WH * columns)


def column_maps():
    cells = WZ * WH
    out = np.zeros((WW, cells, SPAN, cells, WW), np.float32)
    for wj in range(WW):
        for wi in range(WW):
            for c in range(cells):
                out[wj, c, wi - wj + WW - 1, c, wi] = 1.0
    return out.reshape(WW, cells * SPAN, cells * WW)


def token_rows():
    j = np.arange(TOKENS)
    return one_hot((j % WW) * 16 + j // WW, WW * 16)


def head_places():
    return np.stack([one_hot(h * TOKENS + np.arange(TOKENS), PADDED) for h in range(GROUP)])


def fold_map():
    return sum(head_places())


def head_lanes(lanes):
    return np.repeat(np.eye(GROUP, dtype=np.float32), lanes // GROUP, axis=1)


def select_kernel(group_index, window_types, tables_ref, out_ref):
    heads, kinds, positions = tables_ref.shape
    place = lax.axis_index("lev") * WROWS + lax.axis_index("lat") % WROWS
    kind = window_types[place]
    shape = (heads, heads * kinds)
    row = lax.broadcasted_iota(jnp.int32, shape, 0)
    col = lax.broadcasted_iota(jnp.int32, shape, 1)
    pick = jnp.where(col == row * kinds + kind, 1.0, 0.0).astype(BF)
    tables = tables_ref[...].astype(F32).reshape(heads * kinds, positions).astype(BF)
    out_ref[...] = dot(pick, tables).astype(BF)


def bias_kernel(masks_ref, table_ref, cols_ref, rows_ref, places_ref, fold_ref, out_ref, held):
    heads = held.shape[0]
    for wj in range(WW):
        part = dot(table_ref[...], cols_ref[wj]).astype(BF)
        for h in range(heads):
            held[h, 16 * wj : 16 * wj + 16, :] = part[16 * h : 16 * h + 16]
    half = lax.axis_index("lat") % WROWS
    labels = masks_ref[lax.axis_index("lev"), pl.ds(half, 1), :].astype(F32)
    top = lax.broadcasted_iota(jnp.int32, (8, TOKENS), 0) == 0
    labels = jnp.where(top, jnp.broadcast_to(labels, (8, TOKENS)), 0.0)
    across = dot(jnp.ones((TOKENS, 8), BF), dot(labels.astype(BF), fold_ref[...]).astype(BF))
    down = dot_tn(labels.astype(BF), jnp.ones((8, PADDED), BF))
    same = jnp.abs(across - down) < 0.5
    for g in range(heads // GROUP):
        total = dot(held[g * GROUP], places_ref[0])
        for h in range(1, GROUP):
            total = total + dot(held[g * GROUP + h], places_ref[h])
        out_ref[g] = jnp.where(same, dot(rows_ref[...], total.astype(BF)), MASKED) * LOG2E


def fold_kernel(sums_ref, cols_ref, rows_ref, places_ref, out_ref, held):
    groups = sums_ref.shape[0]
    for g in range(groups):
        value = sums_ref[g]
        high = value.astype(BF)
        low = (value - high.astype(F32)).astype(BF)
        for index, part in enumerate((high, low)):
            ordered = dot(rows_ref[...], part).astype(BF)
            for h in range(GROUP):
                block = dot_nt(ordered, places_ref[h]).astype(BF)
                spot = (g * GROUP + h) * 16
                for wj in range(WW):
                    held[index, wj, spot : spot + 16, :] = block[16 * wj : 16 * wj + 16]
    total = jnp.zeros(out_ref.shape, F32)
    for wj in range(WW):
        for index in range(2):
            total = total + dot_nt(held[index, wj], cols_ref[wj])
    out_ref[...] = total.astype(BF)


def norm_parts(values):
    centre = values - jnp.mean(values, axis=-1, keepdims=True)
    spread = jnp.mean(centre * centre, axis=-1, keepdims=True)
    root = lax.rsqrt(spread + 1e-05)
    return centre * root, root


def norm_back(grad, gain, xhat, root):
    u = grad * gain
    return (
        u - jnp.mean(u, axis=-1, keepdims=True) - xhat * jnp.mean(u * xhat, axis=-1, keepdims=True)
    ) * root


def stacked_heads(block, lanes_ref):
    pieces = [block * lanes_ref[h : h + 1, :] for h in range(GROUP)]
    pieces.append(jnp.zeros((PADDED - GROUP * block.shape[0], block.shape[1]), block.dtype))
    return jnp.concatenate(pieces, axis=0)


def own_head(full):
    size = full.shape[0] // GROUP
    return jnp.concatenate(
        [
            full[h * size : (h + 1) * size, h * TOKENS : (h + 1) * TOKENS]
            for h in range(GROUP)
        ],
        axis=0,
    )


def softmax_t(keys, queries, bias, scale):
    scores = dot_nt(keys, queries) * (scale * LOG2E) + bias
    exponent = jnp.exp2(scores - jnp.max(scores, axis=0, keepdims=True))
    return exponent * (1.0 / jnp.sum(exponent, axis=0, keepdims=True))


def to_windows(level_map, levels):
    half = WH * WW
    parts = [dot(level_map, level) for level in levels]
    pieces = []
    for n in range(parts[0].shape[0] // half):
        for part in parts:
            pieces.append(part[n * half : (n + 1) * half])
    return jnp.concatenate(pieces, axis=0)


def to_levels(level_map, value):
    half = WH * WW
    count = value.shape[0] // (2 * half)
    quadrants = [None] * 4
    for z in range(WZ):
        level = [value[(2 * n + z) * half : (2 * n + z + 1) * half] for n in range(count)]
        level = dot(level_map, jnp.concatenate(level, axis=0).astype(BF))
        rows = level.shape[0] // 2
        for side in range(2):
            quadrants[side * WZ + z] = level[side * rows : (side + 1) * rows].astype(BF)
    return quadrants


def my_place():
    return (lax.axis_index("lev") // 2) * 2 + lax.axis_index("lat") % WROWS


def my_core():
    return lax.axis_index("lev") % 2


def place_slot(keep_out, send_outs, owner, rel, start, value):
    @pl.when(my_core() == owner)
    def _():
        keep_out[rel, start : start + value.shape[0]] = value

    @pl.when(my_core() != owner)
    def _():
        at = start
        for out in send_outs:
            if 0 <= at < out.shape[1]:
                out[rel, at : at + value.shape[0]] = value
            at -= out.shape[1]


def scatter_rows(keep_out, send_outs, owner, block, value):
    value = value.astype(BF)
    size = value.shape[0] // 4
    for q in range(4):
        piece = value[q * size : (q + 1) * size]
        place_slot(keep_out, send_outs, owner, q ^ my_place(), block * size, piece)


def scatter_small(keep_out, send_outs, small):
    start = keep_out.shape[1] - 16
    for n in range(8):
        row = jnp.broadcast_to(small[n : n + 1, :], (16, small.shape[1])).astype(BF)
        place_slot(keep_out, send_outs, n // 4, (n % 4) ^ my_place(), start, row)


def my_set(group_index):
    return group_index[lax.axis_index("lat") // WROWS]


def entry_sets(group_index, count, sets):
    samples = lax.axis_size("lat") // WROWS
    if samples > sets:
        return list(range(sets)), [True] * sets
    owners = [group_index[k] for k in range(count)]
    first = []
    for k in range(count):
        fresh = jnp.bool_(True)
        for j in range(k):
            fresh = fresh & (owners[j] != owners[k])
        first.append(fresh)
    return owners, first


def param_row(ref, group):
    return ref[pl.ds(group, 1), :]


def forward_kernel(
    group_index, f0, f1, f2, f3, to_win, to_rows, bias_ref, lanes_ref,
    g1_ref, o1_ref, win_ref, bin_ref, wout_ref, bout_ref, g2_ref, o2_ref,
    wups_ref, bup_ref, wdns_ref, bdn_ref,
    y0, y1, y2, y3, xw_any, triple_any, att_any, gh_out, keep_out, send_out,
    n2_s, n2t_s, cot_s, acc_s, back_s, small_out,
    wup_ref, wdn_ref, xw_out, triple_out, att_out, semaphores,
):
    gid = my_set(group_index)
    tokens, channels = xw_out.shape
    weights = [
        pltpu.make_async_copy(source.at[gid], target, semaphores.at[k])
        for k, (source, target) in enumerate(((wups_ref, wup_ref), (wdns_ref, wdn_ref)))
    ]
    for copy in weights:
        copy.start()
    results = [
        pltpu.make_async_copy(source, target, semaphores.at[2 + k])
        for k, (source, target) in enumerate(
            ((xw_out, xw_any), (triple_out, triple_any), (att_out, att_any))
        )
    ]
    lanes = lanes_ref.shape[1]
    scale = (lanes // GROUP) ** -0.5

    def gathered(which):
        levels = [
            jnp.concatenate([low[which].astype(F32), high[which].astype(F32)], axis=0).astype(BF)
            for low, high in ((f0, f2), (f1, f3))
        ]
        return to_windows(to_win[...], levels)

    x = gathered(0)
    xw_out[...] = x.astype(BF)
    cot_s[...] = gathered(1).astype(BF)
    xhat, _ = norm_parts(x)
    normed = (xhat * param_row(g1_ref, gid) + param_row(o1_ref, gid)).astype(BF)
    bias_row = param_row(bin_ref, gid)
    bias_row = jnp.concatenate(
        [bias_row[:, :channels], jnp.zeros((1, channels), F32), bias_row[:, channels:]], axis=1
    )
    triple_out[...] = (dot(normed, win_ref[...]) + bias_row).astype(BF)
    results[0].start()
    results[1].start()

    def window(n, carry):
        rows = pl.ds(pl.multiple_of(n * TOKENS, 16), TOKENS)
        for g in range(channels // lanes):
            lo = g * lanes
            queries = stacked_heads(triple_out[rows, lo : lo + lanes], lanes_ref)
            keys = triple_out[rows, channels + lo : channels + lo + lanes]
            values = triple_out[rows, 2 * channels + lo : 2 * channels + lo + lanes]
            probs = softmax_t(keys, queries, bias_ref[g], scale).astype(BF)
            full = dot_tn(values, probs)
            att_out[rows, lo : lo + lanes] = own_head(full).T.astype(BF)
        return carry

    lax.fori_loop(0, tokens // TOKENS, window, 0, unroll=2)

    results[2].start()
    mixed = (dot(att_out[...], wout_ref[...]) + param_row(bout_ref, gid)).astype(BF)
    hidden = xw_out[...].astype(F32) + mixed.astype(F32)
    xhat2, root2 = norm_parts(hidden)
    gain2 = param_row(g2_ref, gid)
    n2 = (xhat2 * gain2 + param_row(o2_ref, gid)).astype(BF)
    n2_s[...] = n2
    n2t_s[...] = n2.T
    acc_s[...] = hidden + param_row(bdn_ref, gid)
    per = 4
    step = per * channels

    bup = param_row(bup_ref, gid)
    for copy in weights:
        copy.wait()
    for k in range(wup_ref.shape[1] // step):
        cols = slice(k * step, (k + 1) * step)
        up = wup_ref[:, cols]
        down = wdn_ref[cols, :]
        expanded = dot(n2_s[...], up) + bup[:, cols]
        cdf = 0.5 * (1.0 + lax.erf(expanded * (0.5**0.5)))
        active = (expanded * cdf).astype(BF)
        slope = cdf + expanded * (jnp.exp(-0.5 * expanded * expanded) * 0.3989422804014327)
        grad_expanded = (dot_nt(cot_s[...], down) * slope).astype(BF)
        acc_s[...] += dot(active, down)
        back = dot_nt(grad_expanded, up)
        back_s[...] = back if k == 0 else back_s[...] + back
        grad_up = dot(n2t_s[...], grad_expanded)
        grad_down = dot_tn(active, cot_s[...])
        sums = jnp.sum(grad_expanded.astype(F32), axis=0, keepdims=True)
        for j in range(per):
            part = slice(j * channels, (j + 1) * channels)
            scatter_rows(keep_out, [send_out], 0, per * k + j, grad_up[:, part])
            scatter_rows(keep_out, [send_out], 1, per * k + j, grad_down[part])
            small_out[per * k + j : per * k + j + 1, :] = sums[:, part]

    for ref, value in zip((y0, y1, y2, y3), to_levels(to_rows[...], acc_s[...])):
        ref[...] = value
    cot = cot_s[...].astype(F32)
    grad = back_s[...]
    small_out[4:5, :] = jnp.sum(cot, axis=0, keepdims=True)
    small_out[5:6, :] = jnp.sum(grad * xhat2, axis=0, keepdims=True)
    small_out[6:7, :] = jnp.sum(grad, axis=0, keepdims=True)
    small_out[7:8, :] = jnp.zeros((1, channels), F32)
    scatter_small(keep_out, [send_out], small_out[...])
    gh_out[...] = cot + norm_back(grad, gain2, xhat2, root2)
    for copy in results:
        copy.wait()


def scores_back_kernel(
    group_index, triple_ref, gh_ref, bias_ref, lanes_ref, wout_ref,
    gt_out, sums_out, ga_s,
):
    channels = gh_ref.shape[1]
    tokens = gh_ref.shape[0]
    lanes = lanes_ref.shape[1]
    scale = (lanes // GROUP) ** -0.5
    ga_s[...] = dot_nt(gh_ref[...].astype(BF), wout_ref[...]).astype(BF)
    sums_out[...] = jnp.zeros_like(sums_out)

    def window(n, carry):
        rows = pl.ds(pl.multiple_of(n * TOKENS, 16), TOKENS)
        for g in range(channels // lanes):
            lo = g * lanes
            queries = stacked_heads(triple_ref[rows, lo : lo + lanes], lanes_ref)
            keys = triple_ref[rows, channels + lo : channels + lo + lanes]
            values = triple_ref[rows, 2 * channels + lo : 2 * channels + lo + lanes]
            probs = softmax_t(keys, queries, bias_ref[g], scale)
            grad_att = stacked_heads(ga_s[rows, lo : lo + lanes], lanes_ref)
            grad_probs = dot_nt(values, grad_att)
            row_dot = jnp.sum(probs * grad_probs, axis=0, keepdims=True)
            grad_scores = (probs * (grad_probs - row_dot)).astype(BF)
            sums_out[g] += grad_scores.astype(F32)
            full = dot_tn(keys, grad_scores)
            gt_out[rows, lo : lo + lanes] = (own_head(full) * scale).T.astype(BF)
            gt_out[rows, channels + lo : channels + lo + lanes] = (
                dot(grad_scores, queries) * scale
            ).astype(BF)
            gt_out[rows, 2 * channels + lo : 2 * channels + lo + lanes] = dot(
                probs.astype(BF), grad_att
            ).astype(BF)
        return carry

    lax.fori_loop(0, tokens // TOKENS, window, 0, unroll=2)


def input_back_kernel(
    group_index, xw_ref, att_ref, gh_ref, gt_ref, to_rows, g1_ref, o1_ref, win_ref,
    d0, d1, d2, d3, low_out, band_out, small_out,
):
    gid = my_set(group_index)
    channels = xw_ref.shape[1]
    grad_mixed = gh_ref[...].astype(BF)
    low_out[3] = dot_tn(att_ref[...], grad_mixed).astype(BF)
    small_out[0:1, :] = jnp.sum(grad_mixed.astype(F32), axis=0, keepdims=True)
    xhat, root = norm_parts(xw_ref[...].astype(F32))
    gain = param_row(g1_ref, gid)
    normed = (xhat * gain + param_row(o1_ref, gid)).astype(BF)
    grad_in = dot(normed.T, gt_ref[...])
    grad = dot_nt(gt_ref[...], win_ref[...])
    for part in range(3):
        cols = slice(part * channels, (part + 1) * channels)
        low_out[part] = grad_in[:, cols].astype(BF)
        if part != 1:
            row = 1 + part // 2
            piece = gt_ref[:, cols].astype(F32)
            small_out[row : row + 1, :] = jnp.sum(piece, axis=0, keepdims=True)
    small_out[3:4, :] = jnp.sum(grad * xhat, axis=0, keepdims=True)
    small_out[4:5, :] = jnp.sum(grad, axis=0, keepdims=True)
    small_out[5:16, :] = jnp.zeros((11, channels), F32)
    band_out[...] = small_out[...].astype(BF)
    shifted = norm_back(grad, gain, xhat, root).astype(BF)
    parts = to_levels(to_rows[...], gh_ref[...] + shifted.astype(F32))
    for part, ref in zip(parts, (d0, d1, d2, d3)):
        ref[...] = part


def split_kernel(fields_ref, cot_ref, *outs):
    half = WH // 2
    for out, (row, level) in zip(outs, ((half, 1), (half, 0), (0, 1), (0, 0))):
        for k, ref in enumerate((fields_ref, cot_ref)):
            parts = [ref[row + h, level].astype(F32) for h in range(half)]
            out[k] = jnp.concatenate(parts, axis=0).astype(BF)


def assemble_kernel(own_ref, lev_ref, lat_ref, both_ref, out):
    half, columns = WH // 2, out.shape[2]
    for ref, row, level in (
        (own_ref, half, 1), (lev_ref, half, 0), (lat_ref, 0, 1), (both_ref, 0, 0)
    ):
        value = ref[...].astype(F32)
        for h in range(half):
            out[row + h, level] = value[h * columns : (h + 1) * columns].astype(BF)


def spread_kernel(low_ref, keep_out, *send_outs):
    for block in range(low_ref.shape[0]):
        scatter_rows(keep_out, send_outs, block // 2, block % 2, low_ref[block])


def first_sum_kernel(keep_ref, *refs):
    arrived, outs = refs[:-4], refs[-4:]
    at = 0
    for part in arrived:
        rows = slice(at, at + part.shape[1])
        at += part.shape[1]
        for k in range(4):
            total = keep_ref[k, rows].astype(F32) + part[k].astype(F32)
            outs[k][rows] = total.astype(BF)


def packed_rows(bands):
    return 16 * (-(-(bands + -(-bands // 2)) // 2))


def packed_units(table, channels):
    bands = table.shape[1] // channels
    parts = [table[:, n * channels : (n + 1) * channels].astype(F32) for n in range(bands)]
    units = [part[0:8] for part in parts]
    for n in range(0, bands, 2):
        unit = parts[n][8:16]
        if n + 1 < bands:
            unit = unit + pltpu.roll(parts[n + 1][8:16], 4, 0)
        units.append(unit)
    return units + [jnp.zeros_like(units[0])] * (len(units) % 2)


def unpacked_bands(rows, bands):
    units = []
    for n in range(packed_rows(bands) // 16):
        value = rows(n).astype(F32)
        units += [value[0:8], value[8:16]]
    out = []
    for n in range(bands):
        unit = units[bands + n // 2]
        rest = pltpu.roll(unit, 4, 0) if n % 2 else unit
        out.append(jnp.concatenate([units[n], rest], axis=0).astype(BF))
    return out


def second_sum_kernel(own_ref, y_ref, x_ref, xy_ref, *refs):
    tables, out = refs[:-1], refs[-1]
    rows, channels = own_ref.shape
    total = own_ref[...].astype(F32) + y_ref[...].astype(F32)
    out[:rows] = (total + x_ref[...].astype(F32) + xy_ref[...].astype(F32)).astype(BF)
    if tables:
        units = packed_units(tables[0], channels)
        for n in range(0, len(units), 2):
            at = rows + 8 * n
            out[at : at + 16] = jnp.concatenate(units[n : n + 2], axis=0).astype(BF)
        out[out.shape[0] - 16 :] = tables[1][...]


def stack_kernel(group_index, *refs):
    entries, out, held, arrivals, leavings = refs[:-4], refs[-4], refs[-3], refs[-2], refs[-1]
    count = len(entries)
    mine = lax.axis_index("lat") // WROWS
    samples = lax.axis_size("lat") // WROWS
    inward, outward = [], []
    for k in range(count):
        slot = (mine + samples - k) % samples if samples == count else k
        inward.append(pltpu.make_async_copy(entries[k], held.at[k], arrivals.at[k]))
        outward.append(pltpu.make_async_copy(held.at[k], out.at[slot], leavings.at[k]))
    for copy in inward:
        copy.start()
    for k in range(count):
        inward[k].wait()
        outward[k].start()
    for copy in outward:
        copy.wait()


def anchor_kernel(*refs):
    pass


def slot_of(core_type, index):
    return (index % 2) * 2 + index // 2 if core_type == 0 else index


def fetch_pieces(sources, buffer, semaphores):
    def copies(own, other):
        for core_type, arrays in ((0, own), (1, other)):
            for index in range(4):
                slot = slot_of(core_type, index)
                yield pltpu.make_async_copy(
                    arrays[index],
                    buffer.at[core_type, slot],
                    semaphores.at[core_type, slot],
                )

    @pl.when(my_core() == 0)
    def _():
        for copy in copies(sources[:4], sources[4:]):
            copy.start()

    @pl.when(my_core() == 1)
    def _():
        for copy in copies(sources[4:], sources[:4]):
            copy.start()


def wait_piece(sources, buffer, semaphores, core_type, slot):
    pltpu.make_async_copy(
        sources[0], buffer.at[core_type, slot], semaphores.at[core_type, slot]
    ).wait()


def spread_sets(owners, first, sets, read, write):
    for k in range(len(owners)):

        @pl.when(first[k])
        def _(k=k):
            write(owners[k], False, read(k))

        @pl.when(jnp.logical_not(first[k]))
        def _(k=k):
            write(owners[k], True, read(k))

    if not isinstance(owners[0], int):
        for g in range(sets):
            there = owners[0] == g
            for owner in owners[1:]:
                there = there | (owner == g)

            @pl.when(jnp.logical_not(there))
            def _(g=g):
                write(g, False, [jnp.zeros_like(value) for value in read(0)])


def finish_step(layout, small, outs, buffer, rel, owners, first, sets):
    channels = buffer.shape[4]
    size = channels // 4
    places = []
    for core_type, blocks in enumerate(layout):
        for at, place in enumerate(blocks):
            places.append((core_type, slice(at * size, (at + 1) * size), place))

    def read(k):
        return [buffer[t, rel, k, rows, :].astype(F32) for t, rows, _ in places]

    def write(g, add, values):
        for (_, _, place), value in zip(places, values):
            if place[1] is None:
                index = (g, place[2], 0)
            else:
                index = (g, slice(None), slice(place[1] * channels, (place[1] + 1) * channels))
            ref = outs[place[0]]
            ref[index] = ref[index] + value if add else value

    spread_sets(owners, first, sets, read, write)
    start = len(layout[0]) * size
    q = rel ^ my_place()
    for number, place in enumerate(small):
        if place is None:
            continue

        @pl.when(q == number % 4)
        def _(number=number, place=place):
            out, column = place
            cols = slice(column, column + channels)

            def read(k):
                rows = buffer[number // 4, rel, k, start : start + 16, :]
                return [rows.astype(F32)[0:1]]

            def write(g, add, values):
                index = (pl.ds(g, 1), cols)
                outs[out][index] = outs[out][index] + values[0] if add else values[0]

            spread_sets(owners, first, sets, read, write)


def finish_up_kernel(layout, small, group_index, *refs):
    sources, outs, buffer, semaphores = refs[:8], refs[8:-2], refs[-2], refs[-1]
    step = pl.program_id(0)
    sets, count = outs[0].shape[0], buffer.shape[2]
    owners, first = entry_sets(group_index, count, sets)

    @pl.when(step == 0)
    def _():
        fetch_pieces(sources, buffer, semaphores)

    for core_type in range(2):
        wait_piece(sources, buffer, semaphores, core_type, step)
    finish_step(layout, small, outs, buffer, step, owners, first, sets)


def by_type(sources, number, act):
    own, other = sources[:number], sources[number : 2 * number]

    @pl.when(my_core() == 0)
    def _():
        act((own, other))

    @pl.when(my_core() == 1)
    def _():
        act((other, own))


def row_copies(core_type, index, stage, in_any, out_any, semaphores):
    channels = out_any.shape[2]
    size = channels // 4
    q = slot_of(core_type, index) ^ my_place()
    rows = pl.ds(pl.multiple_of(q * size, size), size)
    if core_type == 0:
        targets = [in_any.at[:, rows, 0:channels], in_any.at[:, rows, channels : 2 * channels]]
    else:
        targets = [in_any.at[:, rows, 2 * channels :], out_any.at[:, rows, :]]
    return [
        pltpu.make_async_copy(stage.at[k], target, semaphores.at[k])
        for k, target in enumerate(targets)
    ]


def finish_rows(piece, stage, owners, first, sets):
    size = stage.shape[2]

    def read(k):
        return [piece[k, n * size : (n + 1) * size, :].astype(F32) for n in range(2)]

    def write(g, add, values):
        for n, value in enumerate(values):
            stage[n, g] = stage[n, g] + value if add else value

    spread_sets(owners, first, sets, read, write)


def finish_near_kernel(group_index, *refs):
    sources, (in_any, out_any), (buffer, stage, arrivals, leavings) = refs[:4], refs[4:6], refs[6:]
    sets, count = stage.shape[3], buffer.shape[2]
    owners, first = entry_sets(group_index, count, sets)
    rows = buffer.shape[3]
    items = [(t, n) for n in range(2) for t in range(2)]

    def start(lists):
        for t, n in items:
            pltpu.make_async_copy(
                lists[t][n].at[:, :rows], buffer.at[t, n], arrivals.at[t, n]
            ).start()

    by_type(sources, 2, start)
    copies = []
    for t, n in items:
        pltpu.make_async_copy(
            sources[0].at[:, :rows], buffer.at[t, n], arrivals.at[t, n]
        ).wait()
        finish_rows(buffer.at[t, n], stage.at[t, n], owners, first, sets)
        copies += row_copies(t, n, stage.at[t, n], in_any, out_any, leavings.at[t, n])
        for copy in copies[-2:]:
            copy.start()
    for copy in copies:
        copy.wait()


def finish_low_kernel(small, group_index, window_types, *refs):
    sources, outs = refs[:8], refs[10:-7]
    buffer, tables, stage, held, arrivals, table_arrivals, leavings = refs[-7:]
    in_any, out_any, out = outs[0], outs[1], outs[-1]
    step = pl.program_id(0)
    sets, count, channels = stage.shape[3], buffer.shape[2], buffer.shape[4]
    heads, kinds, positions = out.shape[1:]
    owners, first = entry_sets(group_index, count, sets)
    top = buffer.shape[3] - tables.shape[3]
    items = [(t, n) for n in range(2) for t in range(2)]

    @pl.when(step == 0)
    def _():
        def start(lists):
            for t, n in items:
                pltpu.make_async_copy(
                    lists[t][2 + n], buffer.at[t, n], arrivals.at[t, n]
                ).start()
            for t, n in items:
                pltpu.make_async_copy(
                    lists[t][n].at[:, top:], tables.at[t, n], table_arrivals.at[t, n]
                ).start()

        by_type(sources, 4, start)
        for t, n in items:
            pltpu.make_async_copy(sources[0], buffer.at[t, n], arrivals.at[t, n]).wait()
            finish_rows(buffer.at[t, n], stage.at[t, n], owners, first, sets)
            for copy in row_copies(t, 2 + n, stage.at[t, n], in_any, out_any, leavings.at[t, n]):
                copy.start()
        for t, n in items:
            pltpu.make_async_copy(
                sources[0].at[:, top:], tables.at[t, n], table_arrivals.at[t, n]
            ).wait()
        for ref in outs[2:-1]:
            ref[...] = jnp.zeros_like(ref)
        bands = held.shape[1] // channels
        for k in range(count):
            sums = jnp.zeros((16, channels), F32)
            for t in range(2):
                for index in range(4):
                    at = ((k * 2 + t) * 4 + slot_of(t, index)) * 16

                    def rows(band, index=index, t=t, k=k):
                        if index < 2:
                            return tables[t, index, k, 16 * band : 16 * band + 16]
                        return buffer[
                            t, index - 2, k, top + 16 * band : top + 16 * band + 16
                        ]

                    for band, value in enumerate(unpacked_bands(rows, bands)):
                        held[at : at + 16, band * channels : (band + 1) * channels] = value
                    sums = sums + rows(packed_rows(bands) // 16).astype(F32)
            for n, (number, column) in enumerate(small):
                index = (pl.ds(owners[k], 1), slice(column, column + channels))
                outs[number][index] = outs[number][index] + sums[n : n + 1]

    shape = (heads * kinds, count * 128)
    row = lax.broadcasted_iota(jnp.int32, shape, 0)
    col = lax.broadcasted_iota(jnp.int32, shape, 1)
    kind_of = jnp.zeros(shape, jnp.int32)
    for t in range(2):
        for r in range(4):
            q = r ^ my_place()
            kind = window_types[q // 2 * 4 + t * 2 + q % 2]
            kind_of = jnp.where(col // 16 % 8 == t * 4 + r, kind, kind_of)
    set_of = jnp.zeros(shape, jnp.int32)
    for k in range(count):
        set_of = jnp.where(col // 128 == k, owners[k], set_of)
    hit = (row // kinds == col % 16) & (row % kinds == kind_of) & (set_of == step)
    value = dot(jnp.where(hit, 1.0, 0.0).astype(BF), held[...])
    out[0] = value[:, :positions].reshape(out.shape[1:])

    @pl.when(step == sets - 1)
    def _():
        for t, n in items:
            for copy in row_copies(t, 2 + n, stage.at[t, n], in_any, out_any, leavings.at[t, n]):
                copy.wait()


def whole(array_or_shape):
    shape = getattr(array_or_shape, "shape", array_or_shape)
    return pl.BlockSpec(shape, lambda i, *_: (0,) * len(shape))


def own_member(array):
    def index(i, group_index, *_):
        return (my_set(group_index),) + (0,) * (array.ndim - 1)

    return pl.BlockSpec((None,) + array.shape[1:], index)


def call(
    kernel, scalars, inputs, out_shapes, *, in_specs=None, out_specs=None, scratch=(), grid=(1,),
    after=(), cost=1.0, aliases=None,
):
    in_specs = [whole(v) for v in inputs] if in_specs is None else in_specs
    out_specs = jax.tree.map(whole, out_shapes) if out_specs is None else out_specs
    count = len(scalars) + len(inputs)
    body = kernel
    if after:

        def body(*refs):
            kernel(*refs[:count], *refs[count + len(after) :])

    after = list(after)

    return pl.pallas_call(
        body,
        grid_spec=pltpu.PrefetchScalarGridSpec(
            num_scalar_prefetch=len(scalars),
            grid=grid,
            in_specs=list(in_specs) + [pl.BlockSpec(memory_space=pl.ANY)] * len(after),
            out_specs=out_specs,
            scratch_shapes=list(scratch),
        ),
        out_shape=out_shapes,
        input_output_aliases=aliases or {},
        compiler_params=pltpu.CompilerParams(vmem_limit_bytes=64 * 1024 * 1024),
        cost_estimate=pl.CostEstimate(
            flops=int(cost * 1.1e9), bytes_accessed=10**3, transcendentals=0
        ),
    )(*scalars, *inputs, *after)


def like(shape, kind=BF):
    return jax.ShapeDtypeStruct(tuple(shape), kind)


def swap(value, axis, distance):
    pairs = [(i, i ^ distance) for i in range(lax.axis_size(axis))]
    return lax.ppermute(value, axis, pairs)


def move_both(value, step, cross):
    lev, lat = lax.axis_size("lev"), lax.axis_size("lat")
    pairs = [
        (a * lat + b, step(a, lev) * lat + (b ^ cross)) for a in range(lev) for b in range(lat)
    ]
    return lax.ppermute(value, ("lev", "lat"), pairs)


def below(a, size):
    return (a - 1) % size


def above(a, size):
    return (a + 1) % size


def over_x(a, size):
    return a ^ 2


def quadrants(fields, cotangent):
    rows = WH // 2 * fields.shape[2]
    shape = like((2, rows, fields.shape[3]))
    own, lev, lat, both = call(split_kernel, [], [fields, cotangent], [shape] * 4, cost=1.0)
    return [own, move_both(lev, below, 0), swap(lat, "lat", 1), move_both(both, below, 1)]


def returned(parts):
    own, lev, lat, both = parts
    return [own, move_both(lev, above, 0), swap(lat, "lat", 1), move_both(both, above, 1)]


def reduce_cores(keep, arrived, after=(), cost=0.1):
    shape = like(keep.shape[1:])
    return call(first_sum_kernel, [], [keep] + arrived, [shape] * 4, after=after, cost=cost)


def move_chips(parts):
    own, along_y, along_x, along_both = parts
    return [own, swap(along_y, "lat", 1), swap(along_x, "lev", 2), move_both(along_both, over_x, 1)]


def reduce_chips(parts, tables=(), after=()):
    rows, channels = parts[0].shape
    if tables:
        rows += packed_rows(tables[0].shape[1] // channels) + 16
    shape = like((rows, channels))
    return call(second_sum_kernel, [], parts + list(tables), shape, after=after, cost=0.1)


def round_samples(share, group_index, sets, after=(), cost=0.1):
    lat = lax.axis_size("lat")
    samples = lat // WROWS
    if samples > sets:
        groups = [[s * WROWS + b for s in range(samples)] for b in range(WROWS)]
        hot = (jnp.arange(sets) == group_index[lax.axis_index("lat") // WROWS]).astype(F32)
        total = hot[:, None, None] * share.astype(F32)[None]
        total = lax.psum(total, "lat", axis_index_groups=groups).astype(BF)
        entries = [total[k] for k in range(sets)]
    else:
        entries = [share]
        for k in range(1, samples):
            pairs = [(i, (i + WROWS * k) % lat) for i in range(lat)]
            entries.append(lax.ppermute(share, "lat", pairs))
    shape = like((len(entries),) + share.shape)
    anywhere = pl.BlockSpec(memory_space=pl.ANY)
    return call(
        stack_kernel,
        [group_index],
        entries,
        shape,
        in_specs=[anywhere] * len(entries),
        out_specs=anywhere,
        scratch=[pltpu.VMEM(shape.shape, BF)] + [pltpu.SemaphoreType.DMA((len(entries),))] * 2,
        after=after,
        cost=cost,
    )


def hop(value, turn):
    lev, lat = lax.axis_size("lev"), lax.axis_size("lat")
    pairs = [
        (a * lat + b, (a ^ 2) * lat + b if a % 2 == turn else a * lat + (b ^ 1))
        for a in range(lev)
        for b in range(lat)
    ]
    return lax.ppermute(value, ("lev", "lat"), pairs)


def anchored(value, after, cost=0.1):
    anywhere = pl.BlockSpec(memory_space=pl.ANY)
    return call(
        anchor_kernel, [], [value], like(value.shape), in_specs=[anywhere], out_specs=anywhere,
        after=after, aliases={0: 0}, cost=cost,
    )


def body(
    fields,
    group_index,
    window_types,
    window_masks,
    first_gain,
    first_offset,
    input_weight,
    input_bias,
    output_weight,
    output_bias,
    second_gain,
    second_offset,
    expand_weight,
    expand_bias,
    reduce_weight,
    reduce_bias,
    position_bias,
    cotangent,
):
    columns = fields.shape[2]
    channels = fields.shape[3]
    sets, kinds, heads, positions = position_bias.shape
    groups = heads // GROUP
    cells = WZ * WH
    tokens = columns * cells
    rows = tokens // 4
    quarter = channels // 4
    lanes = channels // groups
    to_win = jnp.asarray(window_order(columns), BF)
    to_rows = jnp.asarray(window_order(columns).T, BF)
    own_lanes = jnp.asarray(head_lanes(lanes), BF)
    cols_map = jnp.asarray(column_maps(), BF)
    rows_map = jnp.asarray(token_rows(), BF)
    rows_back = jnp.asarray(token_rows().T, BF)
    places = jnp.asarray(head_places(), BF)
    fold = jnp.asarray(fold_map(), BF)

    arrived = quadrants(fields, cotangent)

    by_head = position_bias.transpose(0, 2, 1, 3)
    table = call(
        select_kernel,
        [group_index, window_types],
        [by_head],
        like((heads, positions)),
        in_specs=[own_member(by_head)],
        cost=1.0,
    )
    table = table.reshape(heads, WZ, WZ, WH, WH, SPAN).transpose(0, 2, 4, 1, 3, 5)
    table = table.reshape(heads, cells, cells * SPAN)
    table = jnp.pad(table, ((0, 0), (0, 16 - cells), (0, 0))).reshape(heads * 16, cells * SPAN)
    bias_map = call(
        bias_kernel,
        [],
        [window_masks, table, cols_map, rows_map, places, fold],
        like((groups, TOKENS, PADDED), F32),
        scratch=[pltpu.VMEM((heads, 16 * WW, TOKENS), BF)],
        cost=5.0,
    )

    hidden_units = expand_weight.shape[2]
    assert hidden_units == 4 * channels
    up_rows = 4 * quarter + 16
    low_rows = 2 * quarter
    inputs = (
        arrived
        + [to_win, to_rows, bias_map, own_lanes, first_gain, first_offset]
        + [input_weight, input_bias, output_weight, output_bias, second_gain, second_offset]
        + [expand_weight, expand_bias, reduce_weight, reduce_bias]
    )
    weights = {id(v) for v in (input_weight, output_weight, expand_weight, reduce_weight)}
    quadrant = like((rows, channels))
    anywhere = pl.BlockSpec(memory_space=pl.ANY)
    y0, y1, y2, y3, xw, triple, att, grad_hidden, keep, send = call(
        forward_kernel,
        [group_index],
        inputs,
        [quadrant] * 4
        + [
            like((tokens, channels)),
            like((tokens, 3 * channels)),
            like((tokens, channels)),
            like((tokens, channels), F32),
            like((4, up_rows, channels)),
            like((4, up_rows, channels)),
        ],
        in_specs=[
            anywhere if v is expand_weight or v is reduce_weight
            else own_member(v) if id(v) in weights
            else whole(v)
            for v in inputs
        ],
        out_specs=[whole(quadrant)] * 4
        + [anywhere] * 3
        + [whole((tokens, channels))]
        + [whole((4, up_rows, channels))] * 2,
        scratch=[
            pltpu.VMEM((tokens, channels), BF),
            pltpu.VMEM((channels, tokens), BF),
            pltpu.VMEM((tokens, channels), BF),
            pltpu.VMEM((tokens, channels), F32),
            pltpu.VMEM((tokens, channels), F32),
            pltpu.VMEM((8, channels), F32),
            pltpu.VMEM((channels, hidden_units), BF),
            pltpu.VMEM((hidden_units, channels), BF),
            pltpu.VMEM((tokens, channels), BF),
            pltpu.VMEM((tokens, 3 * channels), BF),
            pltpu.VMEM((tokens, channels), BF),
            pltpu.SemaphoreType.DMA((5,)),
        ],
        cost=33.0,
    )

    up_parts = reduce_cores(keep, [swap(send, "lev", 1)], cost=5.0)
    output_parts = returned([y0, y1, y2, y3])
    inputs = [triple, grad_hidden, bias_map, own_lanes, output_weight]
    grad_triple, score_sums = call(
        scores_back_kernel,
        [group_index],
        inputs,
        [like((tokens, 3 * channels)), like((groups, TOKENS, PADDED), F32)],
        in_specs=[own_member(v) if id(v) in weights else whole(v) for v in inputs],
        scratch=[pltpu.VMEM((tokens, channels), BF)],
        after=[up_parts[3]] + output_parts[1:3],
        cost=20.0,
    )
    up_share = reduce_chips(move_chips(up_parts), after=[grad_triple, output_parts[3]])

    inputs = [xw, att, grad_hidden, grad_triple, to_rows, first_gain, first_offset, input_weight]
    d0, d1, d2, d3, low_grads, low_small = call(
        input_back_kernel,
        [group_index],
        inputs,
        [quadrant] * 4 + [like((4, channels, channels)), like((16, channels))],
        in_specs=[own_member(v) if id(v) in weights else whole(v) for v in inputs],
        scratch=[pltpu.VMEM((16, channels), F32)],
        after=[up_share],
        cost=8.0,
    )
    low_keep, *low_send = call(
        spread_kernel,
        [],
        [low_grads],
        [like((4, low_rows, channels))] + [like((4, quarter, channels))] * 2,
        cost=0.1,
    )
    low_arrived = [swap(send, "lev", 1) for send in low_send]
    up_stack = round_samples(up_share, group_index, sets, after=low_arrived)
    low_parts = reduce_cores(low_keep, low_arrived, after=[up_stack])

    up_hop = hop(up_stack, 0)
    low_sums = move_chips(low_parts)
    output = call(assemble_kernel, [], output_parts, like(fields.shape), cost=1.0)
    table_grad = call(
        fold_kernel,
        [],
        [score_sums, cols_map, rows_back, places],
        like((heads * 16, cells * SPAN)),
        scratch=[pltpu.VMEM((2, WW, heads * 16, TOKENS), BF)],
        after=[up_stack, output],
        cost=7.0,
    )
    table_grad = table_grad.reshape(heads, 16, cells * SPAN)[:, :cells]
    table_grad = table_grad.reshape(heads, WZ, WH, WZ, WH, SPAN).transpose(0, 3, 1, 4, 2, 5)
    wide = -(-positions // channels) * channels
    table_grad = jnp.pad(
        table_grad.reshape(heads, positions), ((0, 16 - heads), (0, wide - positions))
    )
    low_share = reduce_chips(low_sums, [table_grad, low_small], after=[up_hop])

    up_stack = anchored(up_stack, [low_share])
    up_own = [up_stack, up_hop, hop(up_stack, 1), hop(up_hop, 1)]
    low_stack = round_samples(low_share, group_index, sets, after=up_own[2:], cost=10.0)
    up_other = [swap(v, "lev", 1) for v in up_own]
    low_hop = hop(low_stack, 0)
    low_stack = anchored(low_stack, [low_hop], cost=12.0)
    low_own = [low_stack, low_hop, hop(low_stack, 1), hop(low_hop, 1)]

    count = low_stack.shape[0]
    up_shapes = [
        like((sets, channels, hidden_units), F32),
        like((sets, 4, 4, quarter, channels), F32),
        like((sets, hidden_units), F32),
    ] + [like((sets, channels), F32)] * 3
    up_grad, down_grad, bup_grad, bdn_grad, g2_grad, o2_grad = call(
        functools.partial(
            finish_up_kernel,
            [[(0, k) for k in range(4)], [(1, None, k) for k in range(4)]],
            [(2, k * channels) for k in range(4)] + [(3, 0), (4, 0), (5, 0)],
        ),
        [group_index],
        up_own + up_other,
        up_shapes,
        in_specs=[anywhere] * 8,
        out_specs=[
            pl.BlockSpec((sets, quarter, hidden_units), lambda r, g: (0, r ^ my_place(), 0)),
            pl.BlockSpec(
                (sets, 4, 1, quarter, channels), lambda r, g: (0, 0, r ^ my_place(), 0, 0)
            ),
        ]
        + [whole(v) for v in up_shapes[2:]],
        scratch=[
            pltpu.VMEM((2, 4, count, up_rows, channels), BF),
            pltpu.SemaphoreType.DMA((2, 4)),
        ],
        grid=(4,),
        cost=11.0,
    )
    low_other = [swap(v, "lev", 1) for v in low_own[:2]]
    block_shapes = [
        like((sets, channels, 3 * channels), F32),
        like((sets, channels, channels), F32),
    ]
    near = call(
        finish_near_kernel,
        [group_index],
        low_own[:2] + low_other,
        block_shapes,
        in_specs=[anywhere] * 4,
        out_specs=[anywhere] * 2,
        scratch=[
            pltpu.VMEM((2, 2, count, low_rows, channels), BF),
            pltpu.VMEM((2, 2, 2, sets, quarter, channels), F32),
            pltpu.SemaphoreType.DMA((2, 2)),
            pltpu.SemaphoreType.DMA((2, 2, 2)),
        ],
        after=[up_grad],
        cost=5.0,
    )
    low_own[3] = anchored(low_own[3], [near[0]])
    low_other += [swap(v, "lev", 1) for v in low_own[2:]]
    small_shapes = [like((sets, w), F32) for w in (channels, 2 * channels, channels, channels)]
    all_rows = low_stack.shape[1]
    in_grad, out_grad, bout_grad, bin_grad, g1_grad, o1_grad, position_grad = call(
        functools.partial(
            finish_low_kernel, [(2, 0), (3, 0), (3, channels), (4, 0), (5, 0)]
        ),
        [group_index, window_types],
        low_own + low_other + list(near),
        block_shapes + small_shapes + [like((sets, heads, kinds, positions), F32)],
        in_specs=[anywhere] * 10,
        out_specs=[anywhere] * 2
        + [whole(v) for v in small_shapes]
        + [pl.BlockSpec((1, heads, kinds, positions), lambda g, *_: (g, 0, 0, 0))],
        scratch=[
            pltpu.VMEM((2, 2, count, all_rows, channels), BF),
            pltpu.VMEM((2, 2, count, all_rows - low_rows, channels), BF),
            pltpu.VMEM((2, 2, 2, sets, quarter, channels), F32),
            pltpu.VMEM((count * 128, wide), BF),
            pltpu.SemaphoreType.DMA((2, 2)),
            pltpu.SemaphoreType.DMA((2, 2)),
            pltpu.SemaphoreType.DMA((2, 2, 2)),
        ],
        grid=(sets,),
        aliases={10: 0, 11: 1},
        cost=8.0,
    )

    input_grad = call(
        assemble_kernel,
        [],
        returned([d0, d1, d2, d3]),
        like(fields.shape),
        after=[position_grad],
        cost=1.0,
    )
    down_grad = down_grad.reshape(sets, -1, channels)
    position_grad = position_grad.transpose(0, 2, 1, 3)
    return (
        output,
        input_grad,
        g1_grad,
        o1_grad,
        in_grad,
        bin_grad,
        out_grad,
        bout_grad,
        g2_grad,
        o2_grad,
        up_grad,
        bup_grad,
        down_grad,
        bdn_grad,
        position_grad,
    )


def solution(mesh):
    slab = P("lat", "lev", None, None)
    return jax.shard_map(
        body,
        mesh=mesh,
        in_specs=(slab,) + (P(),) * 16 + (slab,),
        out_specs=(slab, slab) + (P(),) * 13,
        check_vma=False,
    )
```

```python
import functools

import jax
import jax.numpy as jnp
import numpy as np
from jax import lax
from jax.experimental import pallas as pl
from jax.experimental.pallas import tpu as pltpu
from jax.sharding import PartitionSpec as P

WZ = 2
WH = 6
WW = 12
WROWS = 2
TOKENS = WZ * WH * WW
GROUP = 4
PADDED = 640
SPAN = 2 * WW - 1
MASKED = -1e30
LOG2E = 1.4426950408889634
BF = jnp.bfloat16
F32 = jnp.float32


def dot(a, b):
    return lax.dot_general(a, b, (((1,), (0,)), ((), ())), preferred_element_type=F32)


def dot_nt(a, b):
    return lax.dot_general(a, b, (((1,), (1,)), ((), ())), preferred_element_type=F32)


def dot_tn(a, b):
    return lax.dot_general(a, b, (((0,), (0,)), ((), ())), preferred_element_type=F32)


def one_hot(index, size):
    return (np.asarray(index)[:, None] == np.arange(size)[None, :]).astype(np.float32)


def window_order(columns):
    windows = columns // WW
    n, h, w = np.meshgrid(np.arange(windows), np.arange(WH), np.arange(WW), indexing="ij")
    source = h * columns + (n * WW + w + WW // 2) % columns
    return one_hot(source.reshape(-1), WH * columns)


def column_maps():
    cells = WZ * WH
    out = np.zeros((WW, cells, SPAN, cells, WW), np.float32)
    for wj in range(WW):
        for wi in range(WW):
            for c in range(cells):
                out[wj, c, wi - wj + WW - 1, c, wi] = 1.0
    return out.reshape(WW, cells * SPAN, cells * WW)


def token_rows():
    j = np.arange(TOKENS)
    return one_hot((j % WW) * 16 + j // WW, WW * 16)


def head_places():
    return np.stack([one_hot(h * TOKENS + np.arange(TOKENS), PADDED) for h in range(GROUP)])


def fold_map():
    return sum(head_places())


def head_lanes(lanes):
    return np.repeat(np.eye(GROUP, dtype=np.float32), lanes // GROUP, axis=1)


def select_kernel(group_index, window_types, tables_ref, out_ref):
    heads, kinds, positions = tables_ref.shape
    place = lax.axis_index("lev") * WROWS + lax.axis_index("lat") % WROWS
    kind = window_types[place]
    shape = (heads, heads * kinds)
    row = lax.broadcasted_iota(jnp.int32, shape, 0)
    col = lax.broadcasted_iota(jnp.int32, shape, 1)
    pick = jnp.where(col == row * kinds + kind, 1.0, 0.0).astype(BF)
    tables = tables_ref[...].astype(F32).reshape(heads * kinds, positions).astype(BF)
    out_ref[...] = dot(pick, tables).astype(BF)


def bias_kernel(masks_ref, table_ref, cols_ref, rows_ref, places_ref, fold_ref, out_ref, held):
    heads = held.shape[0]
    for wj in range(WW):
        part = dot(table_ref[...], cols_ref[wj]).astype(BF)
        for h in range(heads):
            held[h, 16 * wj : 16 * wj + 16, :] = part[16 * h : 16 * h + 16]
    half = lax.axis_index("lat") % WROWS
    labels = masks_ref[lax.axis_index("lev"), pl.ds(half, 1), :].astype(F32)
    top = lax.broadcasted_iota(jnp.int32, (8, TOKENS), 0) == 0
    labels = jnp.where(top, jnp.broadcast_to(labels, (8, TOKENS)), 0.0)
    across = dot(jnp.ones((TOKENS, 8), BF), dot(labels.astype(BF), fold_ref[...]).astype(BF))
    down = dot_tn(labels.astype(BF), jnp.ones((8, PADDED), BF))
    same = jnp.abs(across - down) < 0.5
    for g in range(heads // GROUP):
        total = dot(held[g * GROUP], places_ref[0])
        for h in range(1, GROUP):
            total = total + dot(held[g * GROUP + h], places_ref[h])
        out_ref[g] = jnp.where(same, dot(rows_ref[...], total.astype(BF)), MASKED) * LOG2E


def fold_kernel(sums_ref, cols_ref, rows_ref, places_ref, out_ref, held):
    groups = sums_ref.shape[0]
    for g in range(groups):
        value = sums_ref[g]
        high = value.astype(BF)
        low = (value - high.astype(F32)).astype(BF)
        for index, part in enumerate((high, low)):
            ordered = dot(rows_ref[...], part).astype(BF)
            for h in range(GROUP):
                block = dot_nt(ordered, places_ref[h]).astype(BF)
                spot = (g * GROUP + h) * 16
                for wj in range(WW):
                    held[index, wj, spot : spot + 16, :] = block[16 * wj : 16 * wj + 16]
    total = jnp.zeros(out_ref.shape, F32)
    for wj in range(WW):
        for index in range(2):
            total = total + dot_nt(held[index, wj], cols_ref[wj])
    out_ref[...] = total.astype(BF)


def norm_parts(values):
    centre = values - jnp.mean(values, axis=-1, keepdims=True)
    spread = jnp.mean(centre * centre, axis=-1, keepdims=True)
    root = lax.rsqrt(spread + 1e-05)
    return centre * root, root


def norm_back(grad, gain, xhat, root):
    u = grad * gain
    return (
        u - jnp.mean(u, axis=-1, keepdims=True) - xhat * jnp.mean(u * xhat, axis=-1, keepdims=True)
    ) * root


def stacked_heads(block, lanes_ref):
    pieces = [block * lanes_ref[h : h + 1, :] for h in range(GROUP)]
    pieces.append(jnp.zeros((PADDED - GROUP * block.shape[0], block.shape[1]), block.dtype))
    return jnp.concatenate(pieces, axis=0)


def own_head(full):
    size = full.shape[0] // GROUP
    return jnp.concatenate(
        [
            full[h * size : (h + 1) * size, h * TOKENS : (h + 1) * TOKENS]
            for h in range(GROUP)
        ],
        axis=0,
    )


def softmax_t(keys, queries, bias, scale):
    scores = dot_nt(keys, queries) * (scale * LOG2E) + bias
    exponent = jnp.exp2(scores - jnp.max(scores, axis=0, keepdims=True))
    return exponent * (1.0 / jnp.sum(exponent, axis=0, keepdims=True))


def to_windows(level_map, levels):
    half = WH * WW
    parts = [dot(level_map, level) for level in levels]
    pieces = []
    for n in range(parts[0].shape[0] // half):
        for part in parts:
            pieces.append(part[n * half : (n + 1) * half])
    return jnp.concatenate(pieces, axis=0)


def to_levels(level_map, value):
    half = WH * WW
    count = value.shape[0] // (2 * half)
    quadrants = [None] * 4
    for z in range(WZ):
        level = [value[(2 * n + z) * half : (2 * n + z + 1) * half] for n in range(count)]
        level = dot(level_map, jnp.concatenate(level, axis=0).astype(BF))
        rows = level.shape[0] // 2
        for side in range(2):
            quadrants[side * WZ + z] = level[side * rows : (side + 1) * rows].astype(BF)
    return quadrants


def my_place():
    return (lax.axis_index("lev") // 2) * 2 + lax.axis_index("lat") % WROWS


def my_core():
    return lax.axis_index("lev") % 2


def place_slot(keep_out, send_outs, owner, rel, start, value):
    @pl.when(my_core() == owner)
    def _():
        keep_out[rel, start : start + value.shape[0]] = value

    @pl.when(my_core() != owner)
    def _():
        at = start
        for out in send_outs:
            if 0 <= at < out.shape[1]:
                out[rel, at : at + value.shape[0]] = value
            at -= out.shape[1]


def scatter_rows(keep_out, send_outs, owner, block, value):
    value = value.astype(BF)
    size = value.shape[0] // 4
    for q in range(4):
        piece = value[q * size : (q + 1) * size]
        place_slot(keep_out, send_outs, owner, q ^ my_place(), block * size, piece)


def scatter_small(keep_out, send_outs, small):
    start = keep_out.shape[1] - 16
    for n in range(8):
        row = jnp.broadcast_to(small[n : n + 1, :], (16, small.shape[1])).astype(BF)
        place_slot(keep_out, send_outs, n // 4, (n % 4) ^ my_place(), start, row)


def my_set(group_index):
    return group_index[lax.axis_index("lat") // WROWS]


def entry_sets(group_index, count, sets):
    samples = lax.axis_size("lat") // WROWS
    if samples > sets:
        return list(range(sets)), [True] * sets
    owners = [group_index[k] for k in range(count)]
    first = []
    for k in range(count):
        fresh = jnp.bool_(True)
        for j in range(k):
            fresh = fresh & (owners[j] != owners[k])
        first.append(fresh)
    return owners, first


def param_row(ref, group):
    return ref[pl.ds(group, 1), :]


def forward_kernel(
    group_index, f0, f1, f2, f3, to_win, to_rows, bias_ref, lanes_ref,
    g1_ref, o1_ref, win_ref, bin_ref, wout_ref, bout_ref, g2_ref, o2_ref,
    wups_ref, bup_ref, wdns_ref, bdn_ref,
    y0, y1, y2, y3, xw_any, triple_any, att_any, gh_out, keep_out, send_out,
    n2_s, n2t_s, cot_s, acc_s, back_s, small_out,
    wup_ref, wdn_ref, xw_out, triple_out, att_out, semaphores,
):
    gid = my_set(group_index)
    tokens, channels = xw_out.shape
    weights = [
        pltpu.make_async_copy(source.at[gid], target, semaphores.at[k])
        for k, (source, target) in enumerate(((wups_ref, wup_ref), (wdns_ref, wdn_ref)))
    ]
    for copy in weights:
        copy.start()
    results = [
        pltpu.make_async_copy(source, target, semaphores.at[2 + k])
        for k, (source, target) in enumerate(
            ((xw_out, xw_any), (triple_out, triple_any), (att_out, att_any))
        )
    ]
    lanes = lanes_ref.shape[1]
    scale = (lanes // GROUP) ** -0.5

    def gathered(which):
        levels = [
            jnp.concatenate([low[which].astype(F32), high[which].astype(F32)], axis=0).astype(BF)
            for low, high in ((f0, f2), (f1, f3))
        ]
        return to_windows(to_win[...], levels)

    x = gathered(0)
    xw_out[...] = x.astype(BF)
    cot_s[...] = gathered(1).astype(BF)
    xhat, _ = norm_parts(x)
    normed = (xhat * param_row(g1_ref, gid) + param_row(o1_ref, gid)).astype(BF)
    bias_row = param_row(bin_ref, gid)
    bias_row = jnp.concatenate(
        [bias_row[:, :channels], jnp.zeros((1, channels), F32), bias_row[:, channels:]], axis=1
    )
    triple_out[...] = (dot(normed, win_ref[...]) + bias_row).astype(BF)
    results[0].start()
    results[1].start()

    def window(n, carry):
        rows = pl.ds(pl.multiple_of(n * TOKENS, 16), TOKENS)
        for g in range(channels // lanes):
            lo = g * lanes
            queries = stacked_heads(triple_out[rows, lo : lo + lanes], lanes_ref)
            keys = triple_out[rows, channels + lo : channels + lo + lanes]
            values = triple_out[rows, 2 * channels + lo : 2 * channels + lo + lanes]
            probs = softmax_t(keys, queries, bias_ref[g], scale).astype(BF)
            full = dot_tn(values, probs)
            att_out[rows, lo : lo + lanes] = own_head(full).T.astype(BF)
        return carry

    lax.fori_loop(0, tokens // TOKENS, window, 0, unroll=6)

    results[2].start()
    mixed = (dot(att_out[...], wout_ref[...]) + param_row(bout_ref, gid)).astype(BF)
    hidden = xw_out[...].astype(F32) + mixed.astype(F32)
    xhat2, root2 = norm_parts(hidden)
    gain2 = param_row(g2_ref, gid)
    n2 = (xhat2 * gain2 + param_row(o2_ref, gid)).astype(BF)
    n2_s[...] = n2
    n2t_s[...] = n2.T
    acc_s[...] = hidden + param_row(bdn_ref, gid)
    per = 4
    step = per * channels

    bup = param_row(bup_ref, gid)
    for copy in weights:
        copy.wait()
    for k in range(wup_ref.shape[1] // step):
        cols = slice(k * step, (k + 1) * step)
        up = wup_ref[:, cols]
        down = wdn_ref[cols, :]
        expanded = dot(n2_s[...], up) + bup[:, cols]
        cdf = 0.5 * (1.0 + lax.erf(expanded * (0.5**0.5)))
        active = (expanded * cdf).astype(BF)
        slope = cdf + expanded * (jnp.exp(-0.5 * expanded * expanded) * 0.3989422804014327)
        grad_expanded = (dot_nt(cot_s[...], down) * slope).astype(BF)
        acc_s[...] += dot(active, down)
        back = dot_nt(grad_expanded, up)
        back_s[...] = back if k == 0 else back_s[...] + back
        grad_up = dot(n2t_s[...], grad_expanded)
        grad_down = dot_tn(active, cot_s[...])
        sums = jnp.sum(grad_expanded.astype(F32), axis=0, keepdims=True)
        for j in range(per):
            part = slice(j * channels, (j + 1) * channels)
            scatter_rows(keep_out, [send_out], 0, per * k + j, grad_up[:, part])
            scatter_rows(keep_out, [send_out], 1, per * k + j, grad_down[part])
            small_out[per * k + j : per * k + j + 1, :] = sums[:, part]

    for ref, value in zip((y0, y1, y2, y3), to_levels(to_rows[...], acc_s[...])):
        ref[...] = value
    cot = cot_s[...].astype(F32)
    grad = back_s[...]
    small_out[4:5, :] = jnp.sum(cot, axis=0, keepdims=True)
    small_out[5:6, :] = jnp.sum(grad * xhat2, axis=0, keepdims=True)
    small_out[6:7, :] = jnp.sum(grad, axis=0, keepdims=True)
    small_out[7:8, :] = jnp.zeros((1, channels), F32)
    scatter_small(keep_out, [send_out], small_out[...])
    gh_out[...] = cot + norm_back(grad, gain2, xhat2, root2)
    for copy in results:
        copy.wait()


def scores_back_kernel(
    group_index, triple_ref, gh_ref, bias_ref, lanes_ref, wout_ref,
    gt_out, sums_out, ga_s,
):
    channels = gh_ref.shape[1]
    tokens = gh_ref.shape[0]
    lanes = lanes_ref.shape[1]
    scale = (lanes // GROUP) ** -0.5
    ga_s[...] = dot_nt(gh_ref[...].astype(BF), wout_ref[...]).astype(BF)
    sums_out[...] = jnp.zeros_like(sums_out)

    def window(n, carry):
        rows = pl.ds(pl.multiple_of(n * TOKENS, 16), TOKENS)
        for g in range(channels // lanes):
            lo = g * lanes
            queries = stacked_heads(triple_ref[rows, lo : lo + lanes], lanes_ref)
            keys = triple_ref[rows, channels + lo : channels + lo + lanes]
            values = triple_ref[rows, 2 * channels + lo : 2 * channels + lo + lanes]
            probs = softmax_t(keys, queries, bias_ref[g], scale)
            grad_att = stacked_heads(ga_s[rows, lo : lo + lanes], lanes_ref)
            grad_probs = dot_nt(values, grad_att)
            row_dot = jnp.sum(probs * grad_probs, axis=0, keepdims=True)
            grad_scores = (probs * (grad_probs - row_dot)).astype(BF)
            sums_out[g] += grad_scores.astype(F32)
            full = dot_tn(keys, grad_scores)
            gt_out[rows, lo : lo + lanes] = (own_head(full) * scale).T.astype(BF)
            gt_out[rows, channels + lo : channels + lo + lanes] = (
                dot(grad_scores, queries) * scale
            ).astype(BF)
            gt_out[rows, 2 * channels + lo : 2 * channels + lo + lanes] = dot(
                probs.astype(BF), grad_att
            ).astype(BF)
        return carry

    lax.fori_loop(0, tokens // TOKENS, window, 0, unroll=2)


def input_back_kernel(
    group_index, xw_ref, att_ref, gh_ref, gt_ref, to_rows, g1_ref, o1_ref, win_ref,
    d0, d1, d2, d3, low_out, band_out, small_out,
):
    gid = my_set(group_index)
    channels = xw_ref.shape[1]
    grad_mixed = gh_ref[...].astype(BF)
    low_out[3] = dot_tn(att_ref[...], grad_mixed).astype(BF)
    small_out[0:1, :] = jnp.sum(grad_mixed.astype(F32), axis=0, keepdims=True)
    xhat, root = norm_parts(xw_ref[...].astype(F32))
    gain = param_row(g1_ref, gid)
    normed = (xhat * gain + param_row(o1_ref, gid)).astype(BF)
    grad_in = dot(normed.T, gt_ref[...])
    grad = dot_nt(gt_ref[...], win_ref[...])
    for part in range(3):
        cols = slice(part * channels, (part + 1) * channels)
        low_out[part] = grad_in[:, cols].astype(BF)
        if part != 1:
            row = 1 + part // 2
            piece = gt_ref[:, cols].astype(F32)
            small_out[row : row + 1, :] = jnp.sum(piece, axis=0, keepdims=True)
    small_out[3:4, :] = jnp.sum(grad * xhat, axis=0, keepdims=True)
    small_out[4:5, :] = jnp.sum(grad, axis=0, keepdims=True)
    small_out[5:16, :] = jnp.zeros((11, channels), F32)
    band_out[...] = small_out[...].astype(BF)
    shifted = norm_back(grad, gain, xhat, root).astype(BF)
    parts = to_levels(to_rows[...], gh_ref[...] + shifted.astype(F32))
    for part, ref in zip(parts, (d0, d1, d2, d3)):
        ref[...] = part


def split_kernel(places, fields_ref, cot_ref, *outs):
    half = WH // 2
    for out, (row, level) in zip(outs, places):
        for k, ref in enumerate((fields_ref, cot_ref)):
            parts = [ref[row + h, level].astype(F32) for h in range(half)]
            out[k] = jnp.concatenate(parts, axis=0).astype(BF)


def assemble_kernel(own_ref, lev_ref, lat_ref, both_ref, out):
    half, columns = WH // 2, out.shape[2]
    for ref, row, level in (
        (own_ref, half, 1), (lev_ref, half, 0), (lat_ref, 0, 1), (both_ref, 0, 0)
    ):
        value = ref[...].astype(F32)
        for h in range(half):
            out[row + h, level] = value[h * columns : (h + 1) * columns].astype(BF)


def spread_kernel(low_ref, keep_out, *send_outs):
    for block in range(low_ref.shape[0]):
        scatter_rows(keep_out, send_outs, block // 2, block % 2, low_ref[block])


def first_sum_kernel(keep_ref, *refs):
    arrived, outs = refs[:-4], refs[-4:]
    at = 0
    for part in arrived:
        rows = slice(at, at + part.shape[1])
        at += part.shape[1]
        for k in range(4):
            total = keep_ref[k, rows].astype(F32) + part[k].astype(F32)
            outs[k][rows] = total.astype(BF)


def packed_rows(bands):
    return 16 * (-(-(bands + -(-bands // 2)) // 2))


def packed_units(table, channels):
    bands = table.shape[1] // channels
    parts = [table[:, n * channels : (n + 1) * channels].astype(F32) for n in range(bands)]
    units = [part[0:8] for part in parts]
    for n in range(0, bands, 2):
        unit = parts[n][8:16]
        if n + 1 < bands:
            unit = unit + pltpu.roll(parts[n + 1][8:16], 4, 0)
        units.append(unit)
    return units + [jnp.zeros_like(units[0])] * (len(units) % 2)


def unpacked_bands(rows, bands):
    units = []
    for n in range(packed_rows(bands) // 16):
        value = rows(n).astype(F32)
        units += [value[0:8], value[8:16]]
    out = []
    for n in range(bands):
        unit = units[bands + n // 2]
        rest = pltpu.roll(unit, 4, 0) if n % 2 else unit
        out.append(jnp.concatenate([units[n], rest], axis=0).astype(BF))
    return out


def second_sum_kernel(own_ref, y_ref, x_ref, xy_ref, *refs):
    tables, out = refs[:-1], refs[-1]
    rows, channels = own_ref.shape
    total = own_ref[...].astype(F32) + y_ref[...].astype(F32)
    out[:rows] = (total + x_ref[...].astype(F32) + xy_ref[...].astype(F32)).astype(BF)
    if tables:
        units = packed_units(tables[0], channels)
        for n in range(0, len(units), 2):
            at = rows + 8 * n
            out[at : at + 16] = jnp.concatenate(units[n : n + 2], axis=0).astype(BF)
        out[out.shape[0] - 16 :] = tables[1][...]


def stack_kernel(group_index, *refs):
    entries, out, held, arrivals, leavings = refs[:-4], refs[-4], refs[-3], refs[-2], refs[-1]
    count = len(entries)
    mine = lax.axis_index("lat") // WROWS
    samples = lax.axis_size("lat") // WROWS
    inward, outward = [], []
    for k in range(count):
        slot = (mine + samples - k) % samples if samples == count else k
        inward.append(pltpu.make_async_copy(entries[k], held.at[k], arrivals.at[k]))
        outward.append(pltpu.make_async_copy(held.at[k], out.at[slot], leavings.at[k]))
    for copy in inward:
        copy.start()
    for k in range(count):
        inward[k].wait()
        outward[k].start()
    for copy in outward:
        copy.wait()


def anchor_kernel(*refs):
    pass


def slot_of(core_type, index):
    return (index % 2) * 2 + index // 2 if core_type == 0 else index


def fetch_pieces(sources, buffer, semaphores):
    def copies(own, other):
        for core_type, arrays in ((0, own), (1, other)):
            for index in range(4):
                slot = slot_of(core_type, index)
                yield pltpu.make_async_copy(
                    arrays[index],
                    buffer.at[core_type, slot],
                    semaphores.at[core_type, slot],
                )

    @pl.when(my_core() == 0)
    def _():
        for copy in copies(sources[:4], sources[4:]):
            copy.start()

    @pl.when(my_core() == 1)
    def _():
        for copy in copies(sources[4:], sources[:4]):
            copy.start()


def wait_piece(sources, buffer, semaphores, core_type, slot):
    pltpu.make_async_copy(
        sources[0], buffer.at[core_type, slot], semaphores.at[core_type, slot]
    ).wait()


def spread_sets(owners, first, sets, read, write):
    for k in range(len(owners)):

        @pl.when(first[k])
        def _(k=k):
            write(owners[k], False, read(k))

        @pl.when(jnp.logical_not(first[k]))
        def _(k=k):
            write(owners[k], True, read(k))

    if not isinstance(owners[0], int):
        for g in range(sets):
            there = owners[0] == g
            for owner in owners[1:]:
                there = there | (owner == g)

            @pl.when(jnp.logical_not(there))
            def _(g=g):
                write(g, False, [jnp.zeros_like(value) for value in read(0)])


def finish_step(layout, small, outs, buffer, rel, owners, first, sets):
    channels = buffer.shape[4]
    size = channels // 4
    places = []
    for core_type, blocks in enumerate(layout):
        for at, place in enumerate(blocks):
            places.append((core_type, slice(at * size, (at + 1) * size), place))

    def read(k):
        return [buffer[t, rel, k, rows, :].astype(F32) for t, rows, _ in places]

    def write(g, add, values):
        for (_, _, place), value in zip(places, values):
            if place[1] is None:
                index = (g, place[2], 0)
            else:
                index = (g, slice(None), slice(place[1] * channels, (place[1] + 1) * channels))
            ref = outs[place[0]]
            ref[index] = ref[index] + value if add else value

    spread_sets(owners, first, sets, read, write)
    start = len(layout[0]) * size
    q = rel ^ my_place()
    for number, place in enumerate(small):
        if place is None:
            continue

        @pl.when(q == number % 4)
        def _(number=number, place=place):
            out, column = place
            cols = slice(column, column + channels)

            def read(k):
                rows = buffer[number // 4, rel, k, start : start + 16, :]
                return [rows.astype(F32)[0:1]]

            def write(g, add, values):
                index = (pl.ds(g, 1), cols)
                outs[out][index] = outs[out][index] + values[0] if add else values[0]

            spread_sets(owners, first, sets, read, write)


def finish_up_kernel(layout, small, group_index, *refs):
    sources, outs, buffer, semaphores = refs[:8], refs[8:-2], refs[-2], refs[-1]
    step = pl.program_id(0)
    sets, count = outs[0].shape[0], buffer.shape[2]
    owners, first = entry_sets(group_index, count, sets)

    @pl.when(step == 0)
    def _():
        fetch_pieces(sources, buffer, semaphores)

    for core_type in range(2):
        wait_piece(sources, buffer, semaphores, core_type, step)
    finish_step(layout, small, outs, buffer, step, owners, first, sets)


def by_type(sources, number, act):
    own, other = sources[:number], sources[number : 2 * number]

    @pl.when(my_core() == 0)
    def _():
        act((own, other))

    @pl.when(my_core() == 1)
    def _():
        act((other, own))


def row_copies(core_type, index, stage, in_any, out_any, semaphores):
    channels = out_any.shape[2]
    size = channels // 4
    q = slot_of(core_type, index) ^ my_place()
    rows = pl.ds(pl.multiple_of(q * size, size), size)
    if core_type == 0:
        targets = [in_any.at[:, rows, 0:channels], in_any.at[:, rows, channels : 2 * channels]]
    else:
        targets = [in_any.at[:, rows, 2 * channels :], out_any.at[:, rows, :]]
    return [
        pltpu.make_async_copy(stage.at[k], target, semaphores.at[k])
        for k, target in enumerate(targets)
    ]


def finish_rows(piece, stage, owners, first, sets):
    size = stage.shape[2]

    def read(k):
        return [piece[k, n * size : (n + 1) * size, :].astype(F32) for n in range(2)]

    def write(g, add, values):
        for n, value in enumerate(values):
            stage[n, g] = stage[n, g] + value if add else value

    spread_sets(owners, first, sets, read, write)


def finish_near_kernel(group_index, *refs):
    sources, (in_any, out_any), (buffer, stage, arrivals, leavings) = refs[:4], refs[4:6], refs[6:]
    sets, count = stage.shape[3], buffer.shape[2]
    owners, first = entry_sets(group_index, count, sets)
    rows = buffer.shape[3]
    items = [(t, n) for n in range(2) for t in range(2)]

    def start(lists):
        for t, n in items:
            pltpu.make_async_copy(
                lists[t][n].at[:, :rows], buffer.at[t, n], arrivals.at[t, n]
            ).start()

    by_type(sources, 2, start)
    copies = []
    for t, n in items:
        pltpu.make_async_copy(
            sources[0].at[:, :rows], buffer.at[t, n], arrivals.at[t, n]
        ).wait()
        finish_rows(buffer.at[t, n], stage.at[t, n], owners, first, sets)
        copies += row_copies(t, n, stage.at[t, n], in_any, out_any, leavings.at[t, n])
        for copy in copies[-2:]:
            copy.start()
    for copy in copies:
        copy.wait()


def finish_low_kernel(small, group_index, window_types, *refs):
    sources, outs = refs[:8], refs[10:-7]
    buffer, tables, stage, held, arrivals, table_arrivals, leavings = refs[-7:]
    in_any, out_any, out = outs[0], outs[1], outs[-1]
    step = pl.program_id(0)
    sets, count, channels = stage.shape[3], buffer.shape[2], buffer.shape[4]
    heads, kinds, positions = out.shape[1:]
    owners, first = entry_sets(group_index, count, sets)
    top = buffer.shape[3] - tables.shape[3]
    items = [(t, n) for n in range(2) for t in range(2)]

    @pl.when(step == 0)
    def _():
        def start(lists):
            for t, n in items:
                pltpu.make_async_copy(
                    lists[t][2 + n], buffer.at[t, n], arrivals.at[t, n]
                ).start()
            for t, n in items:
                pltpu.make_async_copy(
                    lists[t][n].at[:, top:], tables.at[t, n], table_arrivals.at[t, n]
                ).start()

        by_type(sources, 4, start)
        for t, n in items:
            pltpu.make_async_copy(sources[0], buffer.at[t, n], arrivals.at[t, n]).wait()
            finish_rows(buffer.at[t, n], stage.at[t, n], owners, first, sets)
            for copy in row_copies(t, 2 + n, stage.at[t, n], in_any, out_any, leavings.at[t, n]):
                copy.start()
        for t, n in items:
            pltpu.make_async_copy(
                sources[0].at[:, top:], tables.at[t, n], table_arrivals.at[t, n]
            ).wait()
        for ref in outs[2:-1]:
            ref[...] = jnp.zeros_like(ref)
        bands = held.shape[1] // channels
        for k in range(count):
            sums = jnp.zeros((16, channels), F32)
            for t in range(2):
                for index in range(4):
                    at = ((k * 2 + t) * 4 + slot_of(t, index)) * 16

                    def rows(band, index=index, t=t, k=k):
                        if index < 2:
                            return tables[t, index, k, 16 * band : 16 * band + 16]
                        return buffer[
                            t, index - 2, k, top + 16 * band : top + 16 * band + 16
                        ]

                    for band, value in enumerate(unpacked_bands(rows, bands)):
                        held[at : at + 16, band * channels : (band + 1) * channels] = value
                    sums = sums + rows(packed_rows(bands) // 16).astype(F32)
            for n, (number, column) in enumerate(small):
                index = (pl.ds(owners[k], 1), slice(column, column + channels))
                outs[number][index] = outs[number][index] + sums[n : n + 1]

    shape = (heads * kinds, count * 128)
    row = lax.broadcasted_iota(jnp.int32, shape, 0)
    col = lax.broadcasted_iota(jnp.int32, shape, 1)
    kind_of = jnp.zeros(shape, jnp.int32)
    for t in range(2):
        for r in range(4):
            q = r ^ my_place()
            kind = window_types[q // 2 * 4 + t * 2 + q % 2]
            kind_of = jnp.where(col // 16 % 8 == t * 4 + r, kind, kind_of)
    set_of = jnp.zeros(shape, jnp.int32)
    for k in range(count):
        set_of = jnp.where(col // 128 == k, owners[k], set_of)
    hit = (row // kinds == col % 16) & (row % kinds == kind_of) & (set_of == step)
    value = dot(jnp.where(hit, 1.0, 0.0).astype(BF), held[...])
    out[0] = value[:, :positions].reshape(out.shape[1:])

    @pl.when(step == sets - 1)
    def _():
        for t, n in items:
            for copy in row_copies(t, 2 + n, stage.at[t, n], in_any, out_any, leavings.at[t, n]):
                copy.wait()


def whole(array_or_shape):
    shape = getattr(array_or_shape, "shape", array_or_shape)
    return pl.BlockSpec(shape, lambda i, *_: (0,) * len(shape))


def own_member(array):
    def index(i, group_index, *_):
        return (my_set(group_index),) + (0,) * (array.ndim - 1)

    return pl.BlockSpec((None,) + array.shape[1:], index)


def call(
    kernel, scalars, inputs, out_shapes, *, in_specs=None, out_specs=None, scratch=(), grid=(1,),
    after=(), cost=1.0, aliases=None,
):
    in_specs = [whole(v) for v in inputs] if in_specs is None else in_specs
    out_specs = jax.tree.map(whole, out_shapes) if out_specs is None else out_specs
    count = len(scalars) + len(inputs)
    body = kernel
    if after:

        def body(*refs):
            kernel(*refs[:count], *refs[count + len(after) :])

    after = list(after)

    return pl.pallas_call(
        body,
        grid_spec=pltpu.PrefetchScalarGridSpec(
            num_scalar_prefetch=len(scalars),
            grid=grid,
            in_specs=list(in_specs) + [pl.BlockSpec(memory_space=pl.ANY)] * len(after),
            out_specs=out_specs,
            scratch_shapes=list(scratch),
        ),
        out_shape=out_shapes,
        input_output_aliases=aliases or {},
        compiler_params=pltpu.CompilerParams(vmem_limit_bytes=64 * 1024 * 1024),
        cost_estimate=pl.CostEstimate(
            flops=int(cost * 1.1e9), bytes_accessed=10**3, transcendentals=0
        ),
    )(*scalars, *inputs, *after)


def like(shape, kind=BF):
    return jax.ShapeDtypeStruct(tuple(shape), kind)


def swap(value, axis, distance):
    pairs = [(i, i ^ distance) for i in range(lax.axis_size(axis))]
    return lax.ppermute(value, axis, pairs)


def move_both(value, step, cross):
    lev, lat = lax.axis_size("lev"), lax.axis_size("lat")
    pairs = [
        (a * lat + b, step(a, lev) * lat + (b ^ cross)) for a in range(lev) for b in range(lat)
    ]
    return lax.ppermute(value, ("lev", "lat"), pairs)


def below(a, size):
    return (a - 1) % size


def above(a, size):
    return (a + 1) % size


def over_x(a, size):
    return a ^ 2


def quadrants(fields, cotangent):
    rows = WH // 2 * fields.shape[2]
    shape = like((2, rows, fields.shape[3]))
    lat, both = call(
        functools.partial(split_kernel, ((0, 1), (0, 0))),
        [],
        [fields, cotangent],
        [shape] * 2,
        cost=1.0,
    )
    own, lev = call(
        functools.partial(split_kernel, ((WH // 2, 1), (WH // 2, 0))),
        [],
        [fields, cotangent],
        [shape] * 2,
        after=[both],
        cost=1.0,
    )
    both, lat = move_both(both, below, 1), swap(lat, "lat", 1)
    return [own, move_both(lev, below, 0), lat, both]


def returned(parts):
    own, lev, lat, both = parts
    return [own, move_both(lev, above, 0), swap(lat, "lat", 1), move_both(both, above, 1)]


def reduce_cores(keep, arrived, after=(), cost=0.1):
    shape = like(keep.shape[1:])
    return call(first_sum_kernel, [], [keep] + arrived, [shape] * 4, after=after, cost=cost)


def move_chips(parts):
    own, along_y, along_x, along_both = parts
    return [own, swap(along_y, "lat", 1), swap(along_x, "lev", 2), move_both(along_both, over_x, 1)]


def reduce_chips(parts, tables=(), after=()):
    rows, channels = parts[0].shape
    if tables:
        rows += packed_rows(tables[0].shape[1] // channels) + 16
    shape = like((rows, channels))
    return call(second_sum_kernel, [], parts + list(tables), shape, after=after, cost=0.1)


def round_samples(share, group_index, sets, after=(), cost=0.1):
    lat = lax.axis_size("lat")
    samples = lat // WROWS
    if samples > sets:
        groups = [[s * WROWS + b for s in range(samples)] for b in range(WROWS)]
        hot = (jnp.arange(sets) == group_index[lax.axis_index("lat") // WROWS]).astype(F32)
        total = hot[:, None, None] * share.astype(F32)[None]
        total = lax.psum(total, "lat", axis_index_groups=groups).astype(BF)
        entries = [total[k] for k in range(sets)]
    else:
        entries = [share]
        for k in range(1, samples):
            pairs = [(i, (i + WROWS * k) % lat) for i in range(lat)]
            entries.append(lax.ppermute(share, "lat", pairs))
    shape = like((len(entries),) + share.shape)
    anywhere = pl.BlockSpec(memory_space=pl.ANY)
    return call(
        stack_kernel,
        [group_index],
        entries,
        shape,
        in_specs=[anywhere] * len(entries),
        out_specs=anywhere,
        scratch=[pltpu.VMEM(shape.shape, BF)] + [pltpu.SemaphoreType.DMA((len(entries),))] * 2,
        after=after,
        cost=cost,
    )


def hop(value, turn):
    lev, lat = lax.axis_size("lev"), lax.axis_size("lat")
    pairs = [
        (a * lat + b, (a ^ 2) * lat + b if a % 2 == turn else a * lat + (b ^ 1))
        for a in range(lev)
        for b in range(lat)
    ]
    return lax.ppermute(value, ("lev", "lat"), pairs)


def anchored(value, after, cost=0.1):
    anywhere = pl.BlockSpec(memory_space=pl.ANY)
    return call(
        anchor_kernel, [], [value], like(value.shape), in_specs=[anywhere], out_specs=anywhere,
        after=after, aliases={0: 0}, cost=cost,
    )


def body(
    fields,
    group_index,
    window_types,
    window_masks,
    first_gain,
    first_offset,
    input_weight,
    input_bias,
    output_weight,
    output_bias,
    second_gain,
    second_offset,
    expand_weight,
    expand_bias,
    reduce_weight,
    reduce_bias,
    position_bias,
    cotangent,
):
    columns = fields.shape[2]
    channels = fields.shape[3]
    sets, kinds, heads, positions = position_bias.shape
    groups = heads // GROUP
    cells = WZ * WH
    tokens = columns * cells
    rows = tokens // 4
    quarter = channels // 4
    lanes = channels // groups
    to_win = jnp.asarray(window_order(columns), BF)
    to_rows = jnp.asarray(window_order(columns).T, BF)
    own_lanes = jnp.asarray(head_lanes(lanes), BF)
    cols_map = jnp.asarray(column_maps(), BF)
    rows_map = jnp.asarray(token_rows(), BF)
    rows_back = jnp.asarray(token_rows().T, BF)
    places = jnp.asarray(head_places(), BF)
    fold = jnp.asarray(fold_map(), BF)

    arrived = quadrants(fields, cotangent)

    by_head = position_bias.transpose(0, 2, 1, 3)
    table = call(
        select_kernel,
        [group_index, window_types],
        [by_head],
        like((heads, positions)),
        in_specs=[own_member(by_head)],
        cost=1.0,
    )
    table = table.reshape(heads, WZ, WZ, WH, WH, SPAN).transpose(0, 2, 4, 1, 3, 5)
    table = table.reshape(heads, cells, cells * SPAN)
    table = jnp.pad(table, ((0, 0), (0, 16 - cells), (0, 0))).reshape(heads * 16, cells * SPAN)
    bias_map = call(
        bias_kernel,
        [],
        [window_masks, table, cols_map, rows_map, places, fold],
        like((groups, TOKENS, PADDED), F32),
        scratch=[pltpu.VMEM((heads, 16 * WW, TOKENS), BF)],
        cost=5.0,
    )

    hidden_units = expand_weight.shape[2]
    assert hidden_units == 4 * channels
    up_rows = 4 * quarter + 16
    low_rows = 2 * quarter
    inputs = (
        arrived
        + [to_win, to_rows, bias_map, own_lanes, first_gain, first_offset]
        + [input_weight, input_bias, output_weight, output_bias, second_gain, second_offset]
        + [expand_weight, expand_bias, reduce_weight, reduce_bias]
    )
    weights = {id(v) for v in (input_weight, output_weight, expand_weight, reduce_weight)}
    quadrant = like((rows, channels))
    anywhere = pl.BlockSpec(memory_space=pl.ANY)
    y0, y1, y2, y3, xw, triple, att, grad_hidden, keep, send = call(
        forward_kernel,
        [group_index],
        inputs,
        [quadrant] * 4
        + [
            like((tokens, channels)),
            like((tokens, 3 * channels)),
            like((tokens, channels)),
            like((tokens, channels), F32),
            like((4, up_rows, channels)),
            like((4, up_rows, channels)),
        ],
        in_specs=[
            anywhere if v is expand_weight or v is reduce_weight
            else own_member(v) if id(v) in weights
            else whole(v)
            for v in inputs
        ],
        out_specs=[whole(quadrant)] * 4
        + [anywhere] * 3
        + [whole((tokens, channels))]
        + [whole((4, up_rows, channels))] * 2,
        scratch=[
            pltpu.VMEM((tokens, channels), BF),
            pltpu.VMEM((channels, tokens), BF),
            pltpu.VMEM((tokens, channels), BF),
            pltpu.VMEM((tokens, channels), F32),
            pltpu.VMEM((tokens, channels), F32),
            pltpu.VMEM((8, channels), F32),
            pltpu.VMEM((channels, hidden_units), BF),
            pltpu.VMEM((hidden_units, channels), BF),
            pltpu.VMEM((tokens, channels), BF),
            pltpu.VMEM((tokens, 3 * channels), BF),
            pltpu.VMEM((tokens, channels), BF),
            pltpu.SemaphoreType.DMA((5,)),
        ],
        cost=33.0,
    )

    up_parts = reduce_cores(keep, [swap(send, "lev", 1)], cost=5.0)
    output_parts = returned([y0, y1, y2, y3])
    inputs = [triple, grad_hidden, bias_map, own_lanes, output_weight]
    grad_triple, score_sums = call(
        scores_back_kernel,
        [group_index],
        inputs,
        [like((tokens, 3 * channels)), like((groups, TOKENS, PADDED), F32)],
        in_specs=[own_member(v) if id(v) in weights else whole(v) for v in inputs],
        scratch=[pltpu.VMEM((tokens, channels), BF)],
        after=[up_parts[3]] + output_parts[1:3],
        cost=20.0,
    )
    up_share = reduce_chips(move_chips(up_parts), after=[grad_triple, output_parts[3]])

    inputs = [xw, att, grad_hidden, grad_triple, to_rows, first_gain, first_offset, input_weight]
    d0, d1, d2, d3, low_grads, low_small = call(
        input_back_kernel,
        [group_index],
        inputs,
        [quadrant] * 4 + [like((4, channels, channels)), like((16, channels))],
        in_specs=[own_member(v) if id(v) in weights else whole(v) for v in inputs],
        scratch=[pltpu.VMEM((16, channels), F32)],
        after=[up_share],
        cost=8.0,
    )
    low_keep, *low_send = call(
        spread_kernel,
        [],
        [low_grads],
        [like((4, low_rows, channels))] + [like((4, quarter, channels))] * 2,
        cost=0.1,
    )
    low_arrived = [swap(send, "lev", 1) for send in low_send]
    up_stack = round_samples(up_share, group_index, sets, after=low_arrived)
    low_parts = reduce_cores(low_keep, low_arrived, after=[up_stack])

    up_hop = hop(up_stack, 0)
    low_sums = move_chips(low_parts)
    output = call(assemble_kernel, [], output_parts, like(fields.shape), cost=1.0)
    table_grad = call(
        fold_kernel,
        [],
        [score_sums, cols_map, rows_back, places],
        like((heads * 16, cells * SPAN)),
        scratch=[pltpu.VMEM((2, WW, heads * 16, TOKENS), BF)],
        after=[up_stack, output],
        cost=7.0,
    )
    table_grad = table_grad.reshape(heads, 16, cells * SPAN)[:, :cells]
    table_grad = table_grad.reshape(heads, WZ, WH, WZ, WH, SPAN).transpose(0, 3, 1, 4, 2, 5)
    wide = -(-positions // channels) * channels
    table_grad = jnp.pad(
        table_grad.reshape(heads, positions), ((0, 16 - heads), (0, wide - positions))
    )
    low_share = reduce_chips(low_sums, [table_grad, low_small], after=[up_hop])

    up_stack = anchored(up_stack, [low_share])
    up_own = [up_stack, up_hop, hop(up_stack, 1), hop(up_hop, 1)]
    low_stack = round_samples(low_share, group_index, sets, after=up_own[2:], cost=10.0)
    up_other = [swap(v, "lev", 1) for v in up_own]
    low_hop = hop(low_stack, 0)
    low_stack = anchored(low_stack, [low_hop], cost=12.0)
    low_own = [low_stack, low_hop, hop(low_stack, 1), hop(low_hop, 1)]

    count = low_stack.shape[0]
    up_shapes = [
        like((sets, channels, hidden_units), F32),
        like((sets, 4, 4, quarter, channels), F32),
        like((sets, hidden_units), F32),
    ] + [like((sets, channels), F32)] * 3
    up_grad, down_grad, bup_grad, bdn_grad, g2_grad, o2_grad = call(
        functools.partial(
            finish_up_kernel,
            [[(0, k) for k in range(4)], [(1, None, k) for k in range(4)]],
            [(2, k * channels) for k in range(4)] + [(3, 0), (4, 0), (5, 0)],
        ),
        [group_index],
        up_own + up_other,
        up_shapes,
        in_specs=[anywhere] * 8,
        out_specs=[
            pl.BlockSpec((sets, quarter, hidden_units), lambda r, g: (0, r ^ my_place(), 0)),
            pl.BlockSpec(
                (sets, 4, 1, quarter, channels), lambda r, g: (0, 0, r ^ my_place(), 0, 0)
            ),
        ]
        + [whole(v) for v in up_shapes[2:]],
        scratch=[
            pltpu.VMEM((2, 4, count, up_rows, channels), BF),
            pltpu.SemaphoreType.DMA((2, 4)),
        ],
        grid=(4,),
        cost=11.0,
    )
    low_other = [swap(v, "lev", 1) for v in low_own[:2]]
    block_shapes = [
        like((sets, channels, 3 * channels), F32),
        like((sets, channels, channels), F32),
    ]
    near = call(
        finish_near_kernel,
        [group_index],
        low_own[:2] + low_other,
        block_shapes,
        in_specs=[anywhere] * 4,
        out_specs=[anywhere] * 2,
        scratch=[
            pltpu.VMEM((2, 2, count, low_rows, channels), BF),
            pltpu.VMEM((2, 2, 2, sets, quarter, channels), F32),
            pltpu.SemaphoreType.DMA((2, 2)),
            pltpu.SemaphoreType.DMA((2, 2, 2)),
        ],
        after=[up_grad],
        cost=5.0,
    )
    low_own[3] = anchored(low_own[3], [near[0]])
    low_other += [swap(v, "lev", 1) for v in low_own[2:]]
    small_shapes = [like((sets, w), F32) for w in (channels, 2 * channels, channels, channels)]
    all_rows = low_stack.shape[1]
    in_grad, out_grad, bout_grad, bin_grad, g1_grad, o1_grad, position_grad = call(
        functools.partial(
            finish_low_kernel, [(2, 0), (3, 0), (3, channels), (4, 0), (5, 0)]
        ),
        [group_index, window_types],
        low_own + low_other + list(near),
        block_shapes + small_shapes + [like((sets, heads, kinds, positions), F32)],
        in_specs=[anywhere] * 10,
        out_specs=[anywhere] * 2
        + [whole(v) for v in small_shapes]
        + [pl.BlockSpec((1, heads, kinds, positions), lambda g, *_: (g, 0, 0, 0))],
        scratch=[
            pltpu.VMEM((2, 2, count, all_rows, channels), BF),
            pltpu.VMEM((2, 2, count, all_rows - low_rows, channels), BF),
            pltpu.VMEM((2, 2, 2, sets, quarter, channels), F32),
            pltpu.VMEM((count * 128, wide), BF),
            pltpu.SemaphoreType.DMA((2, 2)),
            pltpu.SemaphoreType.DMA((2, 2)),
            pltpu.SemaphoreType.DMA((2, 2, 2)),
        ],
        grid=(sets,),
        aliases={10: 0, 11: 1},
        cost=8.0,
    )

    input_grad = call(
        assemble_kernel,
        [],
        returned([d0, d1, d2, d3]),
        like(fields.shape),
        after=[position_grad],
        cost=1.0,
    )
    down_grad = down_grad.reshape(sets, -1, channels)
    position_grad = position_grad.transpose(0, 2, 1, 3)
    return (
        output,
        input_grad,
        g1_grad,
        o1_grad,
        in_grad,
        bin_grad,
        out_grad,
        bout_grad,
        g2_grad,
        o2_grad,
        up_grad,
        bup_grad,
        down_grad,
        bdn_grad,
        position_grad,
    )


def solution(mesh):
    slab = P("lat", "lev", None, None)
    return jax.shard_map(
        body,
        mesh=mesh,
        in_specs=(slab,) + (P(),) * 16 + (slab,),
        out_specs=(slab, slab) + (P(),) * 13,
        check_vma=False,
    )
```
